32 devices in a mesh: dp: 8 (over y, x, core), mp: 4 (over z).
Axes of the slice: x: 2, y: 2, z: 4, core: 2. Of those that a mesh axis runs over, the one named last changes fastest.
Arguments:
- layer_input: bfloat16 [16384, 2048], P(('dp', 'mp')), may hold values from -6 to 6
- segments: int32 [16384], P('dp'), may hold values from 0 to 2, as said below
- padding: int32 [16384], P('dp'), may hold values from 0 to 1, as said below
- w_query: bfloat16 [2048, 2048], P('dp', 'mp'), may hold values from -0.125 to 0.125
- w_key: bfloat16 [2048, 2048], P('dp', 'mp'), may hold values from -0.125 to 0.125
- w_value: bfloat16 [2048, 2048], P('dp', 'mp'), may hold values from -0.125 to 0.125
- w_out: bfloat16 [2048, 2048], P('dp', 'mp'), may hold values from -2 to 2
- w_gate: bfloat16 [2048, 8192], P('dp', 'mp'), may hold values from -0.125 to 0.125
- w_up: bfloat16 [2048, 8192], P('dp', 'mp'), may hold values from -0.125 to 0.125
- w_down: bfloat16 [2048, 8192], P('dp', 'mp'), may hold values from -0.0625 to 0.0625
- cotangent: bfloat16 [16384, 2048], P(('dp', 'mp')), may hold values from -6 to 6
Outputs:
- output: bfloat16 [16384, 2048], P(('dp', 'mp'))
- d_input: float32 [16384, 2048], P(('dp', 'mp'))
- g_query: float32 [2048, 2048], P('dp', 'mp')
- g_key: float32 [2048, 2048], P('dp', 'mp')
- g_value: float32 [2048, 2048], P('dp', 'mp')
- g_out: float32 [2048, 2048], P('dp', 'mp')
- g_gate: float32 [2048, 8192], P('dp', 'mp')
- g_up: float32 [2048, 8192], P('dp', 'mp')
- g_down: float32 [2048, 8192], P('dp', 'mp')
The draws below stay inside these ranges and needn't reach their ends.
Inputs may be any that keep to these rules, and one draw needn't show every extreme that they name: `segments`: each sequence holds three documents numbered 0, 1, 2 in order: the first and the last have 200 to 511 tokens each, the middle one the rest. `padding`: in each sequence the tokens with flag 1 form a nonempty tail lying within its last document.
All inputs are finite; a program needn't handle non-finite values.
Results may differ from the reference program's by a relative error of at most 0.023.
Values may be sent and summed in bfloat16 or wider, within the bound.
A program may use at most 256 MiB of HBM per device.

```python
from functools import partial
import jax
import jax.numpy as jnp
from jax import lax

D = 2048
HEADS = 16
HD = 128
FF = 8192
LEN = 2048
DOC_MIN = 200
SEQS = 8
TOKENS = 16384
TOK_DEV = 512
BLOCK = 512


def doc_layout(key):
    seq_keys = jax.random.split(jax.random.fold_in(key, 7), SEQS)

    def one_seq(sub_key):
        head_len = jax.random.randint(jax.random.fold_in(sub_key, 1), (), DOC_MIN, TOK_DEV)
        tail_len = jax.random.randint(jax.random.fold_in(sub_key, 3), (), DOC_MIN, TOK_DEV)
        pad_count = jax.random.randint(jax.random.fold_in(sub_key, 2), (), 1, tail_len + 1)
        positions = jnp.arange(LEN)
        segment = (positions >= head_len).astype(jnp.int32) + (positions >= LEN - tail_len).astype(jnp.int32)
        pad_flags = (positions >= LEN - pad_count).astype(jnp.int32)
        return (segment, pad_flags)
    return jax.vmap(one_seq)(seq_keys)


def draw_segments(key, part):
    return doc_layout(key)[0].reshape(TOKENS)


def draw_padding(key, part):
    return doc_layout(key)[1].reshape(TOKENS)


def strengthened(array, rng, source, target, shards_of, factor):
    owner, partner = [(jnp.arange(array.shape[dim]) // (array.shape[dim] // shards_of)).reshape([-1 if axis == dim else 1 for axis in range(array.ndim)]) for dim in (source, target)]
    chosen = jax.random.permutation(rng, shards_of)[partner]
    strong = (owner == chosen) | (owner == (partner + shards_of // 2) % shards_of)
    return jnp.where(strong, factor * array, array)


def levels(key, dims, cuts, low, top_value):
    def one(position, shards_of):
        draws = jax.random.uniform(jax.random.fold_in(jax.random.fold_in(key, 6), position), (shards_of,), jnp.float32, low / len(cuts), top_value / len(cuts))
        return jnp.repeat(jnp.exp(draws), dims[position] // shards_of).reshape((-1,) + (1,) * (len(dims) - position - 1))

    gain = one(*cuts[0])
    for cut in cuts[1:]:
        gain = gain * one(*cut)
    return gain


def gaussian(stream_key, shape, deviation, most, cuts=(), kind=jnp.bfloat16):
    drawn = deviation * jax.random.normal(stream_key, shape, jnp.float32)
    if cuts:
        drawn = drawn * levels(stream_key, shape, cuts, -0.22, 0.18)
    return jnp.clip(drawn, -most, most).astype(kind)


def heavy_noise(rng, extent, width, limit, shards, heavy, kind=jnp.bfloat16):
    values = width * jax.random.normal(rng, extent, jnp.float32)
    if shards:
        values = values * levels(rng, extent, shards, -0.22, 0.18)
    return jnp.clip(strengthened(values, jax.random.fold_in(rng, 3), *heavy), -limit, limit).astype(kind)


def setup_inputs(seed: int = 0) -> dict:
    key_of = jax.random.split(jax.random.key(seed), 12)
    layer_input = gaussian(key_of[0], (TOKENS, D), 1.0, 6.0, ((0, 32),))
    segments = draw_segments(jax.random.fold_in(key_of[11], 71), 0)
    padding = draw_padding(jax.random.fold_in(key_of[11], 71), 0)
    w_query = gaussian(key_of[3], (D, D), D ** -0.5, 0.125, ((0, 8), (1, 4)))
    w_key = gaussian(key_of[4], (D, D), D ** -0.5, 0.125, ((0, 8), (1, 4)))
    w_value = gaussian(key_of[5], (D, D), D ** -0.5, 0.125, ((0, 8), (1, 4)))
    w_out = gaussian(key_of[6], (D, D), (max(1, D // 256)) ** -0.5, 2.0, ((0, 8), (1, 4)))
    w_gate = gaussian(key_of[7], (D, FF), D ** -0.5, 0.125, ((0, 8), (1, 4)))
    w_up = gaussian(key_of[8], (D, FF), D ** -0.5, 0.125, ((0, 8), (1, 4)))
    w_down = gaussian(key_of[9], (D, FF), FF ** -0.5, 0.0625, ((0, 8), (1, 4)))
    cotangent = heavy_noise(key_of[10], (TOKENS, D), 1.0, 6.0, ((0, 32),), (0, 1, 32, 2.75))
    return {"layer_input": layer_input, "segments": segments, "padding": padding, "w_query": w_query, "w_key": w_key, "w_value": w_value, "w_out": w_out, "w_gate": w_gate, "w_up": w_up, "w_down": w_down, "cotangent": cotangent}


eps = 1e-05
highest = lax.Precision.HIGHEST

@jax.custom_vjp
def low(v):
    return lax.optimization_barrier(v.astype(jnp.bfloat16)).astype(jnp.float32)

@jax.custom_vjp
def low_back(v):
    return v

def low_keep(v):
    return (low(v), None)

def low_pass(kept, grad):
    return (grad,)

def back_keep(v):
    return (v, None)

def back_low(kept, grad):
    return (low(grad),)
low.defvjp(low_keep, low_pass)
low_back.defvjp(back_keep, back_low)

def layer_norm(tok_rows):
    average = lax.optimization_barrier(jnp.mean(tok_rows, axis=-1, keepdims=True))
    centred = tok_rows - average
    variance = lax.optimization_barrier(jnp.mean(centred * centred, axis=-1, keepdims=True))
    return centred * lax.rsqrt(variance + eps)

def dot_high(left, right):
    return jnp.dot(left, right, precision=highest, preferred_element_type=jnp.float32)

def rope_tables(length, head_size):
    half_size = head_size // 2
    positions = jnp.arange(length).astype(jnp.float32)[:, None]
    frequency = 10000.0 ** (-jnp.arange(half_size).astype(jnp.float32) / half_size)
    angles = positions * frequency[None, :]
    return (jnp.cos(angles), jnp.sin(angles))

def rotate(per_head, cos_tab, sin_tab):
    half_size = per_head.shape[-1] // 2
    front_half = per_head[..., :half_size]
    back_half = per_head[..., half_size:]
    cos_part = cos_tab[:, None, :]
    sin_part = sin_tab[:, None, :]
    return jnp.concatenate([front_half * cos_part - back_half * sin_part, back_half * cos_part + front_half * sin_part], axis=-1)

def visible(segment, padding, offset, count):
    q_pos = offset + jnp.arange(count).astype(jnp.int32)
    k_pos = jnp.arange(segment.shape[0]).astype(jnp.int32)
    seg_rows = lax.dynamic_slice_in_dim(segment, offset, count)
    causal = k_pos[None, :] <= q_pos[:, None]
    same_doc = seg_rows[:, None] == segment[None, :]
    real_key = (padding[None, :] == 0) | (k_pos[None, :] == q_pos[:, None])
    return causal & same_doc & real_key

def attend_block(queries, key_rows, value_rows, segment, padding, offset):
    q_blk = lax.dynamic_slice_in_dim(queries, offset, BLOCK, 0)
    allowed = visible(segment, padding, offset, BLOCK)
    scores = jnp.einsum('qhd,khd->hqk', q_blk, key_rows, precision=highest) * HD ** (-0.5)
    scores = low_back(scores)
    scores = jnp.where(allowed[None], scores, -1e+30)
    row_max = lax.optimization_barrier(jnp.max(scores, axis=-1, keepdims=True))
    weights = jnp.exp(scores - row_max)
    probs = low(weights / lax.optimization_barrier(jnp.sum(weights, axis=-1, keepdims=True)))
    return jnp.einsum('hqk,khd->qhd', probs, value_rows, precision=highest)

def layer(tok_rows, w_query, w_key, w_value, w_out, w_gate, w_up, w_down, segment, padding):
    length = tok_rows.shape[0]
    cos_tab, sin_tab = rope_tables(length, HD)
    norm1 = low(layer_norm(tok_rows))
    q_lin = low_back(dot_high(norm1, w_query)).reshape(length, HEADS, HD)
    k_lin = low_back(dot_high(norm1, w_key)).reshape(length, HEADS, HD)
    values = low(low_back(dot_high(norm1, w_value))).reshape(length, HEADS, HD)
    queries = low(rotate(q_lin, cos_tab, sin_tab))
    key_rows = low(rotate(k_lin, cos_tab, sin_tab))
    offsets = jnp.arange(length // BLOCK).astype(jnp.int32) * BLOCK
    block_fn = jax.checkpoint(partial(attend_block, queries, key_rows, values, segment, padding))
    attended = lax.map(block_fn, offsets).reshape(length, D)
    attended = low(low_back(attended))
    attn_out = low_back(dot_high(attended, w_out.T))
    hidden = tok_rows + attn_out
    norm2 = low(layer_norm(hidden))
    gate = low_back(dot_high(norm2, w_gate))
    up_lin = low_back(dot_high(norm2, w_up))
    act = low(jax.nn.silu(gate) * up_lin)
    mlp_out = low_back(dot_high(act, w_down.T))
    return hidden + mlp_out

def reference(layer_input, segments, padding, w_query, w_key, w_value, w_out, w_gate, w_up, w_down, cotangent):
    weights = tuple((w.astype(jnp.float32) for w in (w_query, w_key, w_value, w_out, w_gate, w_up, w_down)))
    rows_all = layer_input.astype(jnp.float32).reshape(SEQS, LEN, D)
    cot_all = cotangent.astype(jnp.float32).reshape(SEQS, LEN, D)
    seg_all = segments.reshape(SEQS, LEN)
    pad_all = padding.reshape(SEQS, LEN)

    def one_seq(running, element):
        tok_rows, cot_rows, segment, pad_rows = element

        def forward(inputs, *mats):
            return layer(inputs, *mats, segment, pad_rows)
        result, pullback = jax.vjp(forward, tok_rows, *weights)
        gradients = pullback(cot_rows)
        running = tuple((a + b for a, b in zip(running, gradients[1:])))
        return (running, (result.astype(jnp.bfloat16), gradients[0]))
    initial = tuple((jnp.zeros(w.shape, jnp.float32) for w in weights))
    totals, (outputs, d_inputs) = lax.scan(one_seq, initial, (rows_all, cot_all, seg_all, pad_all))
    return (outputs.reshape(TOKENS, D), d_inputs.reshape(TOKENS, D), totals[0], totals[1], totals[2], totals[3], totals[4], totals[5], totals[6])
```

```python
import functools
import jax
import jax.numpy as jnp
from jax import lax
from jax.experimental import pallas as pl
from jax.experimental.pallas import tpu as pltpu
from jax.sharding import Mesh, PartitionSpec as P

HD = 128
SCALE = HD ** (-0.5)
LOG2E = 1.4426950408889634
NEG = -1e30
eps = 1e-05
NT = (((1,), (1,)), ((), ()))
TN = (((0,), (0,)), ((), ()))


def layer_norm(tok_rows):
    average = jnp.mean(tok_rows, axis=-1, keepdims=True)
    centred = tok_rows - average
    variance = jnp.mean(centred * centred, axis=-1, keepdims=True)
    return centred * lax.rsqrt(variance + eps)


def swiglu(gate, up_lin):
    return jax.nn.silu(gate) * up_lin


def dot(left, right, dims=(((1,), (0,)), ((), ()))):
    return lax.dot_general(left, right, dims, preferred_element_type=jnp.float32)


def low(value):
    return value.astype(jnp.bfloat16)

def visit_lists(pos, end, blk):
    first = pos[::blk]
    most = jnp.max(end.reshape(-1, blk), axis=1)
    met = (first[None, :] <= first[:, None]) & (most[None, :] >= first[:, None])
    count = jnp.sum(met, axis=1, dtype=jnp.int32)
    keys = jnp.argsort(~met, axis=1, stable=True).astype(jnp.int32)
    total = jnp.sum(count, dtype=jnp.int32)
    pairs = jnp.argsort(~met.reshape(-1), stable=True).astype(jnp.int32)
    return first, count, keys.reshape(-1), total.reshape(1), pairs


def turned(value, cos_ref, sin_ref, sign):
    return value * cos_ref[...] + sign * pltpu.roll(value, HD // 2, 1) * sin_ref[...]


def allowed_of(first_q, first_k, end_row):
    blk = end_row.shape[1]
    t = first_q + lax.broadcasted_iota(jnp.int32, (blk, 1), 0)
    u = first_k + lax.broadcasted_iota(jnp.int32, (1, blk), 1)
    return (u <= t) & (t <= end_row)


def forward_kernel(
    hpg, first, count, keys, q_lin, k_lin, v_lin, cos_ref, sin_ref, end_ref,
    att_ref, lse_ref, q_ref, k_ref, v_ref
):
    n_k, blk = end_ref.shape
    for h in range(hpg):
        cols = slice(h * HD, (h + 1) * HD)
        q_ref[:, cols] = turned(q_lin[:, cols], cos_ref, sin_ref, 1.0).astype(jnp.bfloat16)
        k_ref[:, cols] = turned(k_lin[:, cols], cos_ref, sin_ref, 1.0).astype(jnp.bfloat16)
        v_ref[:, cols] = v_lin[:, cols].astype(jnp.bfloat16)

    @pl.loop(0, n_k)
    def _(i):
        rows = pl.ds(pl.multiple_of(i * blk, blk), blk)

        def step(n, carry):
            j = keys[i * n_k + n]
            spot = pl.ds(pl.multiple_of(j * blk, blk), blk)
            allowed = allowed_of(first[i], first[j], end_ref[pl.ds(j, 1), :])
            out = []
            for h in range(hpg):
                cols = slice(h * HD, (h + 1) * HD)
                top, total, acc = carry[h]
                scores = dot(q_ref[rows, cols], k_ref[spot, cols], NT)
                scores = jnp.where(allowed, scores * (SCALE * LOG2E), NEG)
                new_top = jnp.maximum(top, jnp.max(scores, axis=1, keepdims=True))
                weights = jnp.exp2(scores - new_top)
                shrink = jnp.exp2(top - new_top)
                total = total * shrink + jnp.sum(weights, axis=1, keepdims=True)
                acc = acc * shrink + dot(weights.astype(jnp.bfloat16), v_ref[spot, cols])
                out.append((new_top, total, acc))
            return tuple(out)

        start = tuple(
            (
                jnp.full((blk, 1), NEG, jnp.float32),
                jnp.zeros((blk, 1), jnp.float32),
                jnp.zeros((blk, HD), jnp.float32),
            )
            for _ in range(hpg)
        )
        done = lax.fori_loop(0, count[i], step, start)
        for h in range(hpg):
            cols = slice(h * HD, (h + 1) * HD)
            top, total, acc = done[h]
            att_ref[rows, cols] = low(acc / total)
            lse_ref[rows, cols] = jnp.broadcast_to(top + jnp.log2(total), (blk, HD))


def attend(qkv, cos, sin, end_rows, lists, heads, hpg):
    length = qkv.shape[0]
    first, count, keys, _, _ = lists
    groups = heads // hpg
    wide = hpg * HD
    col = lambda k: pl.BlockSpec((length, wide), lambda g, *_: (0, k * groups + g))
    whole = lambda a: pl.BlockSpec(a.shape, lambda g, *_: (0, 0))
    low = jax.ShapeDtypeStruct((length, heads * HD), jnp.bfloat16)
    return pl.pallas_call(
        functools.partial(forward_kernel, hpg),
        grid_spec=pltpu.PrefetchScalarGridSpec(
            num_scalar_prefetch=3,
            grid=(groups,),
            in_specs=[col(0), col(1), col(2), whole(cos), whole(sin), whole(end_rows)],
            out_specs=[col(0)] * 5,
        ),
        out_shape=[low, jax.ShapeDtypeStruct(low.shape, jnp.float32), low, low, low],
        compiler_params=pltpu.CompilerParams(vmem_limit_bytes=48 * 2**20),
        cost_estimate=pl.CostEstimate(
            flops=2 * length * length * HD * heads,
            bytes_accessed=length * heads * HD * 24,
            transcendentals=heads * length * length // 2,
        ),
    )(first, count, keys, qkv, qkv, qkv, cos, sin, end_rows)


def backward_kernel(
    hpg, first, total, pairs, q_ref, k_ref, v_ref, grad_ref, att_ref, lse_ref,
    cos_ref, sin_ref, end_ref, dq_ref, dk_ref, dv_ref, dq_acc, dk_acc, dv_acc, delta
):
    n_k, blk = end_ref.shape
    dq_acc[...] = jnp.zeros_like(dq_acc)
    dk_acc[...] = jnp.zeros_like(dk_acc)
    dv_acc[...] = jnp.zeros_like(dv_acc)
    for h in range(hpg):
        cols = slice(h * HD, (h + 1) * HD)
        prod = grad_ref[:, cols].astype(jnp.float32) * att_ref[:, cols].astype(jnp.float32)
        delta[:, cols] = jnp.broadcast_to(jnp.sum(prod, axis=1, keepdims=True), prod.shape)

    def step(n, carry):
        code = pairs[n]
        i, j = code // n_k, code % n_k
        rows = pl.ds(pl.multiple_of(i * blk, blk), blk)
        spot = pl.ds(pl.multiple_of(j * blk, blk), blk)
        allowed = allowed_of(first[i], first[j], end_ref[pl.ds(j, 1), :])
        for h in range(hpg):
            cols = slice(h * HD, (h + 1) * HD)
            q, k, v, grad = q_ref[rows, cols], k_ref[spot, cols], v_ref[spot, cols], grad_ref[rows, cols]
            scores = dot(q, k, NT) * (SCALE * LOG2E)
            lse = lse_ref[rows, h * HD : h * HD + 1]
            probs = jnp.where(allowed, jnp.exp2(scores - lse), 0.0)
            d_probs = dot(grad, v, NT)
            d_scores = (probs * (d_probs - delta[rows, h * HD : h * HD + 1])).astype(jnp.bfloat16)
            dv_acc[spot, cols] += dot(probs.astype(jnp.bfloat16), grad, TN)
            dk_acc[spot, cols] += dot(d_scores, q, TN)
            dq_acc[rows, cols] += dot(d_scores, k)
        return carry

    lax.fori_loop(0, total[0], step, 0)
    for h in range(hpg):
        cols = slice(h * HD, (h + 1) * HD)
        dq_ref[:, cols] = turned(dq_acc[:, cols] * SCALE, cos_ref, sin_ref, -1.0).astype(jnp.bfloat16)
        dk_ref[:, cols] = turned(dk_acc[:, cols] * SCALE, cos_ref, sin_ref, -1.0).astype(jnp.bfloat16)
        dv_ref[:, cols] = dv_acc[:, cols].astype(jnp.bfloat16)


def attend_back(q, k, v, grad, att, lse, cos, sin, end_rows, lists, heads, hpg):
    length = q.shape[0]
    first, _, _, total, pairs = lists
    groups = heads // hpg
    wide = hpg * HD
    col = pl.BlockSpec((length, wide), lambda g, *_: (0, g))
    whole = lambda a: pl.BlockSpec(a.shape, lambda g, *_: (0, 0))
    low = jax.ShapeDtypeStruct((length, heads * HD), jnp.bfloat16)
    return pl.pallas_call(
        functools.partial(backward_kernel, hpg),
        grid_spec=pltpu.PrefetchScalarGridSpec(
            num_scalar_prefetch=3,
            grid=(groups,),
            in_specs=[col] * 6 + [whole(cos), whole(sin), whole(end_rows)],
            out_specs=[col] * 3,
            scratch_shapes=[pltpu.VMEM((length, wide), jnp.float32)] * 4,
        ),
        out_shape=[low] * 3,
        compiler_params=pltpu.CompilerParams(vmem_limit_bytes=48 * 2**20),
        cost_estimate=pl.CostEstimate(
            flops=5 * length * length * HD * heads,
            bytes_accessed=length * heads * HD * 20,
            transcendentals=heads * length * length // 2,
        ),
    )(first, total, pairs, q, k, v, grad, att, lse, cos, sin, end_rows)


def flip(value, axis):
    return lax.ppermute(value, axis, [(0, 1), (1, 0)])


def body(places, x, segments, padding, w_query, w_key, w_value, w_out, w_gate, w_up, w_down, cot):
    rest, core, high, lower = places
    pair = (core, high)
    c, h = lax.axis_index(core), lax.axis_index(high)
    same = c == h
    first_core = c == 0

    def swap(value):
        return lax.ppermute(value, pair, [(0, 0), (1, 2), (2, 1), (3, 3)])

    def gather_low(value):
        parts = [value]
        for axis in lower:
            parts = parts + [flip(part, axis) for part in parts]
        return parts

    def gather(value):
        parts = gather_low(value)
        return jnp.concatenate([piece for part in parts for piece in (part, flip(part, core))])

    def scatter(product, n_parts):
        far = []
        for part in reversed(range(n_parts)):
            mine, other = product(part)
            far.insert(0, (mine, flip(other, core)))
        sums = [mine.astype(jnp.float32) + other.astype(jnp.float32) for mine, other in far]
        for axis in reversed(lower):
            half = len(sums) // 2
            sums = [sums[k] + flip(low(sums[half + k]), axis).astype(jnp.float32) for k in range(half)]
        return sums[0]

    def gather_weight(shard):
        to_far0 = lax.ppermute(shard, pair, [(0, 1), (1, 2)])
        to_far1 = lax.ppermute(shard, pair, [(2, 1), (3, 2)])
        near = lax.ppermute(shard, pair, [(2, 0), (1, 3)])
        s0 = jnp.where(same, jnp.where(first_core, shard, near), to_far0)
        s1 = jnp.where(same, jnp.where(first_core, near, shard), to_far1)
        return lax.all_gather(jnp.concatenate([s0, s1]), rest, axis=0, tiled=True)

    def scatter_weight(partial):
        both = lax.psum_scatter(partial, rest, scatter_dimension=0, tiled=True)
        rows = both.shape[0] // 2
        s0, s1 = both[:rows], both[rows:]
        near = lax.ppermute(jnp.where(first_core, s1, s0), pair, [(0, 2), (3, 1)])
        from0 = lax.ppermute(s0, pair, [(1, 0), (2, 1)])
        from1 = lax.ppermute(s1, pair, [(1, 2), (2, 3)])
        kept = jnp.where(same, jnp.where(first_core, s0, s1), near)
        far = jnp.where(first_core, from0, from1)
        return kept.astype(jnp.float32) + far.astype(jnp.float32)

    own = x.shape[0]
    n_parts = 2 ** len(lower)
    length = 2 * n_parts * own
    cols = w_query.shape[1]
    heads = cols // HD
    blk = min(512, own)

    spot = jnp.int32(0)
    for axis in lower:
        spot = spot * 2 + lax.axis_index(axis)
    quarters = []
    order = [0]
    for k in range(len(lower)):
        order = order + [part + 2 ** (len(lower) - 1 - k) for part in order]
    for part in order:
        for other in (0, 1):
            quarters.append((c ^ other) * n_parts + (spot ^ part))
    position = jnp.concatenate([q * own + jnp.arange(own, dtype=jnp.int32) for q in quarters])
    marks = jnp.stack([segments, padding])
    marks = jnp.where(same, marks, flip(marks, core))
    seg, pad = marks[0], marks[1]
    last = jnp.sum((seg[None, :] <= seg[:, None]).astype(jnp.int32), axis=1) - 1
    end = jnp.where(pad == 0, last, jnp.arange(length, dtype=jnp.int32))
    end = jnp.concatenate([lax.dynamic_slice_in_dim(end, q * own, own) for q in quarters])
    lists = visit_lists(position, end, blk)
    end_rows = end.reshape(-1, blk)
    frequency = 10000.0 ** (-jnp.arange(HD // 2).astype(jnp.float32) / (HD // 2))
    angles = position.astype(jnp.float32)[:, None] * frequency[None, :]
    cos, sin = jnp.cos(angles), jnp.sin(angles)
    cos = jnp.concatenate([cos, cos], axis=1)
    sin = jnp.concatenate([-sin, sin], axis=1)

    x_own = swap(x).astype(jnp.float32)
    norm1_own, norm1_pull = jax.vjp(layer_norm, x_own)
    w_qkv = gather_weight(jnp.concatenate([w_query, w_key, w_value], axis=1))
    norm1 = gather(low(norm1_own))
    full_out = gather_weight(w_out)
    full_gate = gather_weight(w_gate)
    full_up = gather_weight(w_up)
    cot_own = swap(cot)
    cots = gather(cot_own)
    full_down = gather_weight(w_down)

    qkv = dot(norm1, w_qkv)
    attended, lse, q, k, v = attend(qkv, cos, sin, end_rows, lists, heads, 1)

    def halves(product, values):
        def of(part):
            lo = part * 2 * own
            both = low(product(*(value[lo : lo + 2 * own] for value in values)))
            return both[:own], both[own:]

        return of

    hidden = x_own + scatter(halves(lambda a: dot(a, full_out, NT), (attended,)), n_parts)
    norm2_own, norm2_pull = jax.vjp(layer_norm, hidden)
    norm2 = gather(low(norm2_own))
    gate = dot(norm2, full_gate)
    up_lin = dot(norm2, full_up)
    act, act_pull = jax.vjp(swiglu, gate, up_lin)
    act_low = low(act)
    d_act = dot(cots, full_down)
    d_gate_f, d_up_f = act_pull(d_act)
    d_gate, d_up = low(d_gate_f), low(d_up_f)
    d_norm2 = scatter(
        halves(lambda a, b: dot(a, full_gate, NT) + dot(b, full_up, NT), (d_gate, d_up)), n_parts
    )
    d_hidden = cot_own.astype(jnp.float32) + norm2_pull(d_norm2)[0]
    d_hiddens = gather(low(d_hidden))

    mlp = scatter(halves(lambda a: dot(a, full_down, NT), (act_low,)), n_parts)
    output = swap(low(hidden + mlp))
    g_down = scatter_weight(low(dot(cots, act_low, TN)))
    g_gate = scatter_weight(low(dot(norm2, d_gate, TN)))
    g_up = scatter_weight(low(dot(norm2, d_up, TN)))

    d_attended = low(dot(d_hiddens, full_out))
    dq, dk, dv = attend_back(q, k, v, d_attended, attended, lse, cos, sin, end_rows, lists, heads, 1)
    d_qkv = jnp.concatenate([dq, dk, dv], axis=1)
    d_norm1 = scatter(halves(lambda a: dot(a, w_qkv, NT), (d_qkv,)), n_parts)
    d_input = swap(low(d_hidden + norm1_pull(d_norm1)[0])).astype(jnp.float32)
    g_out = scatter_weight(low(dot(d_hiddens, attended, TN)))
    g_qkv = scatter_weight(low(dot(norm1, d_qkv, TN)))
    return (
        output,
        d_input,
        g_qkv[:, :cols],
        g_qkv[:, cols : 2 * cols],
        g_qkv[:, 2 * cols :],
        g_out,
        g_gate,
        g_up,
        g_down,
    )


def solution(mesh):
    dp, mp = mesh.devices.shape
    n_dp, n_mp = dp.bit_length() - 1, mp.bit_length() - 1
    dp_axes = tuple("d%d" % k for k in range(n_dp))
    mp_axes = tuple("m%d" % k for k in range(n_mp))
    fine = Mesh(mesh.devices.reshape((2,) * (n_dp + n_mp)), dp_axes + mp_axes)
    places = (dp_axes[:-1], dp_axes[-1], mp_axes[0], mp_axes[1:])
    tokens = P(dp_axes + mp_axes, None)
    weight = P(dp_axes, mp_axes)
    return jax.shard_map(
        functools.partial(body, places),
        mesh=fine,
        in_specs=(tokens, P(dp_axes), P(dp_axes)) + (weight,) * 7 + (tokens,),
        out_specs=(tokens, tokens) + (weight,) * 7,
        check_vma=False,
    )
```

```python
import functools
import jax
import jax.numpy as jnp
import numpy as np
from jax import lax
from jax.experimental import pallas as pl
from jax.experimental.pallas import tpu as pltpu
from jax.sharding import Mesh, PartitionSpec as P

HD = 128
SCALE = HD ** (-0.5)
LOG2E = 1.4426950408889634
NEG = -1e30
eps = 1e-05
NT = (((1,), (1,)), ((), ()))
TN = (((0,), (0,)), ((), ()))


def layer_norm(tok_rows):
    average = jnp.mean(tok_rows, axis=-1, keepdims=True)
    centred = tok_rows - average
    variance = jnp.mean(centred * centred, axis=-1, keepdims=True)
    return centred * lax.rsqrt(variance + eps)


def swiglu(gate, up_lin):
    return jax.nn.silu(gate) * up_lin


def dot(left, right, dims=(((1,), (0,)), ((), ()))):
    return lax.dot_general(left, right, dims, preferred_element_type=jnp.float32)


def low(value):
    return value.astype(jnp.bfloat16)

def visit_lists(pos, end, blk):
    first = pos[::blk]
    most = jnp.max(end.reshape(-1, blk), axis=1)
    met = (first[None, :] <= first[:, None]) & (most[None, :] >= first[:, None])
    count = jnp.sum(met, axis=1, dtype=jnp.int32)
    keys = jnp.argsort(~met, axis=1, stable=True).astype(jnp.int32)
    total = jnp.sum(count, dtype=jnp.int32)
    pairs = jnp.argsort(~met.reshape(-1), stable=True).astype(jnp.int32)
    return first, count, keys.reshape(-1), total.reshape(1), pairs


def turned(value, cos_ref, sin_ref, sign):
    return value * cos_ref[...] + sign * pltpu.roll(value, HD // 2, 1) * sin_ref[...]


def allowed_of(first_q, first_k, end_row):
    blk = end_row.shape[1]
    t = first_q + lax.broadcasted_iota(jnp.int32, (blk, 1), 0)
    u = first_k + lax.broadcasted_iota(jnp.int32, (1, blk), 1)
    return (u <= t) & (t <= end_row)


def backward_kernel(
    hpg, n_after, first, total, pairs, q_ref, k_ref, v_ref, grad_ref, att_ref, lse_ref,
    cos_ref, sin_ref, end_ref, *refs
):
    dq_ref, dk_ref, dv_ref, dq_acc, dk_acc, dv_acc, delta, lses = refs[n_after:]
    n_k, blk = end_ref.shape
    dq_acc[...] = jnp.zeros_like(dq_acc)
    dk_acc[...] = jnp.zeros_like(dk_acc)
    dv_acc[...] = jnp.zeros_like(dv_acc)
    lanes = lax.broadcasted_iota(jnp.int32, lse_ref.shape, 1)
    for h in range(hpg):
        cols = slice(h * HD, (h + 1) * HD)
        mine = jnp.where(lanes == pl.program_id(0) * hpg + h, lse_ref[...], 0.0)
        lses[:, cols] = jnp.broadcast_to(jnp.sum(mine, axis=1, keepdims=True), mine.shape)
        prod = grad_ref[:, cols].astype(jnp.float32) * att_ref[:, cols].astype(jnp.float32)
        delta[:, cols] = jnp.broadcast_to(jnp.sum(prod, axis=1, keepdims=True), prod.shape)

    def step(n, carry):
        code = pairs[n]
        i, j = code // n_k, code % n_k
        rows = pl.ds(pl.multiple_of(i * blk, blk), blk)
        spot = pl.ds(pl.multiple_of(j * blk, blk), blk)
        allowed = allowed_of(first[i], first[j], end_ref[pl.ds(j, 1), :])
        for h in range(hpg):
            cols = slice(h * HD, (h + 1) * HD)
            q, k, v, grad = q_ref[rows, cols], k_ref[spot, cols], v_ref[spot, cols], grad_ref[rows, cols]
            scores = dot(q, k, NT) * (SCALE * LOG2E)
            lse = lses[rows, h * HD : h * HD + 1]
            probs = jnp.where(allowed, jnp.exp2(scores - lse), 0.0)
            d_probs = dot(grad, v, NT)
            d_scores = (probs * (d_probs - delta[rows, h * HD : h * HD + 1])).astype(jnp.bfloat16)
            dv_acc[spot, cols] += dot(probs.astype(jnp.bfloat16), grad, TN)
            dk_acc[spot, cols] += dot(d_scores, q, TN)
            dq_acc[rows, cols] += dot(d_scores, k)
        return carry

    lax.fori_loop(0, total[0], step, 0)
    for h in range(hpg):
        cols = slice(h * HD, (h + 1) * HD)
        dq_ref[:, cols] = turned(dq_acc[:, cols] * SCALE, cos_ref, sin_ref, -1.0).astype(jnp.bfloat16)
        dk_ref[:, cols] = turned(dk_acc[:, cols] * SCALE, cos_ref, sin_ref, -1.0).astype(jnp.bfloat16)
        dv_ref[:, cols] = dv_acc[:, cols].astype(jnp.bfloat16)


def attend_back(q, k, v, grad, att, lse, cos, sin, end_rows, lists, heads, hpg, after=()):
    length = q.shape[0]
    first, _, _, total, pairs = lists
    groups = heads // hpg
    wide = hpg * HD
    col = pl.BlockSpec((length, wide), lambda g, *_: (0, g))
    whole = lambda a: pl.BlockSpec(a.shape, lambda g, *_: (0, 0))
    low = jax.ShapeDtypeStruct((length, heads * HD), jnp.bfloat16)
    return pl.pallas_call(
        functools.partial(backward_kernel, hpg, len(after)),
        grid_spec=pltpu.PrefetchScalarGridSpec(
            num_scalar_prefetch=3,
            grid=(groups,),
            in_specs=[col] * 5
            + [whole(lse), whole(cos), whole(sin), whole(end_rows)]
            + [pl.BlockSpec(memory_space=pl.ANY)] * len(after),
            out_specs=[col] * 3,
            scratch_shapes=[pltpu.VMEM((length, wide), jnp.float32)] * 5,
        ),
        out_shape=[low] * 3,
        compiler_params=pltpu.CompilerParams(vmem_limit_bytes=48 * 2**20),
        cost_estimate=pl.CostEstimate(
            flops=5 * length * length * HD * heads,
            bytes_accessed=length * heads * HD * 20,
            transcendentals=heads * length * length // 2,
        ),
    )(first, total, pairs, q, k, v, grad, att, lse, cos, sin, end_rows, *after)


MESH = pl.DeviceIdType.MESH
CHUNKS = 4
SEMS = 224
MATS = ("qkv", "out", "gate", "up", "down")


def flipped(bit, other):
    return bit + other - 2 * bit * other


class Links:
    def __init__(self, places, send, recv):
        self.rest, self.core, self.high, self.lower = places
        self.c, self.h = lax.axis_index(self.core), lax.axis_index(self.high)
        self.r = [lax.axis_index(axis) for axis in self.rest]
        self.low = [lax.axis_index(axis) for axis in self.lower]
        self.same = self.c == self.h
        self.n_parts = 2 ** len(self.lower)
        self.send, self.recv, self.used, self.unsent = send, recv, 0, []
        self.across = {self.core: 1 - self.c}

    def beside(self, k):
        return {self.lower[k]: 1 - self.low[k]}

    def over(self, k):
        return {self.rest[k]: 1 - self.r[k]}

    def group(self, mask):
        total = 0
        for k, bit in enumerate(self.r):
            total = total * 2 + (1 - bit if mask >> k & 1 else bit)
        return total

    def swap_piece(self, number):
        other, part = number % 2, number // 2
        return flipped(self.c, other) * self.n_parts + self.turn(part)

    def piece(self, quarter):
        other, part = flipped(self.c, quarter // self.n_parts), self.turn(quarter % self.n_parts)
        return part * 2 + other

    def turn(self, part):
        total = 0
        for k, bit in enumerate(self.low):
            digit = part // 2 ** (len(self.low) - 1 - k) % 2
            total = total * 2 + flipped(bit, digit)
        return total

    def greet(self):
        barrier = pltpu.get_barrier_semaphore()
        partners = [
            self.across,
            {self.high: 1 - self.h},
            {self.core: 1 - self.c, self.high: 1 - self.h},
        ]
        partners += [self.beside(k) for k in range(len(self.lower))]
        partners += [self.over(k) for k in range(len(self.rest))]
        for partner in partners:
            pl.semaphore_signal(barrier, inc=1, device_id=partner, device_id_type=MESH)
        pl.semaphore_wait(barrier, len(partners))

    def take(self, count=1):
        self.used += count
        return self.used - count

    def copy(self, src, dst, partner, spot=None, recv=None):
        spot = self.take() if spot is None else spot
        made = pltpu.make_async_remote_copy(
            src_ref=src, dst_ref=dst, send_sem=self.send.at[spot],
            recv_sem=self.recv.at[spot if recv is None else recv],
            device_id=partner, device_id_type=MESH,
        )
        return made

    def push(self, src, dst, partner):
        made = self.copy(src, dst, partner)
        made.start()
        self.unsent.append(made)
        return made


class Weight:
    def __init__(self, links, shard, full):
        self.links, self.shard, self.full = links, shard, full
        self.rows = shard.shape[0]
        self.arrive = links.take(2)
        self.near, self.far = links.take(), links.take()
        self.stages = []
        n = len(links.rest)
        for step in range(n):
            stage = []
            for half in range(2):
                order = list(range(n)) if half == 0 else list(reversed(range(n)))
                have = [0]
                for k in order[:step]:
                    have = have + [mask | 1 << k for mask in have]
                stage += [(half, mask, order[step], links.take()) for mask in have]
            self.stages.append(stage)

    def slot(self, mask, core):
        start = (self.links.group(mask) * 2 + core) * self.rows
        return self.full.at[pl.ds(pl.multiple_of(start, self.rows), self.rows)]

    def near_copy(self):
        links = self.links
        return links.copy(
            self.shard, self.slot(0, links.c), links.across, self.near, self.arrive + links.c
        )

    def far_copy(self):
        links = self.links
        return links.copy(
            self.shard, self.slot(0, links.c), {links.core: links.h, links.high: 1 - links.h},
            self.far, self.arrive + links.c,
        )

    def send_near(self):
        links = self.links

        @pl.when(links.same)
        def _():
            pltpu.make_async_copy(
                self.shard, self.slot(0, links.c), links.recv.at[self.arrive + links.c]
            ).start()

        @pl.when(~links.same)
        def _():
            self.near_copy().start()

    def send_far(self):
        self.far_copy().start()

    def stage_copies(self, step):
        for half, mask, axis, spot in self.stages[step]:
            block = self.slot(mask, half)
            yield self.links.copy(block, block, self.links.over(axis), spot)

    def event(self, step):
        if step == 0:
            for core in range(2):
                block = self.slot(0, core)
                pltpu.make_async_copy(block, block, self.links.recv.at[self.arrive + core]).wait()
        else:
            for copy in self.stage_copies(step - 1):
                copy.wait_recv()
        if step < len(self.stages):
            for copy in self.stage_copies(step):
                copy.start()

    def finish(self):
        @pl.when(~self.links.same)
        def _():
            self.near_copy().wait_send()

        self.far_copy().wait_send()
        for step in range(len(self.stages)):
            for copy in self.stage_copies(step):
                copy.wait_send()


class Spread:
    def __init__(self, links, full, own):
        self.links, self.full, self.own, self.chunk = links, full, own, own // CHUNKS
        self.moves = {}
        n = len(links.lower)
        for k in range(CHUNKS):
            have = [0]
            for step in range(n):
                value = 2 ** (n - 1 - step)
                for part in have:
                    self.moves[k, part, step] = (part | value, links.take())
                have = have + [part | value for part in have]
            for part in range(links.n_parts):
                self.moves[k, part, None] = (part, links.take())

    def rows(self, part, other, k):
        return pl.ds((part * 2 + other) * self.own + k * self.chunk, self.chunk)

    def made(self, k, part, step, src=None):
        goal, spot = self.moves[k, part, step]
        links = self.links
        partner = links.across if step is None else links.beside(step)
        src = self.full.at[self.rows(part, 0, k)] if src is None else src
        dst = self.full.at[self.rows(goal, 1 if step is None else 0, k)]
        return links.copy(src, dst, partner, spot)

    def first_step(self, part):
        n = len(self.links.lower)
        return [s for s in range(n) if (0, part, s) in self.moves]

    def own_ready(self, k):
        for step in self.first_step(0):
            self.made(k, 0, step).start()
        self.made(k, 0, None).start()

    def pass_on(self, k):
        n = len(self.links.lower)
        for step in range(n):
            value = 2 ** (n - 1 - step)
            for part in range(self.links.n_parts):
                if (k, part, step) in self.moves:
                    self.made(k, part, step).wait_recv()
                    goal = part | value
                    for later in self.first_step(goal):
                        self.made(k, goal, later).start()
                    self.made(k, goal, None).start()

    def wait_near(self):
        for k in range(CHUNKS):
            self.made(k, 0, None).wait_recv()

    def wait_far(self):
        for k in range(CHUNKS):
            for part in range(1, self.links.n_parts):
                self.made(k, part, None).wait_recv()

    def finish(self):
        for k, part, step in self.moves:
            self.made(k, part, step).wait_send()


def normed(value):
    average = jnp.mean(value, axis=-1, keepdims=True)
    centred = value - average
    variance = jnp.mean(centred * centred, axis=-1, keepdims=True)
    return centred * lax.rsqrt(variance + eps)


def spin(value, cos, sin):
    return value * cos + pltpu.roll(value, HD // 2, 1) * sin


def first_kernel(
    places, x, end_mine, cos_ref, sin_ref, w_qkv, w_out, w_gate, w_up, w_down, cot,
    norm1, qkv_all, out_all, gate_all, up_all, down_all, q_ref, k_ref, v_ref, att_ref, lse_ref, x_own, hidden,
    norm2, cot_own, norm1_v, qkv_v, out_v, end_other, p_mine, p_other, p_come, line, send, recv, local,
):
    links = Links(places, send, recv)
    own = x.shape[0]
    n_parts, n_pieces = links.n_parts, 2 * links.n_parts
    n_low = len(links.lower)
    chunk = own // CHUNKS
    heads = q_ref.shape[1] // HD
    width = heads * HD
    weights = {
        name: Weight(links, shard, full)
        for name, shard, full in zip(
            MATS,
            (w_qkv, w_out, w_gate, w_up, w_down),
            (qkv_v, out_v, gate_all, up_all, down_all),
        )
    }
    n_steps = len(links.rest)
    swap_spots = [links.take() for _ in range(CHUNKS)]
    cot_spot, end_spot = links.take(), links.take()
    trade = {links.core: links.h, links.high: links.c}

    def swap_copy(k):
        rows = pl.ds(k * chunk, chunk)
        return links.copy(x.at[rows], x_own.at[rows], trade, swap_spots[k])

    def swap_local(k):
        rows = pl.ds(k * chunk, chunk)
        return pltpu.make_async_copy(x.at[rows], x_own.at[rows], recv.at[swap_spots[k]])

    def cot_copy():
        return links.copy(cot, cot_own, trade, cot_spot)

    def cot_local():
        return pltpu.make_async_copy(cot, cot_own, recv.at[cot_spot])

    end_copy = links.copy(end_mine, end_other, links.across, end_spot)
    spread1 = Spread(links, norm1_v, own)
    norm2_v = norm1_v
    spread2 = Spread(links, norm2_v, own)
    across_spots = [links.take() for _ in range(n_parts)]
    line_spots = {
        (part, k): links.take() for part in range(1, n_parts) for k in range(CHUNKS)
    }

    links.greet()
    end_copy.start()
    weights["qkv"].send_near()
    weights["qkv"].send_far()

    @pl.when(links.same)
    def _():
        for k in range(CHUNKS):
            swap_local(k).start()

    @pl.when(~links.same)
    def _():
        for k in range(CHUNKS):
            swap_copy(k).start()

    for name in MATS[1:]:
        weights[name].send_near()

    def norm_chunk(k):
        rows = pl.ds(k * chunk, chunk)
        norm1_v[rows, :] = low(normed(x_own[rows, :].astype(jnp.float32)))
        spread1.own_ready(k)

    def run(name, *steps):
        for step in steps:
            weights[name].event(step)

    last = n_steps

    @pl.when(links.same)
    def _():
        for k in range(CHUNKS):
            swap_local(k).wait()
            norm_chunk(k)
        run("qkv", *range(last))
        run("out", *range(last))
        run("qkv", last)
        run("out", last)
        run("gate", 0)

    @pl.when(~links.same)
    def _():
        run("qkv", 0)
        for k in range(CHUNKS):
            swap_copy(k).wait_recv()
            norm_chunk(k)
            if k == 1:
                run("qkv", *range(1, last))
        run("qkv", last)

    weights["out"].send_far()
    end_copy.wait_recv()
    for k in range(CHUNKS):
        spread1.pass_on(k)

    keep = [pltpu.make_async_copy(qkv_v, qkv_all, local.at[0])]
    keep[0].start()

    def project(pieces):
        for section, goal in enumerate((q_ref, k_ref, v_ref)):
            for number in pieces:
                rows = slice(number * own, (number + 1) * own)
                spot = pl.ds(pl.multiple_of(links.swap_piece(number) * own, own), own)

                @pl.loop(0, heads // 2)
                def _(tile, section=section, goal=goal, rows=rows, spot=spot):
                    start = pl.multiple_of(tile * 2 * HD, 2 * HD)
                    made = dot(norm1_v[rows, :], qkv_v[:, pl.ds(section * width + start, 2 * HD)])
                    for k in range(2):
                        value = made[:, k * HD : (k + 1) * HD]
                        if section < 2:
                            value = spin(value, cos_ref[spot, :], sin_ref[spot, :])
                        goal[rows, pl.ds(pl.multiple_of(start + k * HD, HD), HD)] = low(value)

    spread1.wait_near()
    project((0, 1))
    weights["gate"].send_far()

    @pl.when(links.same)
    def _():
        run("gate", *range(1, last))

    @pl.when(~links.same)
    def _():
        run("out", 0)

    spread1.wait_far()
    project(range(2, n_pieces))
    keep.append(pltpu.make_async_copy(norm1_v, norm1, local.at[1]))
    keep[-1].start()
    weights["up"].send_far()

    @pl.when(links.same)
    def _():
        run("gate", last)
        run("up", 0)

    @pl.when(~links.same)
    def _():
        run("out", *range(1, last + 1))

    keep.append(pltpu.make_async_copy(out_v, out_all, local.at[2]))
    keep[-1].start()

    lanes = lax.broadcasted_iota(jnp.int32, (own, HD), 1)
    for head in range(heads):
        cols = slice(head * HD, (head + 1) * HD)

        @pl.loop(0, n_pieces)
        def _(i, head=head, cols=cols):
            rows = pl.ds(pl.multiple_of(i * own, own), own)
            quarter = links.swap_piece(i)

            def step(n, carry):
                top, total, acc = carry
                spot = pl.ds(pl.multiple_of(links.piece(n) * own, own), own)
                end = jnp.where(links.same, end_mine[pl.ds(n, 1), :], end_other[pl.ds(n, 1), :])
                allowed = allowed_of(quarter * own, n * own, end)
                scores = dot(q_ref[rows, cols], k_ref[spot, cols], NT)
                scores = jnp.where(allowed, scores * (SCALE * LOG2E), NEG)
                new_top = jnp.maximum(top, jnp.max(scores, axis=1, keepdims=True))
                grown = jnp.exp2(scores - new_top)
                shrink = jnp.exp2(top - new_top)
                total = total * shrink + jnp.sum(grown, axis=1, keepdims=True)
                return new_top, total, acc * shrink + dot(low(grown), v_ref[spot, cols])

            top, total, acc = lax.fori_loop(
                0, quarter + 1, step,
                (
                    jnp.full((own, 1), NEG, jnp.float32),
                    jnp.zeros((own, 1), jnp.float32),
                    jnp.zeros((own, HD), jnp.float32),
                ),
            )
            att_ref[rows, cols] = low(acc / total)
            lse = jnp.broadcast_to(top + jnp.log2(total), (own, HD))
            lse_ref[rows, :] = lse if head == 0 else jnp.where(lanes == head, lse, lse_ref[rows, :])

        if head == 0:
            weights["down"].send_far()

            @pl.when(links.same)
            def _():
                run("up", *range(1, last))

        if head == heads // 2 - 1:

            @pl.when(~links.same)
            def _():
                run("gate", 0)

        if head == heads // 2:

            @pl.when(links.same)
            def _():
                run("up", last)
                run("down", 0)

            @pl.when(~links.same)
            def _():
                run("gate", *range(1, last))

    @pl.when(links.same)
    def _():
        cot_local().start()
        run("down", *range(1, last))

    @pl.when(~links.same)
    def _():
        cot_copy().start()
        run("gate", last)

    keep.pop(1).wait()
    spread1.finish()

    def across_copy(part):
        return links.copy(p_other.at[part], p_come.at[part], links.across, across_spots[part])

    def line_copy(part, k):
        rows = pl.ds(k * chunk, chunk)
        step = n_low - part.bit_length()
        return links.copy(
            p_mine.at[part, rows], line.at[part - 1, rows], links.beside(step), line_spots[part, k]
        )

    def out_rows(number, goal):
        rows = slice(number * own, (number + 1) * own)
        tile = 512

        @pl.loop(0, out_v.shape[0] // tile)
        def _(n):
            start = pl.multiple_of(n * tile, tile)
            goal[:, pl.ds(start, tile)] = low(
                dot(att_ref[rows, :], out_v[pl.ds(start, tile), :], NT)
            )

    for part in reversed(range(n_parts)):
        out_rows(part * 2 + 1, p_other.at[part])
        across_copy(part).start()
        out_rows(part * 2, p_mine.at[part])
        across_copy(part).wait_recv()
        for k in range(CHUNKS):
            rows = pl.ds(k * chunk, chunk)
            total = p_mine[part, rows, :].astype(jnp.float32) + p_come[part, rows, :].astype(jnp.float32)
            if part == 0:
                hidden[rows, :] = x_own[rows, :].astype(jnp.float32) + total
            else:
                step = part.bit_length() - 1
                for high in range(step + 1, n_low):
                    more = part | 1 << high
                    line_copy(more, k).wait_recv()
                    total = total + line[more - 1, rows, :].astype(jnp.float32)
                p_mine[part, rows, :] = low(total)
                line_copy(part, k).start()

    @pl.when(links.same)
    def _():
        run("down", last)

    @pl.when(~links.same)
    def _():
        run("up", *range(last))

    for k in range(CHUNKS):
        rows = pl.ds(k * chunk, chunk)
        total = hidden[rows, :]
        for step in range(n_low):
            line_copy(1 << step, k).wait_recv()
            total = total + line[(1 << step) - 1, rows, :].astype(jnp.float32)
        hidden[rows, :] = total
        norm2_v[rows, :] = low(normed(total))
        spread2.own_ready(k)

    @pl.when(~links.same)
    def _():
        run("up", last)
        run("down", *range(last))

    for k in range(CHUNKS):
        spread2.pass_on(k)
    spread2.wait_near()
    spread2.wait_far()
    keep.append(pltpu.make_async_copy(norm2_v, norm2, local.at[3]))
    keep[-1].start()

    @pl.when(links.same)
    def _():
        cot_local().wait()

    @pl.when(~links.same)
    def _():
        run("down", last)
        cot_copy().wait()
        for k in range(CHUNKS):
            swap_copy(k).wait_send()

    end_copy.wait_send()
    spread2.finish()
    for weight in weights.values():
        weight.finish()
    for part in range(n_parts):
        across_copy(part).wait_send()
    for part, k in line_spots:
        line_copy(part, k).wait_send()
    for made in keep:
        made.wait()


def first_half(places, x, end_mine, cos, sin, mats, cot):
    own, model = x.shape
    n_parts = 2 ** len(places[3])
    length = 2 * n_parts * own
    groups = 2 ** len(places[0])
    width = mats[1].shape[1]
    shape = lambda *dims: jax.ShapeDtypeStruct(dims, jnp.bfloat16)
    wide = lambda *dims: jax.ShapeDtypeStruct(dims, jnp.float32)
    here, there = pl.BlockSpec(memory_space=pltpu.VMEM), pl.BlockSpec(memory_space=pl.ANY)
    fulls = [shape(2 * groups * mat.shape[0], mat.shape[1]) for mat in mats]
    bf = lambda *dims: pltpu.VMEM(dims, jnp.bfloat16)
    return pl.pallas_call(
        functools.partial(first_kernel, places),
        in_specs=[there, here, here, here] + [there] * 6,
        out_specs=[there] * 6 + [here] * 7 + [there] * 2,
        out_shape=[shape(length, model)]
        + fulls
        + [shape(length, width)] * 4
        + [wide(length, HD), shape(own, model), wide(own, model)]
        + [shape(length, model), shape(own, model)],
        scratch_shapes=[
            bf(length, model),
            bf(*fulls[0].shape),
            bf(*fulls[1].shape),
            pltpu.VMEM(end_mine.shape, jnp.int32),
            bf(n_parts, own, model),
            bf(n_parts, own, model),
            bf(n_parts, own, model),
            bf(max(n_parts - 1, 1), own, model),
            pltpu.SemaphoreType.DMA((SEMS,)),
            pltpu.SemaphoreType.DMA((SEMS,)),
            pltpu.SemaphoreType.DMA((4,)),
        ],
        compiler_params=pltpu.CompilerParams(
            collective_id=0, has_side_effects=True, vmem_limit_bytes=61 * 2**20
        ),
        cost_estimate=pl.CostEstimate(
            flops=8 * length * model * width,
            bytes_accessed=100 * 2**20,
            transcendentals=length * length * 4,
        ),
    )(x, end_mine, cos, sin, *mats, cot)


def hold(value, *after):
    return lax.optimization_barrier((value,) + after)[0]


def turn_tables(length):
    frequency = 10000.0 ** (-np.arange(HD // 2, dtype=np.float32) / np.float32(HD // 2))
    angles = np.arange(length, dtype=np.float32)[:, None] * frequency.astype(np.float32)[None, :]
    cos, sin = np.cos(angles), np.sin(angles)
    return (
        jnp.asarray(np.concatenate([cos, cos], axis=1), jnp.float32),
        jnp.asarray(np.concatenate([-sin, sin], axis=1), jnp.float32),
    )


def flip(value, axis):
    return lax.ppermute(value, axis, [(0, 1), (1, 0)])


def body(places, x, segments, padding, w_query, w_key, w_value, w_out, w_gate, w_up, w_down, cot):
    rest, core, high, lower = places
    pair = (core, high)
    c, h = lax.axis_index(core), lax.axis_index(high)
    same = c == h
    first_core = c == 0

    def swap(value):
        return lax.ppermute(value, pair, [(0, 0), (1, 2), (2, 1), (3, 3)])

    def gather_low(value):
        parts = [value]
        for axis in reversed(lower):
            parts = parts + [flip(part, axis) for part in parts]
        return parts

    def gather(value):
        parts = gather_low(value)
        return jnp.concatenate([piece for part in parts for piece in (part, flip(part, core))])

    def scatter(product, n_parts, after=None):
        far = []
        for part in reversed(range(n_parts)):
            mine, other = product(part)
            far.insert(0, (mine, flip(other, core)))
        sums = [mine.astype(jnp.float32) + other.astype(jnp.float32) for mine, other in far]
        for axis in lower:
            half = len(sums) // 2
            come = [flip(low(sums[half + k]), axis) for k in range(half)]
            if after is not None and axis == lower[-1]:
                come = [hold(part, *after) for part in come]
            sums = [sums[k] + come[k].astype(jnp.float32) for k in range(half)]
        return sums[0]

    def scatter_weight(partial):
        both = lax.psum_scatter(partial, rest, scatter_dimension=0, tiled=True)
        rows = both.shape[0] // 2
        s0, s1 = both[:rows], both[rows:]
        near = lax.ppermute(jnp.where(first_core, s1, s0), pair, [(0, 2), (3, 1)])
        from0 = lax.ppermute(s0, pair, [(1, 0), (2, 1)])
        from1 = lax.ppermute(s1, pair, [(1, 2), (2, 3)])
        kept = jnp.where(same, jnp.where(first_core, s0, s1), near)
        far = jnp.where(first_core, from0, from1)
        return kept.astype(jnp.float32) + far.astype(jnp.float32)

    own = x.shape[0]
    n_parts = 2 ** len(lower)
    length = 2 * n_parts * own
    cols = w_query.shape[1]
    heads = cols // HD
    blk = min(512, own)

    spot = jnp.int32(0)
    for axis in lower:
        spot = spot * 2 + lax.axis_index(axis)
    quarters = []
    for part in range(n_parts):
        for other in (0, 1):
            quarters.append((c ^ other) * n_parts + (spot ^ part))
    position = jnp.concatenate([q * own + jnp.arange(own, dtype=jnp.int32) for q in quarters])
    counts = [jnp.sum(segments <= number, dtype=jnp.int32) for number in range(3)]
    last = jnp.where(segments == 0, counts[0], jnp.where(segments == 1, counts[1], counts[2])) - 1
    end_own = jnp.where(padding == 0, last, jnp.arange(length, dtype=jnp.int32))
    end = jnp.where(same, end_own, flip(end_own, core))
    end = jnp.concatenate([lax.dynamic_slice_in_dim(end, q * own, own) for q in quarters])
    lists = visit_lists(position, end, blk)
    end_rows = end.reshape(-1, blk)
    cos_all, sin_all = turn_tables(length)
    cos = jnp.concatenate([lax.dynamic_slice_in_dim(cos_all, q * own, own) for q in quarters])
    sin = jnp.concatenate([lax.dynamic_slice_in_dim(sin_all, q * own, own) for q in quarters])
    mats = (jnp.concatenate([w_query, w_key, w_value], axis=1), w_out, w_gate, w_up, w_down)
    (norm1, w_qkv, full_out, full_gate, full_up, full_down, q, k, v, attended, lse, x_low, hidden, norm2,
     cot_own) = first_half(places, x, end_own.reshape(-1, own), cos_all, sin_all, mats, cot)
    x_own = x_low.astype(jnp.float32)
    norm1_pull = jax.vjp(layer_norm, x_own)[1]
    norm2_pull = jax.vjp(layer_norm, hidden)[1]
    cots = gather(cot_own)

    def halves(product, values):
        def of(part):
            lo = part * 2 * own
            both = low(product(*(value[lo : lo + 2 * own] for value in values)))
            return both[:own], both[own:]

        return of

    gate = dot(norm2, full_gate)
    up_lin = dot(norm2, full_up)
    act, act_pull = jax.vjp(swiglu, gate, up_lin)
    act_low = low(act)
    d_act = dot(cots, full_down)
    d_gate_f, d_up_f = act_pull(d_act)
    d_gate, d_up = low(d_gate_f), low(d_up_f)
    p_down = low(dot(cots, act_low, TN))
    p_mlp = [halves(lambda a: dot(a, full_down, NT), (act_low,))(part) for part in range(n_parts)]
    d_norm2 = scatter(
        halves(lambda a, b: dot(a, full_gate, NT) + dot(b, full_up, NT), (d_gate, d_up)),
        n_parts,
        [p_down] + [half for part in p_mlp for half in part],
    )
    d_hidden = cot_own.astype(jnp.float32) + norm2_pull(d_norm2)[0]
    p_gate = low(dot(norm2, d_gate, TN))
    p_up = low(dot(norm2, d_up, TN))
    d_hiddens = hold(gather(low(d_hidden)), p_gate, p_up)

    mlp = scatter(lambda part: p_mlp[part], n_parts)
    output = swap(low(hidden + mlp))
    g_down, g_gate, g_up = scatter_weight(p_down), scatter_weight(p_gate), scatter_weight(p_up)

    d_attended = low(dot(d_hiddens, full_out))
    dq, dk, dv = attend_back(q, k, v, d_attended, attended, lse, cos, sin, end_rows, lists, heads, 1)
    d_qkv = jnp.concatenate([dq, dk, dv], axis=1)
    d_norm1 = scatter(halves(lambda a: dot(a, w_qkv, NT), (d_qkv,)), n_parts)
    d_input = swap(low(d_hidden + norm1_pull(d_norm1)[0])).astype(jnp.float32)
    g_out = scatter_weight(low(dot(d_hiddens, attended, TN)))
    g_qkv = scatter_weight(low(dot(norm1, d_qkv, TN)))
    return (
        output,
        d_input,
        g_qkv[:, :cols],
        g_qkv[:, cols : 2 * cols],
        g_qkv[:, 2 * cols :],
        g_out,
        g_gate,
        g_up,
        g_down,
    )


def solution(mesh):
    dp, mp = mesh.devices.shape
    n_dp, n_mp = dp.bit_length() - 1, mp.bit_length() - 1
    dp_axes = tuple("d%d" % k for k in range(n_dp))
    mp_axes = tuple("m%d" % k for k in range(n_mp))
    fine = Mesh(mesh.devices.reshape((2,) * (n_dp + n_mp)), dp_axes + mp_axes)
    places = (dp_axes[:-1], dp_axes[-1], mp_axes[0], mp_axes[1:])
    tokens = P(dp_axes + mp_axes, None)
    weight = P(dp_axes, mp_axes)
    return jax.shard_map(
        functools.partial(body, places),
        mesh=fine,
        in_specs=(tokens, P(dp_axes), P(dp_axes)) + (weight,) * 7 + (tokens,),
        out_specs=(tokens, tokens) + (weight,) * 7,
        check_vma=False,
    )
```

```python
import functools
import jax
import jax.numpy as jnp
import numpy as np
from jax import lax
from jax.experimental import pallas as pl
from jax.experimental.pallas import tpu as pltpu
from jax.sharding import Mesh, PartitionSpec as P

HD = 128
SCALE = HD ** (-0.5)
LOG2E = 1.4426950408889634
NEG = -1e30
eps = 1e-05
NN = (((1,), (0,)), ((), ()))
NT = (((1,), (1,)), ((), ()))
TN = (((0,), (0,)), ((), ()))


def dot(left, right, dims=(((1,), (0,)), ((), ()))):
    return lax.dot_general(left, right, dims, preferred_element_type=jnp.float32)


def low(value):
    return value.astype(jnp.bfloat16)

def allowed_of(first_q, first_k, end_row):
    blk = end_row.shape[1]
    t = first_q + lax.broadcasted_iota(jnp.int32, (blk, 1), 0)
    u = first_k + lax.broadcasted_iota(jnp.int32, (1, blk), 1)
    return (u <= t) & (t <= end_row)


MESH = pl.DeviceIdType.MESH
CHUNKS = 4
SEMS = 224
MATS = ("qkv", "out", "gate", "up", "down")


def flipped(bit, other):
    return bit + other - 2 * bit * other


class Links:
    def __init__(self, places, send, recv):
        self.rest, self.core, self.high, self.lower = places
        self.c, self.h = lax.axis_index(self.core), lax.axis_index(self.high)
        self.r = [lax.axis_index(axis) for axis in self.rest]
        self.low = [lax.axis_index(axis) for axis in self.lower]
        self.same = self.c == self.h
        self.n_parts = 2 ** len(self.lower)
        self.send, self.recv, self.used, self.unsent = send, recv, 0, []
        self.across = {self.core: 1 - self.c}

    def beside(self, k):
        return {self.lower[k]: 1 - self.low[k]}

    def over(self, k):
        return {self.rest[k]: 1 - self.r[k]}

    def group(self, mask):
        total = 0
        for k, bit in enumerate(self.r):
            total = total * 2 + (1 - bit if mask >> k & 1 else bit)
        return total

    def swap_piece(self, number):
        other, part = number % 2, number // 2
        return flipped(self.c, other) * self.n_parts + self.turn(part)

    def piece(self, quarter):
        other, part = flipped(self.c, quarter // self.n_parts), self.turn(quarter % self.n_parts)
        return part * 2 + other

    def turn(self, part):
        total = 0
        for k, bit in enumerate(self.low):
            digit = part // 2 ** (len(self.low) - 1 - k) % 2
            total = total * 2 + flipped(bit, digit)
        return total

    def greet(self):
        barrier = pltpu.get_barrier_semaphore()
        partners = [
            self.across,
            {self.high: 1 - self.h},
            {self.core: 1 - self.c, self.high: 1 - self.h},
        ]
        partners += [self.beside(k) for k in range(len(self.lower))]
        partners += [self.over(k) for k in range(len(self.rest))]
        for partner in partners:
            pl.semaphore_signal(barrier, inc=1, device_id=partner, device_id_type=MESH)
        pl.semaphore_wait(barrier, len(partners))

    def take(self, count=1):
        self.used += count
        return self.used - count

    def copy(self, src, dst, partner, spot=None, recv=None):
        spot = self.take() if spot is None else spot
        made = pltpu.make_async_remote_copy(
            src_ref=src, dst_ref=dst, send_sem=self.send.at[spot],
            recv_sem=self.recv.at[spot if recv is None else recv],
            device_id=partner, device_id_type=MESH,
        )
        return made

    def push(self, src, dst, partner):
        made = self.copy(src, dst, partner)
        made.start()
        self.unsent.append(made)
        return made


class Weight:
    def __init__(self, links, shard, full):
        self.links, self.shard, self.full = links, shard, full
        self.rows = shard.shape[0]
        self.arrive = links.take(2)
        self.near, self.far = links.take(), links.take()
        self.stages = []
        n = len(links.rest)
        for step in range(n):
            stage = []
            for half in range(2):
                order = list(range(n)) if half == 0 else list(reversed(range(n)))
                have = [0]
                for k in order[:step]:
                    have = have + [mask | 1 << k for mask in have]
                stage += [(half, mask, order[step], links.take()) for mask in have]
            self.stages.append(stage)

    def slot(self, mask, core):
        start = (self.links.group(mask) * 2 + core) * self.rows
        return self.full.at[pl.ds(pl.multiple_of(start, self.rows), self.rows)]

    def near_copy(self):
        links = self.links
        return links.copy(
            self.shard, self.slot(0, links.c), links.across, self.near, self.arrive + links.c
        )

    def far_copy(self):
        links = self.links
        return links.copy(
            self.shard, self.slot(0, links.c), {links.core: links.h, links.high: 1 - links.h},
            self.far, self.arrive + links.c,
        )

    def send_near(self):
        links = self.links

        @pl.when(links.same)
        def _():
            pltpu.make_async_copy(
                self.shard, self.slot(0, links.c), links.recv.at[self.arrive + links.c]
            ).start()

        @pl.when(~links.same)
        def _():
            self.near_copy().start()

    def send_far(self):
        self.far_copy().start()

    def stage_copies(self, step):
        for half, mask, axis, spot in self.stages[step]:
            block = self.slot(mask, half)
            yield self.links.copy(block, block, self.links.over(axis), spot)

    def event(self, step):
        if step == 0:
            for core in range(2):
                block = self.slot(0, core)
                pltpu.make_async_copy(block, block, self.links.recv.at[self.arrive + core]).wait()
        else:
            for copy in self.stage_copies(step - 1):
                copy.wait_recv()
        if step < len(self.stages):
            for copy in self.stage_copies(step):
                copy.start()

    def finish(self):
        @pl.when(~self.links.same)
        def _():
            self.near_copy().wait_send()

        self.far_copy().wait_send()
        for step in range(len(self.stages)):
            for copy in self.stage_copies(step):
                copy.wait_send()


class Spread:
    def __init__(self, links, full, own):
        self.links, self.full, self.own, self.chunk = links, full, own, own // CHUNKS
        self.moves = {}
        n = len(links.lower)
        for k in range(CHUNKS):
            have = [0]
            for step in range(n):
                value = 2 ** (n - 1 - step)
                for part in have:
                    self.moves[k, part, step] = (part | value, links.take())
                have = have + [part | value for part in have]
            for part in range(links.n_parts):
                self.moves[k, part, None] = (part, links.take())

    def rows(self, part, other, k):
        return pl.ds((part * 2 + other) * self.own + k * self.chunk, self.chunk)

    def made(self, k, part, step, src=None):
        goal, spot = self.moves[k, part, step]
        links = self.links
        partner = links.across if step is None else links.beside(step)
        src = self.full.at[self.rows(part, 0, k)] if src is None else src
        dst = self.full.at[self.rows(goal, 1 if step is None else 0, k)]
        return links.copy(src, dst, partner, spot)

    def first_step(self, part):
        n = len(self.links.lower)
        return [s for s in range(n) if (0, part, s) in self.moves]

    def own_ready(self, k):
        for step in self.first_step(0):
            self.made(k, 0, step).start()
        self.made(k, 0, None).start()

    def pass_on(self, k):
        n = len(self.links.lower)
        for step in range(n):
            value = 2 ** (n - 1 - step)
            for part in range(self.links.n_parts):
                if (k, part, step) in self.moves:
                    self.made(k, part, step).wait_recv()
                    goal = part | value
                    for later in self.first_step(goal):
                        self.made(k, goal, later).start()
                    self.made(k, goal, None).start()

    def wait_near(self):
        for k in range(CHUNKS):
            self.made(k, 0, None).wait_recv()

    def wait_far(self):
        for k in range(CHUNKS):
            for part in range(1, self.links.n_parts):
                self.made(k, part, None).wait_recv()

    def finish(self):
        for k, part, step in self.moves:
            self.made(k, part, step).wait_send()


def normed(value):
    average = jnp.mean(value, axis=-1, keepdims=True)
    centred = value - average
    variance = jnp.mean(centred * centred, axis=-1, keepdims=True)
    return centred * lax.rsqrt(variance + eps)


def spin(value, cos, sin):
    return value * cos + pltpu.roll(value, HD // 2, 1) * sin


def first_kernel(
    places, x, end_mine, cos_ref, sin_ref, w_qkv, w_out, w_gate, w_up, w_down, cot,
    norm1, qkv_all, out_all, gate_all, up_all, down_all, q_ref, k_ref, v_ref, att_ref, lse_ref, x_own, hidden,
    norm2, cot_own, norm1_v, qkv_v, out_v, end_other, p_mine, p_other, p_come, line, send, recv, local,
):
    links = Links(places, send, recv)
    own = x.shape[0]
    n_parts, n_pieces = links.n_parts, 2 * links.n_parts
    n_low = len(links.lower)
    chunk = own // CHUNKS
    heads = q_ref.shape[1] // HD
    width = heads * HD
    weights = {
        name: Weight(links, shard, full)
        for name, shard, full in zip(
            MATS,
            (w_qkv, w_out, w_gate, w_up, w_down),
            (qkv_v, out_v, gate_all, up_all, down_all),
        )
    }
    n_steps = len(links.rest)
    swap_spots = [links.take() for _ in range(CHUNKS)]
    cot_spot, end_spot = links.take(), links.take()
    trade = {links.core: links.h, links.high: links.c}

    def swap_copy(k):
        rows = pl.ds(k * chunk, chunk)
        return links.copy(x.at[rows], x_own.at[rows], trade, swap_spots[k])

    def swap_local(k):
        rows = pl.ds(k * chunk, chunk)
        return pltpu.make_async_copy(x.at[rows], x_own.at[rows], recv.at[swap_spots[k]])

    def cot_copy():
        return links.copy(cot, cot_own, trade, cot_spot)

    def cot_local():
        return pltpu.make_async_copy(cot, cot_own, recv.at[cot_spot])

    end_copy = links.copy(end_mine, end_other, links.across, end_spot)
    spread1 = Spread(links, norm1_v, own)
    norm2_v = norm1_v
    spread2 = Spread(links, norm2_v, own)
    across_spots = [links.take() for _ in range(n_parts)]
    line_spots = {
        (part, k): links.take() for part in range(1, n_parts) for k in range(CHUNKS)
    }

    links.greet()
    end_copy.start()
    weights["qkv"].send_near()
    weights["qkv"].send_far()

    @pl.when(links.same)
    def _():
        for k in range(CHUNKS):
            swap_local(k).start()

    @pl.when(~links.same)
    def _():
        for k in range(CHUNKS):
            swap_copy(k).start()

    for name in MATS[1:]:
        weights[name].send_near()

    def norm_chunk(k):
        rows = pl.ds(k * chunk, chunk)
        norm1_v[rows, :] = low(normed(x_own[rows, :].astype(jnp.float32)))
        spread1.own_ready(k)

    def run(name, *steps):
        for step in steps:
            weights[name].event(step)

    last = n_steps

    @pl.when(links.same)
    def _():
        for k in range(CHUNKS):
            swap_local(k).wait()
            norm_chunk(k)
        run("qkv", *range(last))
        run("out", *range(last))
        run("qkv", last)
        run("out", last)
        run("gate", 0)

    @pl.when(~links.same)
    def _():
        run("qkv", 0)
        for k in range(CHUNKS):
            swap_copy(k).wait_recv()
            norm_chunk(k)
            if k == 1:
                run("qkv", *range(1, last))
        run("qkv", last)

    weights["out"].send_far()
    end_copy.wait_recv()
    for k in range(CHUNKS):
        spread1.pass_on(k)

    keep = [pltpu.make_async_copy(qkv_v, qkv_all, local.at[0])]
    keep[0].start()

    def project(pieces):
        for section, goal in enumerate((q_ref, k_ref, v_ref)):
            for number in pieces:
                rows = slice(number * own, (number + 1) * own)
                spot = pl.ds(pl.multiple_of(links.swap_piece(number) * own, own), own)

                @pl.loop(0, heads // 2)
                def _(tile, section=section, goal=goal, rows=rows, spot=spot):
                    start = pl.multiple_of(tile * 2 * HD, 2 * HD)
                    made = dot(norm1_v[rows, :], qkv_v[:, pl.ds(section * width + start, 2 * HD)])
                    for k in range(2):
                        value = made[:, k * HD : (k + 1) * HD]
                        if section < 2:
                            value = spin(value, cos_ref[spot, :], sin_ref[spot, :])
                        goal[rows, pl.ds(pl.multiple_of(start + k * HD, HD), HD)] = low(value)

    spread1.wait_near()
    project((0, 1))
    weights["gate"].send_far()

    @pl.when(links.same)
    def _():
        run("gate", *range(1, last))

    @pl.when(~links.same)
    def _():
        run("out", 0)

    spread1.wait_far()
    project(range(2, n_pieces))
    keep.append(pltpu.make_async_copy(norm1_v, norm1, local.at[1]))
    keep[-1].start()
    weights["up"].send_far()

    @pl.when(links.same)
    def _():
        run("gate", last)
        run("up", 0)

    @pl.when(~links.same)
    def _():
        run("out", *range(1, last + 1))

    keep.append(pltpu.make_async_copy(out_v, out_all, local.at[2]))
    keep[-1].start()

    lanes = lax.broadcasted_iota(jnp.int32, (own, HD), 1)
    for head in range(heads):
        cols = slice(head * HD, (head + 1) * HD)

        @pl.loop(0, n_pieces)
        def _(i, head=head, cols=cols):
            rows = pl.ds(pl.multiple_of(i * own, own), own)
            quarter = links.swap_piece(i)

            def step(n, carry):
                top, total, acc = carry
                spot = pl.ds(pl.multiple_of(links.piece(n) * own, own), own)
                end = jnp.where(links.same, end_mine[pl.ds(n, 1), :], end_other[pl.ds(n, 1), :])
                allowed = allowed_of(quarter * own, n * own, end)
                scores = dot(q_ref[rows, cols], k_ref[spot, cols], NT)
                scores = jnp.where(allowed, scores * (SCALE * LOG2E), NEG)
                new_top = jnp.maximum(top, jnp.max(scores, axis=1, keepdims=True))
                grown = jnp.exp2(scores - new_top)
                shrink = jnp.exp2(top - new_top)
                total = total * shrink + jnp.sum(grown, axis=1, keepdims=True)
                return new_top, total, acc * shrink + dot(low(grown), v_ref[spot, cols])

            top, total, acc = lax.fori_loop(
                0, quarter + 1, step,
                (
                    jnp.full((own, 1), NEG, jnp.float32),
                    jnp.zeros((own, 1), jnp.float32),
                    jnp.zeros((own, HD), jnp.float32),
                ),
            )
            att_ref[rows, cols] = low(acc / total)
            lse = jnp.broadcast_to(top + jnp.log2(total), (own, HD))
            lse_ref[rows, :] = lse if head == 0 else jnp.where(lanes == head, lse, lse_ref[rows, :])

        if head == 0:
            weights["down"].send_far()

            @pl.when(links.same)
            def _():
                run("up", *range(1, last))

        if head == heads // 2 - 1:

            @pl.when(~links.same)
            def _():
                run("gate", 0)

        if head == heads // 2:

            @pl.when(links.same)
            def _():
                run("up", last)
                run("down", 0)

            @pl.when(~links.same)
            def _():
                run("gate", *range(1, last))

    @pl.when(links.same)
    def _():
        cot_local().start()
        run("down", *range(1, last))

    @pl.when(~links.same)
    def _():
        cot_copy().start()
        run("gate", last)

    keep.pop(1).wait()
    spread1.finish()

    def across_copy(part):
        return links.copy(p_other.at[part], p_come.at[part], links.across, across_spots[part])

    def line_copy(part, k):
        rows = pl.ds(k * chunk, chunk)
        step = n_low - part.bit_length()
        return links.copy(
            p_mine.at[part, rows], line.at[part - 1, rows], links.beside(step), line_spots[part, k]
        )

    def out_rows(number, goal):
        rows = slice(number * own, (number + 1) * own)
        tile = 512

        @pl.loop(0, out_v.shape[0] // tile)
        def _(n):
            start = pl.multiple_of(n * tile, tile)
            goal[:, pl.ds(start, tile)] = low(
                dot(att_ref[rows, :], out_v[pl.ds(start, tile), :], NT)
            )

    for part in reversed(range(n_parts)):
        out_rows(part * 2 + 1, p_other.at[part])
        across_copy(part).start()
        out_rows(part * 2, p_mine.at[part])
        across_copy(part).wait_recv()
        for k in range(CHUNKS):
            rows = pl.ds(k * chunk, chunk)
            total = p_mine[part, rows, :].astype(jnp.float32) + p_come[part, rows, :].astype(jnp.float32)
            if part == 0:
                hidden[rows, :] = x_own[rows, :].astype(jnp.float32) + total
            else:
                step = part.bit_length() - 1
                for high in range(step + 1, n_low):
                    more = part | 1 << high
                    line_copy(more, k).wait_recv()
                    total = total + line[more - 1, rows, :].astype(jnp.float32)
                p_mine[part, rows, :] = low(total)
                line_copy(part, k).start()

    @pl.when(links.same)
    def _():
        run("down", last)

    @pl.when(~links.same)
    def _():
        run("up", *range(last))

    for k in range(CHUNKS):
        rows = pl.ds(k * chunk, chunk)
        total = hidden[rows, :]
        for step in range(n_low):
            line_copy(1 << step, k).wait_recv()
            total = total + line[(1 << step) - 1, rows, :].astype(jnp.float32)
        hidden[rows, :] = total
        norm2_v[rows, :] = low(normed(total))
        spread2.own_ready(k)

    @pl.when(~links.same)
    def _():
        run("up", last)
        run("down", *range(last))

    for k in range(CHUNKS):
        spread2.pass_on(k)
    spread2.wait_near()
    spread2.wait_far()
    keep.append(pltpu.make_async_copy(norm2_v, norm2, local.at[3]))
    keep[-1].start()

    @pl.when(links.same)
    def _():
        cot_local().wait()

    @pl.when(~links.same)
    def _():
        run("down", last)
        cot_copy().wait()
        for k in range(CHUNKS):
            swap_copy(k).wait_send()

    end_copy.wait_send()
    spread2.finish()
    for weight in weights.values():
        weight.finish()
    for part in range(n_parts):
        across_copy(part).wait_send()
    for part, k in line_spots:
        line_copy(part, k).wait_send()
    for made in keep:
        made.wait()


def first_half(places, x, end_mine, cos, sin, mats, cot):
    own, model = x.shape
    n_parts = 2 ** len(places[3])
    length = 2 * n_parts * own
    groups = 2 ** len(places[0])
    width = mats[1].shape[1]
    shape = lambda *dims: jax.ShapeDtypeStruct(dims, jnp.bfloat16)
    wide = lambda *dims: jax.ShapeDtypeStruct(dims, jnp.float32)
    here, there = pl.BlockSpec(memory_space=pltpu.VMEM), pl.BlockSpec(memory_space=pl.ANY)
    fulls = [shape(2 * groups * mat.shape[0], mat.shape[1]) for mat in mats]
    bf = lambda *dims: pltpu.VMEM(dims, jnp.bfloat16)
    return pl.pallas_call(
        functools.partial(first_kernel, places),
        in_specs=[there, here, here, here] + [there] * 6,
        out_specs=[there] * 6 + [here] * 7 + [there] * 2,
        out_shape=[shape(length, model)]
        + fulls
        + [shape(length, width)] * 4
        + [wide(length, HD), shape(own, model), wide(own, model)]
        + [shape(length, model), shape(own, model)],
        scratch_shapes=[
            bf(length, model),
            bf(*fulls[0].shape),
            bf(*fulls[1].shape),
            pltpu.VMEM(end_mine.shape, jnp.int32),
            bf(n_parts, own, model),
            bf(n_parts, own, model),
            bf(n_parts, own, model),
            bf(max(n_parts - 1, 1), own, model),
            pltpu.SemaphoreType.DMA((SEMS,)),
            pltpu.SemaphoreType.DMA((SEMS,)),
            pltpu.SemaphoreType.DMA((4,)),
        ],
        compiler_params=pltpu.CompilerParams(
            collective_id=0, has_side_effects=True, vmem_limit_bytes=61 * 2**20
        ),
        cost_estimate=pl.CostEstimate(
            flops=8 * length * model * width,
            bytes_accessed=100 * 2**20,
            transcendentals=length * length * 4,
        ),
    )(x, end_mine, cos, sin, *mats, cot)


def matmul(kind, left, right, out, rows, cols):
    depth = left.shape[0] if kind == TN else left.shape[1]

    def tile(a, b, made):
        made[...] = low(dot(a[...], b[...], kind))

    a_spec = (
        pl.BlockSpec((depth, rows), lambda i, j: (0, i))
        if kind == TN
        else pl.BlockSpec((rows, depth), lambda i, j: (i, 0))
    )
    b_spec = (
        pl.BlockSpec((cols, depth), lambda i, j: (j, 0))
        if kind == NT
        else pl.BlockSpec((depth, cols), lambda i, j: (0, j))
    )
    pltpu.emit_pipeline(
        tile,
        grid=(out.shape[0] // rows, out.shape[1] // cols),
        in_specs=[a_spec, b_spec],
        out_specs=[pl.BlockSpec((rows, cols), lambda i, j: (i, j))],
    )(left, right, out)


def two_products(left1, right1, left2, right2, out, cols):
    def tile(a, b, c, d, made):
        made[...] = low(dot(a[...], b[...], NT) + dot(c[...], d[...], NT))

    rows, depth = left1.shape
    held = pl.BlockSpec((rows, depth), lambda j: (0, 0))
    moving = pl.BlockSpec((cols, depth), lambda j: (j, 0))
    pltpu.emit_pipeline(
        tile,
        grid=(out.shape[1] // cols,),
        in_specs=[held, moving, held, moving],
        out_specs=[pl.BlockSpec((rows, cols), lambda j: (0, j))],
    )(left1, right1, left2, right2, out)


def by_rows(make, rows, ins, outs):
    spec = lambda ref: pl.BlockSpec((rows, ref.shape[1]), lambda i: (i, 0))
    pltpu.emit_pipeline(
        make,
        grid=(outs[0].shape[0] // rows,),
        in_specs=[spec(ref) for ref in ins],
        out_specs=[spec(ref) for ref in outs],
    )(*ins, *outs)


def gated(norm, cots, w_gate, w_up, w_down, act, d_gate, d_up, rows, cols):
    def tile(n, c, wg, wu, wd, act_t, gate_t, up_t):
        gate, up = dot(n[...], wg[...]), dot(n[...], wu[...])
        d_act = dot(c[...], wd[...])
        s = 1.0 / (1.0 + jnp.exp(-gate))
        silu = gate * s
        act_t[...] = low(silu * up)
        gate_t[...] = low(d_act * up * s * (1.0 + gate * (1.0 - s)))
        up_t[...] = low(d_act * silu)

    depth = norm.shape[1]
    row = pl.BlockSpec((rows, depth), lambda i, j: (i, 0))
    col = pl.BlockSpec((depth, cols), lambda i, j: (0, j))
    made = pl.BlockSpec((rows, cols), lambda i, j: (i, j))
    pltpu.emit_pipeline(
        tile,
        grid=(act.shape[0] // rows, act.shape[1] // cols),
        in_specs=[row, row, col, col, col],
        out_specs=[made] * 3,
    )(norm, cots, w_gate, w_up, w_down, act, d_gate, d_up)


def norm_back(value, grad):
    average = jnp.mean(value, axis=-1, keepdims=True)
    centred = value - average
    r = lax.rsqrt(jnp.mean(centred * centred, axis=-1, keepdims=True) + eps)
    n = centred * r
    return r * (
        grad - jnp.mean(grad, axis=-1, keepdims=True) - n * jnp.mean(grad * n, axis=-1, keepdims=True)
    )


class Sums:
    def __init__(self, links, mine, other, come, ready, line):
        self.links, self.mine, self.other = links, mine, other
        self.come, self.ready, self.line = come, ready, line
        n_parts, self.own, _ = mine.shape
        self.chunk = self.own // CHUNKS
        self.spots = [links.take() for _ in range(n_parts)]
        self.line_spots = {
            (part, k): links.take() for part in range(1, n_parts) for k in range(CHUNKS)
        }

    def across(self, part):
        links = self.links
        return links.copy(self.other.at[part], self.come.at[part], links.across, self.spots[part])

    def along(self, part, k):
        links = self.links
        rows = pl.ds(k * self.chunk, self.chunk)
        step = len(links.lower) - part.bit_length()
        return links.copy(
            self.ready.at[part - 1, rows], self.line.at[part - 1, rows], links.beside(step),
            self.line_spots[part, k],
        )

    def more(self, part):
        return [part | 1 << k for k in range(part.bit_length(), len(self.links.lower))]

    def far(self, part):
        self.across(part).wait_recv()
        ins = [self.mine.at[part], self.come.at[part]]
        for number in self.more(part):
            for k in range(CHUNKS):
                self.along(number, k).wait_recv()
            ins.append(self.line.at[number - 1])

        def make(*refs):
            total = refs[0][...].astype(jnp.float32)
            for ref in refs[1:-1]:
                total = total + ref[...].astype(jnp.float32)
            refs[-1][...] = low(total)

        by_rows(make, self.chunk, ins, [self.ready.at[part - 1]])
        for k in range(CHUNKS):
            self.along(part, k).start()

    def arrived(self, k):
        if k == 0:
            self.across(0).wait_recv()
        for number in self.more(0):
            self.along(number, k).wait_recv()

    def terms(self, rows):
        return [self.mine.at[0, rows], self.come.at[0, rows]] + [
            self.line.at[number - 1, rows] for number in self.more(0)
        ]

    def finish(self):
        for part in range(self.mine.shape[0]):
            self.across(part).wait_send()
        for part, k in self.line_spots:
            self.along(part, k).wait_send()


class Gradient:
    def __init__(self, links, partial, come, stage, stage_sems, near, far):
        self.links, self.partial, self.come, self.stage = links, partial, come, stage
        self.stage_sems, self.near, self.far = stage_sems, near, far
        self.rows = near.shape[0]
        n = len(links.rest)
        self.n = n
        self.kept, self.sent, self.place, self.spots = {}, {}, {}, {}
        for half in range(2):
            order = list(reversed(range(n))) if half == 0 else list(range(n))
            have = list(range(2**n))
            for step, axis in enumerate(order):
                self.sent[half, step] = (axis, [mask for mask in have if mask >> axis & 1])
                have = [mask for mask in have if not mask >> axis & 1]
                self.kept[half, step] = have
                for mask in have:
                    self.place[half, step, mask] = len(self.place)
                    self.spots[half, step, mask] = links.take()
        self.near_spot, self.far_spot = links.take(), links.take()
        self.out_spots = [links.take(), links.take()]

    def slot(self, mask, half):
        start = (self.links.group(mask) * 2 + half) * self.rows
        return self.partial.at[pl.ds(pl.multiple_of(start, self.rows), self.rows)]

    def block(self, half, step, mask):
        return self.come.at[self.place[half, step, mask]]

    def copies(self, step):
        for half in range(2):
            axis, masks = self.sent[half, step]
            for mask in masks:
                goal = mask & ~(1 << axis)
                src = self.slot(mask, half) if step == 0 else self.block(half, step - 1, mask)
                yield self.links.copy(
                    src, self.block(half, step, goal), self.links.over(axis), self.spots[half, step, goal]
                )

    def loads(self):
        number = 0
        for half in range(2):
            for mask in self.kept[half, 0]:
                yield pltpu.make_async_copy(
                    self.slot(mask, half), self.stage.at[number], self.stage_sems.at[number]
                )
                number += 1

    def start(self):
        for copy in self.copies(0):
            copy.start()
        for load in self.loads():
            load.start()

    def step(self, step):
        for copy in self.copies(step):
            copy.wait_recv()
        if step == 0:
            for load in self.loads():
                load.wait()
        number = 0
        for half in range(2):
            for mask in self.kept[half, step]:
                goal = self.block(half, step, mask)
                add = self.stage.at[number] if step == 0 else self.block(half, step - 1, mask)
                number += 1
                rows = min(64, self.rows)

                @pl.loop(0, self.rows // rows)
                def _(i, goal=goal, add=add):
                    spot = pl.ds(pl.multiple_of(i * rows, rows), rows)
                    goal[spot, :] = low(
                        goal[spot, :].astype(jnp.float32) + add[spot, :].astype(jnp.float32)
                    )

        if step + 1 < self.n:
            for copy in self.copies(step + 1):
                copy.start()
        else:
            self.hand()

    def total(self, half):
        first, second = (self.place[k, self.n - 1, 0] for k in range(2))
        return self.come.at[first + half * (second - first)]

    def near_local(self):
        links = self.links
        return pltpu.make_async_copy(self.total(links.c), self.near, links.recv.at[self.near_spot])

    def near_copy(self):
        links = self.links
        return links.copy(self.total(1 - links.c), self.near, links.across, self.near_spot)

    def far_copy(self, half):
        links = self.links
        return links.copy(
            self.total(half), self.far, {links.core: half, links.high: links.c},
            self.out_spots[half], self.far_spot,
        )

    def hand(self):
        links = self.links

        @pl.when(links.same)
        def _():
            self.near_local().start()
            self.near_copy().start()

        @pl.when(~links.same)
        def _():
            for half in range(2):
                self.far_copy(half).start()

    def finish(self):
        links = self.links
        for step in range(self.n):
            for copy in self.copies(step):
                copy.wait_send()

        @pl.when(links.same)
        def _():
            self.near_local().wait()
            self.near_copy().wait_send()

        @pl.when(~links.same)
        def _():
            self.near_copy().wait_recv()
            for half in range(2):
                self.far_copy(half).wait_send()

        self.far_copy(0).wait_recv()


def attention_back(links, q, k, v, grad, att, lse_ref, cos_ref, sin_ref, end_ref, d_q, d_k, d_v, heads, start):
    length = q.shape[0]
    n_pieces, own = end_ref.shape

    def scoped(dq_acc, dk_acc, dv_acc, delta, lses):
        def one(q_ref, k_ref, v_ref, grad_ref, att_ref, dq_ref, dk_ref, dv_ref):
            head = pl.program_id(0) + start
            dq_acc[...] = jnp.zeros_like(dq_acc)
            dk_acc[...] = jnp.zeros_like(dk_acc)
            dv_acc[...] = jnp.zeros_like(dv_acc)
            lanes = lax.broadcasted_iota(jnp.int32, lse_ref.shape, 1)
            mine = jnp.where(lanes == head, lse_ref[...], 0.0)
            lses[...] = jnp.broadcast_to(jnp.sum(mine, axis=1, keepdims=True), mine.shape)
            prod = grad_ref[...].astype(jnp.float32) * att_ref[...].astype(jnp.float32)
            delta[...] = jnp.broadcast_to(jnp.sum(prod, axis=1, keepdims=True), prod.shape)

            @pl.loop(0, n_pieces)
            def _(i):
                rows = pl.ds(pl.multiple_of(i * own, own), own)
                quarter = links.swap_piece(i)

                def step(n, carry):
                    spot = pl.ds(pl.multiple_of(links.piece(n) * own, own), own)
                    allowed = allowed_of(quarter * own, n * own, end_ref[pl.ds(n, 1), :])
                    qb, kb, vb, gb = q_ref[rows, :], k_ref[spot, :], v_ref[spot, :], grad_ref[rows, :]
                    scores = dot(qb, kb, NT) * (SCALE * LOG2E)
                    probs = jnp.where(allowed, jnp.exp2(scores - lses[rows, 0:1]), 0.0)
                    d_probs = dot(gb, vb, NT)
                    d_scores = low(probs * (d_probs - delta[rows, 0:1]))
                    dv_acc[spot, :] += dot(low(probs), gb, TN)
                    dk_acc[spot, :] += dot(d_scores, qb, TN)
                    dq_acc[rows, :] += dot(d_scores, kb)
                    return carry

                lax.fori_loop(0, quarter + 1, step, 0)

            for number in range(n_pieces):
                rows = slice(number * own, (number + 1) * own)
                spot = pl.ds(pl.multiple_of(links.swap_piece(number) * own, own), own)
                cos, sin = cos_ref[spot, :], sin_ref[spot, :]
                dq_ref[rows, :] = low(spin(dq_acc[rows, :] * SCALE, cos, -sin))
                dk_ref[rows, :] = low(spin(dk_acc[rows, :] * SCALE, cos, -sin))
            dv_ref[...] = low(dv_acc[...])

        col = pl.BlockSpec((length, HD), lambda g: (0, g + start))
        pltpu.emit_pipeline(
            one, grid=(heads,), in_specs=[col] * 5, out_specs=[col] * 3
        )(q, k, v, grad, att, d_q, d_k, d_v)

    wide = pltpu.VMEM((length, HD), jnp.float32)
    pl.run_scoped(scoped, wide, wide, wide, wide, wide)


def second_kernel(
    places, norm2, cot, w_gate, w_up, w_down, w_out, w_qkv, norm1, q, k, v, att, hidden, x_own,
    lse_ref, cos_ref, sin_ref, end_ref,
    out_low, d_input, near_down, near_gate, near_up, near_out, near_qkv,
    far_down, far_gate, far_up, far_out, far_qkv,
    cots, act, d_gate, d_up, p_down, p_gate, p_up, p_out, p_qkv, dh, d_hidden, d_att, d_qkv,
    mine2, other2, come2, ready2, line2, mine3, other3, come3, ready3, line3,
    mine1, other1, come1, ready1, line1, out_mine, d_mine,
    come_down, come_gate, come_up, come_out, come_qkv, stage0, stage1, stage_out, send, recv, local, stage_sems,
):
    links = Links(places, send, recv)
    own, model = cot.shape
    n_parts = links.n_parts
    width = q.shape[1]
    heads = width // HD
    chunk = own // CHUNKS
    trade = {links.core: links.h, links.high: links.c}
    spread_c, spread_d = Spread(links, cots, own), Spread(links, dh, own)
    sums2 = Sums(links, mine2, other2, come2, ready2, line2)
    sums3 = Sums(links, mine3, other3, come3, ready3, line3)
    sums1 = Sums(links, mine1, other1, come1, ready1, line1)
    swap_spots = [links.take() for _ in range(CHUNKS)]
    out_spot = links.take()
    grad = lambda partial, come, stage, sems, near, far: Gradient(
        links, partial, come, stage, stage_sems.at[sems], near, far
    )
    g_down = grad(p_down, come_down, stage0, 0, near_down, far_down)
    g_gate = grad(p_gate, come_gate, stage1, 1, near_gate, far_gate)
    g_up = grad(p_up, come_up, stage0, 0, near_up, far_up)
    g_out = grad(p_out, come_out, stage_out, 2, near_out, far_out)
    g_qkv = grad(p_qkv, come_qkv, stage1.at[:, :, pl.ds(0, 3 * width)], 1, near_qkv, far_qkv)

    def piece(ref, part, other):
        return ref.at[pl.ds((part * 2 + other) * own, own)]

    near, rest = pl.ds(0, 2 * own), pl.ds(2 * own, 2 * own * (n_parts - 1))

    def trade_start(src, dst, spot):
        @pl.when(links.same)
        def _():
            pltpu.make_async_copy(src, dst, recv.at[spot]).start()

        @pl.when(~links.same)
        def _():
            links.copy(src, dst, trade, spot).start()

    def trade_wait(src, dst, spot):
        @pl.when(links.same)
        def _():
            pltpu.make_async_copy(src, dst, recv.at[spot]).wait()

        @pl.when(~links.same)
        def _():
            links.copy(src, dst, trade, spot).wait()

    links.greet()
    first = pltpu.make_async_copy(cot, piece(cots, 0, 0), local.at[0])
    first.start()
    first.wait()
    for k_ in range(CHUNKS):
        spread_c.own_ready(k_)
    spread_c.wait_near()

    def feed_forward(rows):
        gated(
            norm2.at[rows], cots.at[rows], w_gate, w_up, w_down, act.at[rows], d_gate.at[rows],
            d_up.at[rows], min(512, 2 * own), 256,
        )

    feed_forward(near)
    for k_ in range(CHUNKS):
        spread_c.pass_on(k_)
    spread_c.wait_far()
    feed_forward(rest)
    matmul(TN, cots, act, p_down, 1024, 512)
    g_down.start()

    def partials2(part, other, goal):
        two_products(
            piece(d_gate, part, other), w_gate, piece(d_up, part, other), w_up, goal.at[part], 512
        )

    def each_part(sums, make):
        for part in reversed(range(n_parts)):
            make(part, 1, sums.other)
            sums.across(part).start()
            make(part, 0, sums.mine)
            if part:
                sums.far(part)

    each_part(sums2, partials2)
    g_down.step(0)
    matmul(TN, norm2, d_gate, p_gate, 1024, 512)
    g_gate.start()
    g_down.step(1)
    for step in range(2, g_down.n):
        g_down.step(step)

    def hidden_back(hid, c, *refs):
        *terms, wide_out, low_out = refs
        total = terms[0][...].astype(jnp.float32)
        for term in terms[1:]:
            total = total + term[...].astype(jnp.float32)
        made = c[...].astype(jnp.float32) + norm_back(hid[...], total)
        wide_out[...] = made
        low_out[...] = low(made)

    for k_ in range(CHUNKS):
        rows = pl.ds(k_ * chunk, chunk)
        sums2.arrived(k_)
        by_rows(
            hidden_back, chunk // 2, [hidden.at[rows], cot.at[rows]] + sums2.terms(rows),
            [d_hidden.at[rows], dh.at[rows]],
        )
        spread_d.own_ready(k_)

    matmul(TN, norm2, d_up, p_up, 1024, 512)
    g_up.start()

    def partials3(part, other, goal):
        matmul(NT, piece(act, part, other), w_down, goal.at[part], own, 512)

    for part in reversed(range(n_parts)):
        partials3(part, 1, other3)
        sums3.across(part).start()
        partials3(part, 0, mine3)
    for k_ in range(CHUNKS):
        spread_d.pass_on(k_)
    g_gate.step(0)
    spread_d.wait_near()
    spread_d.wait_far()
    matmul(NN, dh, w_out, d_att, own, width)
    for part in reversed(range(1, n_parts)):
        sums3.far(part)
    matmul(TN, dh, att, p_out, 1024, width)
    g_out.start()
    d_q, d_k, d_v = (d_qkv.at[:, pl.ds(s * width, width)] for s in range(3))
    half = heads // 2
    attention_back(
        links, q, k, v, d_att, att, lse_ref, cos_ref, sin_ref, end_ref, d_q, d_k, d_v, half, 0
    )
    for step in range(1, g_gate.n):
        g_gate.step(step)
    attention_back(
        links, q, k, v, d_att, att, lse_ref, cos_ref, sin_ref, end_ref, d_q, d_k, d_v, heads - half, half
    )

    def partials1(part, other, goal):
        matmul(NT, piece(d_qkv, part, other), w_qkv, goal.at[part], own, 512)

    each_part(sums1, partials1)

    def finish_out(hid, *refs):
        *terms, made = refs
        total = hid[...]
        for term in terms:
            total = total + term[...].astype(jnp.float32)
        made[...] = low(total)

    g_up.step(0)
    for k_ in range(CHUNKS):
        sums3.arrived(k_)
    by_rows(finish_out, chunk, [hidden] + sums3.terms(pl.ds(0, own)), [out_mine])
    matmul(TN, norm1, d_qkv, p_qkv, 1024, width)
    g_qkv.start()
    for step in range(1, g_up.n):
        g_up.step(step)
    g_out.step(0)

    def input_back(x, d, *refs):
        *terms, made = refs
        total = terms[0][...].astype(jnp.float32)
        for term in terms[1:]:
            total = total + term[...].astype(jnp.float32)
        made[...] = low(d[...] + norm_back(x[...].astype(jnp.float32), total))

    for k_ in range(CHUNKS):
        rows = pl.ds(k_ * chunk, chunk)
        sums1.arrived(k_)
        by_rows(
            input_back, chunk // 2, [x_own.at[rows], d_hidden.at[rows]] + sums1.terms(rows),
            [d_mine.at[rows]],
        )
        trade_start(d_mine.at[rows], d_input.at[rows], swap_spots[k_])
    trade_start(out_mine, out_low, out_spot)
    for step in range(1, g_out.n):
        g_out.step(step)
    for step in range(g_qkv.n):
        g_qkv.step(step)
    for k_ in range(CHUNKS):
        rows = pl.ds(k_ * chunk, chunk)
        trade_wait(d_mine.at[rows], d_input.at[rows], swap_spots[k_])
    trade_wait(out_mine, out_low, out_spot)
    for thing in (spread_c, spread_d, sums1, sums2, sums3, g_down, g_gate, g_up, g_out, g_qkv):
        thing.finish()


def second_half(places, norm2, cot, fulls, norm1, q, k, v, att, hidden, x_own, lse, cos, sin, end):
    own, model = cot.shape
    length, width = q.shape
    w_qkv, w_out, w_gate, w_up, w_down = fulls
    ff = w_gate.shape[1]
    groups = 2 ** len(places[0])
    n_parts = 2 ** len(places[3])
    rows = model // (2 * groups)
    shape = lambda *dims: jax.ShapeDtypeStruct(dims, jnp.bfloat16)
    wide = lambda *dims: jax.ShapeDtypeStruct(dims, jnp.float32)
    here, there = pl.BlockSpec(memory_space=pltpu.VMEM), pl.BlockSpec(memory_space=pl.ANY)
    pieces = [shape(rows, cols) for cols in (ff, ff, ff, width, 3 * width)]
    sums = [shape(n_parts, own, model)] * 3 + [shape(n_parts - 1, own, model)] * 2
    out_shape = (
        [shape(own, model)] * 2
        + pieces * 2
        + [shape(length, model)]
        + [shape(length, ff)] * 3
        + [shape(model, cols) for cols in (ff, ff, ff, width, 3 * width)]
        + [shape(length, model), wide(own, model), shape(length, width), shape(length, 3 * width)]
        + sums * 3
        + [shape(own, model)] * 2
    )
    bf = lambda *dims: pltpu.VMEM(dims, jnp.bfloat16)
    blocks = 2 * (groups - 1)
    made = pl.pallas_call(
        functools.partial(second_kernel, places),
        in_specs=[there] * 14 + [here] * 4,
        out_specs=[there] * len(out_shape),
        out_shape=out_shape,
        scratch_shapes=[
            bf(blocks, rows, ff),
            bf(blocks, rows, ff),
            bf(blocks, rows, ff),
            bf(blocks, rows, width),
            bf(blocks, rows, 3 * width),
            bf(groups, rows, ff),
            bf(groups, rows, max(ff, 3 * width)),
            bf(groups, rows, width),
            pltpu.SemaphoreType.DMA((SEMS,)),
            pltpu.SemaphoreType.DMA((SEMS,)),
            pltpu.SemaphoreType.DMA((2,)),
            pltpu.SemaphoreType.DMA((3, groups)),
        ],
        compiler_params=pltpu.CompilerParams(
            collective_id=1, has_side_effects=True, vmem_limit_bytes=61 * 2**20
        ),
        cost_estimate=pl.CostEstimate(
            flops=18 * length * model * ff, bytes_accessed=300 * 2**20, transcendentals=length * length * 4
        ),
    )(
        norm2, cot, w_gate, w_up, w_down, w_out, w_qkv, norm1, q, k, v, att, hidden, x_own, lse, cos, sin, end
    )
    grads = [
        a.astype(jnp.float32) + b.astype(jnp.float32) for a, b in zip(made[2:7], made[7:12])
    ]
    return made[0], made[1], grads


def body(places, x, segments, padding, w_query, w_key, w_value, w_out, w_gate, w_up, w_down, cot):
    own = x.shape[0]
    length = segments.shape[0]
    cols = w_query.shape[1]
    same = lax.axis_index(places[1]) == lax.axis_index(places[2])
    counts = [jnp.sum(segments <= number, dtype=jnp.int32) for number in range(3)]
    last = jnp.where(segments == 0, counts[0], jnp.where(segments == 1, counts[1], counts[2])) - 1
    end_own = jnp.where(padding == 0, last, jnp.arange(length, dtype=jnp.int32)).reshape(-1, own)
    end = jnp.where(same, end_own, lax.ppermute(end_own, places[1], [(0, 1), (1, 0)]))
    cos, sin = turn_tables(length)
    mats = (jnp.concatenate([w_query, w_key, w_value], axis=1), w_out, w_gate, w_up, w_down)
    norm1, *fulls, q, k, v, att, lse, x_own, hidden, norm2, cot_own = first_half(
        places, x, end_own, cos, sin, mats, cot
    )
    output, d_input, (g_down, g_gate, g_up, g_out, g_qkv) = second_half(
        places, norm2, cot_own, fulls, norm1, q, k, v, att, hidden, x_own, lse, cos, sin, end
    )
    return (
        output,
        d_input.astype(jnp.float32),
        g_qkv[:, :cols],
        g_qkv[:, cols : 2 * cols],
        g_qkv[:, 2 * cols :],
        g_out,
        g_gate,
        g_up,
        g_down,
    )


def turn_tables(length):
    frequency = 10000.0 ** (-np.arange(HD // 2, dtype=np.float32) / np.float32(HD // 2))
    angles = np.arange(length, dtype=np.float32)[:, None] * frequency.astype(np.float32)[None, :]
    cos, sin = np.cos(angles), np.sin(angles)
    return (
        jnp.asarray(np.concatenate([cos, cos], axis=1), jnp.float32),
        jnp.asarray(np.concatenate([-sin, sin], axis=1), jnp.float32),
    )


def solution(mesh):
    dp, mp = mesh.devices.shape
    n_dp, n_mp = dp.bit_length() - 1, mp.bit_length() - 1
    dp_axes = tuple("d%d" % k for k in range(n_dp))
    mp_axes = tuple("m%d" % k for k in range(n_mp))
    fine = Mesh(mesh.devices.reshape((2,) * (n_dp + n_mp)), dp_axes + mp_axes)
    places = (dp_axes[:-1], dp_axes[-1], mp_axes[0], mp_axes[1:])
    tokens = P(dp_axes + mp_axes, None)
    weight = P(dp_axes, mp_axes)
    return jax.shard_map(
        functools.partial(body, places),
        mesh=fine,
        in_specs=(tokens, P(dp_axes), P(dp_axes)) + (weight,) * 7 + (tokens,),
        out_specs=(tokens, tokens) + (weight,) * 7,
        check_vma=False,
    )
```

```python
import functools
import jax
import jax.numpy as jnp
import numpy as np
from jax import lax
from jax.experimental import pallas as pl
from jax.experimental.pallas import tpu as pltpu
from jax.sharding import Mesh, PartitionSpec as P

HD = 128
SCALE = HD ** (-0.5)
LOG2E = 1.4426950408889634
NEG = -1e30
eps = 1e-05
NN = (((1,), (0,)), ((), ()))
NT = (((1,), (1,)), ((), ()))
TN = (((0,), (0,)), ((), ()))


def dot(left, right, dims=(((1,), (0,)), ((), ()))):
    return lax.dot_general(left, right, dims, preferred_element_type=jnp.float32)


def low(value):
    return value.astype(jnp.bfloat16)

def allowed_of(first_q, first_k, end_row):
    blk = end_row.shape[1]
    t = first_q + lax.broadcasted_iota(jnp.int32, (blk, 1), 0)
    u = first_k + lax.broadcasted_iota(jnp.int32, (1, blk), 1)
    return (u <= t) & (t <= end_row)


MESH = pl.DeviceIdType.MESH
CHUNKS = 4
SEMS = 224
MATS = ("qkv", "out", "gate", "up", "down")


def flipped(bit, other):
    return bit + other - 2 * bit * other


class Links:
    def __init__(self, places, send, recv):
        self.rest, self.core, self.high, self.lower = places
        self.c, self.h = lax.axis_index(self.core), lax.axis_index(self.high)
        self.r = [lax.axis_index(axis) for axis in self.rest]
        self.low = [lax.axis_index(axis) for axis in self.lower]
        self.same = self.c == self.h
        self.n_parts = 2 ** len(self.lower)
        self.send, self.recv, self.used, self.unsent = send, recv, 0, []
        self.across = {self.core: 1 - self.c}

    def beside(self, k):
        return {self.lower[k]: 1 - self.low[k]}

    def over(self, k):
        return {self.rest[k]: 1 - self.r[k]}

    def group(self, mask):
        total = 0
        for k, bit in enumerate(self.r):
            total = total * 2 + (1 - bit if mask >> k & 1 else bit)
        return total

    def swap_piece(self, number):
        other, part = number % 2, number // 2
        return flipped(self.c, other) * self.n_parts + self.turn(part)

    def piece(self, quarter):
        other, part = flipped(self.c, quarter // self.n_parts), self.turn(quarter % self.n_parts)
        return part * 2 + other

    def turn(self, part):
        total = 0
        for k, bit in enumerate(self.low):
            digit = part // 2 ** (len(self.low) - 1 - k) % 2
            total = total * 2 + flipped(bit, digit)
        return total

    def greet(self):
        barrier = pltpu.get_barrier_semaphore()
        partners = [
            self.across,
            {self.high: 1 - self.h},
            {self.core: 1 - self.c, self.high: 1 - self.h},
        ]
        partners += [self.beside(k) for k in range(len(self.lower))]
        partners += [self.over(k) for k in range(len(self.rest))]
        for partner in partners:
            pl.semaphore_signal(barrier, inc=1, device_id=partner, device_id_type=MESH)
        pl.semaphore_wait(barrier, len(partners))

    def take(self, count=1):
        self.used += count
        return self.used - count

    def copy(self, src, dst, partner, spot=None, recv=None):
        spot = self.take() if spot is None else spot
        made = pltpu.make_async_remote_copy(
            src_ref=src, dst_ref=dst, send_sem=self.send.at[spot],
            recv_sem=self.recv.at[spot if recv is None else recv],
            device_id=partner, device_id_type=MESH,
        )
        return made

    def push(self, src, dst, partner):
        made = self.copy(src, dst, partner)
        made.start()
        self.unsent.append(made)
        return made


class Weight:
    def __init__(self, links, shard, full):
        self.links, self.shard, self.full = links, shard, full
        self.rows = shard.shape[0]
        self.arrive = links.take(2)
        self.near, self.far = links.take(), links.take()
        self.stages = []
        n = len(links.rest)
        for step in range(n):
            stage = []
            for half in range(2):
                order = list(range(n)) if half == 0 else list(reversed(range(n)))
                have = [0]
                for k in order[:step]:
                    have = have + [mask | 1 << k for mask in have]
                stage += [(half, mask, order[step], links.take()) for mask in have]
            self.stages.append(stage)

    def slot(self, mask, core):
        start = (self.links.group(mask) * 2 + core) * self.rows
        return self.full.at[pl.ds(pl.multiple_of(start, self.rows), self.rows)]

    def near_copy(self):
        links = self.links
        return links.copy(
            self.shard, self.slot(0, links.c), links.across, self.near, self.arrive + links.c
        )

    def far_copy(self):
        links = self.links
        return links.copy(
            self.shard, self.slot(0, links.c), {links.core: links.h, links.high: 1 - links.h},
            self.far, self.arrive + links.c,
        )

    def keep_near(self, src):
        links = self.links
        pltpu.make_async_copy(
            src, self.slot(0, links.c), links.recv.at[self.arrive + links.c]
        ).start()

    def send_far(self):
        self.far_copy().start()

    def sent_far(self):
        self.far_copy().wait_send()

    def stage_copies(self, step):
        for half, mask, axis, spot in self.stages[step]:
            block = self.slot(mask, half)
            yield self.links.copy(block, block, self.links.over(axis), spot)

    def event(self, step):
        if step == 0:
            for core in range(2):
                block = self.slot(0, core)
                pltpu.make_async_copy(block, block, self.links.recv.at[self.arrive + core]).wait()
        else:
            for copy in self.stage_copies(step - 1):
                copy.wait_recv()
        if step < len(self.stages):
            for copy in self.stage_copies(step):
                copy.start()

    def finish(self):
        @pl.when(~self.links.same)
        def _():
            self.near_copy().wait_send()

        for step in range(len(self.stages)):
            for copy in self.stage_copies(step):
                copy.wait_send()


class Spread:
    def __init__(self, links, full, own):
        self.links, self.full, self.own, self.chunk = links, full, own, own // CHUNKS
        self.moves = {}
        n = len(links.lower)
        for k in range(CHUNKS):
            have = [0]
            for step in range(n):
                value = 2 ** (n - 1 - step)
                for part in have:
                    self.moves[k, part, step] = (part | value, links.take())
                have = have + [part | value for part in have]
            for part in range(links.n_parts):
                self.moves[k, part, None] = (part, links.take())

    def rows(self, part, other, k):
        return pl.ds((part * 2 + other) * self.own + k * self.chunk, self.chunk)

    def made(self, k, part, step, src=None):
        goal, spot = self.moves[k, part, step]
        links = self.links
        partner = links.across if step is None else links.beside(step)
        src = self.full.at[self.rows(part, 0, k)] if src is None else src
        dst = self.full.at[self.rows(goal, 1 if step is None else 0, k)]
        return links.copy(src, dst, partner, spot)

    def first_step(self, part):
        n = len(self.links.lower)
        return [s for s in range(n) if (0, part, s) in self.moves]

    def own_ready(self, k, src=None):
        for step in self.first_step(0):
            self.made(k, 0, step, src).start()
        self.made(k, 0, None, src).start()

    def pass_on(self, k):
        n = len(self.links.lower)
        for step in range(n):
            value = 2 ** (n - 1 - step)
            for part in range(self.links.n_parts):
                if (k, part, step) in self.moves:
                    self.made(k, part, step).wait_recv()
                    goal = part | value
                    for later in self.first_step(goal):
                        self.made(k, goal, later).start()
                    self.made(k, goal, None).start()

    def wait_near(self):
        for k in range(CHUNKS):
            self.made(k, 0, None).wait_recv()

    def wait_far(self):
        for k in range(CHUNKS):
            for part in range(1, self.links.n_parts):
                self.made(k, part, None).wait_recv()

    def finish(self):
        for k, part, step in self.moves:
            self.made(k, part, step).wait_send()


def normed(value):
    average = jnp.mean(value, axis=-1, keepdims=True)
    centred = value - average
    variance = jnp.mean(centred * centred, axis=-1, keepdims=True)
    return centred * lax.rsqrt(variance + eps)


def spin(value, cos, sin):
    return value * cos + pltpu.roll(value, HD // 2, 1) * sin


def first_kernel(
    places, x, end_mine, cos_ref, sin_ref, w_qkv, w_out, w_gate, w_up, w_down, cot,
    norm1, qkv_all, out_all, gate_all, up_all, down_all, q_ref, k_ref, v_ref, att_ref, lse_ref, x_own, hidden,
    norm2, cot_own, norm1_v, qkv_v, out_v, end_other, p_mine, p_other, p_come, line, send, recv, local,
):
    links = Links(places, send, recv)
    own = x.shape[0]
    n_parts, n_pieces = links.n_parts, 2 * links.n_parts
    n_low = len(links.lower)
    chunk = own // CHUNKS
    heads = q_ref.shape[1] // HD
    width = heads * HD
    weights = {
        name: Weight(links, shard, full)
        for name, shard, full in zip(
            MATS,
            (w_qkv, w_out, w_gate, w_up, w_down),
            (qkv_v, out_v, gate_all, up_all, down_all),
        )
    }
    n_steps = len(links.rest)
    swap_spots = [links.take() for _ in range(CHUNKS)]
    cot_spot, end_spot = links.take(), links.take()
    trade = {links.core: links.h, links.high: links.c}

    def swap_copy(k):
        rows = pl.ds(k * chunk, chunk)
        return links.copy(x.at[rows], x_own.at[rows], trade, swap_spots[k])

    def swap_local(k):
        rows = pl.ds(k * chunk, chunk)
        return pltpu.make_async_copy(x.at[rows], x_own.at[rows], recv.at[swap_spots[k]])

    def cot_copy():
        return links.copy(cot, cot_own, trade, cot_spot)

    def cot_local():
        return pltpu.make_async_copy(p_mine.at[0], cot_own, recv.at[cot_spot])

    end_copy = links.copy(end_mine, end_other, links.across, end_spot)
    spread1 = Spread(links, norm1_v, own)
    norm2_v = norm1_v
    spread2 = Spread(links, norm2_v, own)
    across_spots = [links.take() for _ in range(n_parts)]
    line_spots = {
        (part, k): links.take() for part in range(1, n_parts) for k in range(CHUNKS)
    }

    rest = []
    for number, name in enumerate(MATS[2:]):
        shard = weights[name].shard
        rows, cols = shard.shape
        hold = p_other.at[number // 2, pl.ds(number % 2 * rows, rows), pl.ds(0, cols)]
        rest.append((name, hold, pltpu.make_async_copy(shard, hold, local.at[number])))
    cot_load = pltpu.make_async_copy(cot, p_mine.at[0], local.at[3])

    links.greet()
    end_copy.start()
    weights["qkv"].send_far()

    @pl.when(links.same)
    def _():
        for k in range(CHUNKS):
            swap_local(k).start()
        for name in MATS[:2]:
            weights[name].keep_near(weights[name].shard)
        for _, _, load in rest:
            load.start()
        cot_load.start()

    @pl.when(~links.same)
    def _():
        for name in MATS:
            weights[name].near_copy().start()

    def norm_chunk(k):
        rows = pl.ds(k * chunk, chunk)
        norm1_v[rows, :] = low(normed(x_own[rows, :].astype(jnp.float32)))
        spread1.own_ready(k)

    def run(name, *steps):
        for step in steps:
            weights[name].event(step)

    last = n_steps

    @pl.when(links.same)
    def _():
        for k in range(CHUNKS):
            swap_local(k).wait()
            norm_chunk(k)
        for name, hold, load in rest:
            load.wait()
            weights[name].keep_near(hold)
        cot_load.wait()
        cot_local().start()
        run("qkv", *range(last + 1))
        run("out", *range(last + 1))
        weights["qkv"].sent_far()
        run("gate", *range(last + 1))
        run("up", 0)

    @pl.when(~links.same)
    def _():
        weights["qkv"].sent_far()
        for k in range(2):
            swap_copy(k).start()
        run("qkv", 0)
        for k in range(CHUNKS):
            swap_copy(k).wait_send()
            if k + 2 < CHUNKS:
                swap_copy(k + 2).start()
            swap_copy(k).wait_recv()
            norm_chunk(k)
            if k == 1:
                run("qkv", *range(1, last))
        run("qkv", last)

    weights["out"].send_far()
    end_copy.wait_recv()
    for k in range(CHUNKS):
        spread1.pass_on(k)

    keep = [pltpu.make_async_copy(qkv_v, qkv_all, local.at[4])]
    keep[0].start()

    def project(pieces):
        for section, goal in enumerate((q_ref, k_ref, v_ref)):
            for number in pieces:
                rows = slice(number * own, (number + 1) * own)
                spot = pl.ds(pl.multiple_of(links.swap_piece(number) * own, own), own)

                @pl.loop(0, heads // 2)
                def _(tile, section=section, goal=goal, rows=rows, spot=spot):
                    start = pl.multiple_of(tile * 2 * HD, 2 * HD)
                    made = dot(norm1_v[rows, :], qkv_v[:, pl.ds(section * width + start, 2 * HD)])
                    for k in range(2):
                        value = made[:, k * HD : (k + 1) * HD]
                        if section < 2:
                            value = spin(value, cos_ref[spot, :], sin_ref[spot, :])
                        goal[rows, pl.ds(pl.multiple_of(start + k * HD, HD), HD)] = low(value)

    weights["gate"].send_far()
    spread1.wait_near()
    project((0, 1))

    @pl.when(links.same)
    def _():
        run("up", *range(1, last))

    @pl.when(~links.same)
    def _():
        run("out", 0)

    spread1.wait_far()
    project(range(2, n_pieces))
    keep.append(pltpu.make_async_copy(norm1_v, norm1, local.at[5]))
    keep[-1].start()

    @pl.when(links.same)
    def _():
        run("up", last)
        run("down", 0)

    @pl.when(~links.same)
    def _():
        run("out", *range(1, last + 1))

    keep.append(pltpu.make_async_copy(out_v, out_all, local.at[6]))
    keep[-1].start()

    lanes = lax.broadcasted_iota(jnp.int32, (own, HD), 1)
    for head in range(heads):
        cols = slice(head * HD, (head + 1) * HD)

        @pl.loop(0, n_pieces)
        def _(i, head=head, cols=cols):
            rows = pl.ds(pl.multiple_of(i * own, own), own)
            quarter = links.swap_piece(i)

            def step(n, carry):
                top, total, acc = carry
                spot = pl.ds(pl.multiple_of(links.piece(n) * own, own), own)
                end = jnp.where(links.same, end_mine[pl.ds(n, 1), :], end_other[pl.ds(n, 1), :])
                allowed = allowed_of(quarter * own, n * own, end)
                scores = dot(q_ref[rows, cols], k_ref[spot, cols], NT)
                scores = jnp.where(allowed, scores * (SCALE * LOG2E), NEG)
                new_top = jnp.maximum(top, jnp.max(scores, axis=1, keepdims=True))
                grown = jnp.exp2(scores - new_top)
                shrink = jnp.exp2(top - new_top)
                total = total * shrink + jnp.sum(grown, axis=1, keepdims=True)
                return new_top, total, acc * shrink + dot(low(grown), v_ref[spot, cols])

            top, total, acc = lax.fori_loop(
                0, quarter + 1, step,
                (
                    jnp.full((own, 1), NEG, jnp.float32),
                    jnp.zeros((own, 1), jnp.float32),
                    jnp.zeros((own, HD), jnp.float32),
                ),
            )
            att_ref[rows, cols] = low(acc / total)
            lse = jnp.broadcast_to(top + jnp.log2(total), (own, HD))
            lse_ref[rows, :] = lse if head == 0 else jnp.where(lanes == head, lse, lse_ref[rows, :])

        if head == 0:

            @pl.when(links.same)
            def _():
                run("down", *range(1, last))

        if head == heads // 2 - 1:
            weights["gate"].sent_far()
            weights["up"].send_far()

    @pl.when(links.same)
    def _():
        cot_local().wait()
        run("down", last)

    @pl.when(~links.same)
    def _():
        run("gate", 0)

    keep.pop(1).wait()
    spread1.finish()

    def across_copy(part):
        return links.copy(p_other.at[part], p_come.at[part], links.across, across_spots[part])

    def line_copy(part, k):
        rows = pl.ds(k * chunk, chunk)
        step = n_low - part.bit_length()
        return links.copy(
            p_mine.at[part, rows], line.at[part - 1, rows], links.beside(step), line_spots[part, k]
        )

    def out_rows(number, goal):
        rows = slice(number * own, (number + 1) * own)
        tile = 512

        @pl.loop(0, out_v.shape[0] // tile)
        def _(n):
            start = pl.multiple_of(n * tile, tile)
            goal[:, pl.ds(start, tile)] = low(
                dot(att_ref[rows, :], out_v[pl.ds(start, tile), :], NT)
            )

    for part in reversed(range(n_parts)):
        out_rows(part * 2 + 1, p_other.at[part])
        across_copy(part).start()
        out_rows(part * 2, p_mine.at[part])
        across_copy(part).wait_recv()
        for k in range(CHUNKS):
            rows = pl.ds(k * chunk, chunk)
            total = p_mine[part, rows, :].astype(jnp.float32) + p_come[part, rows, :].astype(jnp.float32)
            if part == 0:
                hidden[rows, :] = x_own[rows, :].astype(jnp.float32) + total
            else:
                step = part.bit_length() - 1
                for high in range(step + 1, n_low):
                    more = part | 1 << high
                    line_copy(more, k).wait_recv()
                    total = total + line[more - 1, rows, :].astype(jnp.float32)
                p_mine[part, rows, :] = low(total)
                if k < 2 or part & (part - 1):
                    line_copy(part, k).start()

    @pl.when(~links.same)
    def _():
        run("gate", *range(1, last))

    lined = [1 << step for step in range(n_low)]
    for k in range(CHUNKS):
        rows = pl.ds(k * chunk, chunk)
        for part in lined:
            line_copy(part, k).wait_send()
            if k + 2 < CHUNKS:
                line_copy(part, k + 2).start()
        total = hidden[rows, :]
        for part in lined:
            line_copy(part, k).wait_recv()
            total = total + line[part - 1, rows, :].astype(jnp.float32)
        hidden[rows, :] = total
        norm2_v[rows, :] = low(normed(total))
        spread2.own_ready(k)
        if k == 0:
            weights["up"].sent_far()
            weights["down"].send_far()

        @pl.when(~links.same)
        def _():
            if k == 1:
                run("gate", last)
                run("up", 0)
            if k == 2:
                run("up", *range(1, last))

    for k in range(CHUNKS):

        @pl.when(~links.same)
        def _():
            if k == 0:
                run("up", last)
            if k == 1:
                run("down", 0)
            if k == 2:
                run("down", *range(1, last))

        if k == 1:
            weights["down"].sent_far()

            @pl.when(~links.same)
            def _():
                cot_copy().start()

        spread2.pass_on(k)

    spread2.wait_near()
    spread2.wait_far()
    keep.append(pltpu.make_async_copy(norm2_v, norm2, local.at[7]))
    keep[-1].start()

    @pl.when(~links.same)
    def _():
        run("down", last)
        cot_copy().wait()

    end_copy.wait_send()
    spread2.finish()
    for weight in weights.values():
        weight.finish()
    weights["out"].sent_far()
    for part in range(n_parts):
        across_copy(part).wait_send()
    for part, k in line_spots:
        if part & (part - 1):
            line_copy(part, k).wait_send()
    for made in keep:
        made.wait()


def first_half(places, x, end_mine, cos, sin, mats, cot):
    own, model = x.shape
    n_parts = 2 ** len(places[3])
    length = 2 * n_parts * own
    groups = 2 ** len(places[0])
    width = mats[1].shape[1]
    shape = lambda *dims: jax.ShapeDtypeStruct(dims, jnp.bfloat16)
    wide = lambda *dims: jax.ShapeDtypeStruct(dims, jnp.float32)
    here, there = pl.BlockSpec(memory_space=pltpu.VMEM), pl.BlockSpec(memory_space=pl.ANY)
    fulls = [shape(2 * groups * mat.shape[0], mat.shape[1]) for mat in mats]
    bf = lambda *dims: pltpu.VMEM(dims, jnp.bfloat16)
    return pl.pallas_call(
        functools.partial(first_kernel, places),
        in_specs=[there, here, here, here] + [there] * 6,
        out_specs=[there] * 6 + [here] * 7 + [there] * 2,
        out_shape=[shape(length, model)]
        + fulls
        + [shape(length, width)] * 4
        + [wide(length, HD), shape(own, model), wide(own, model)]
        + [shape(length, model), shape(own, model)],
        scratch_shapes=[
            bf(length, model),
            bf(*fulls[0].shape),
            bf(*fulls[1].shape),
            pltpu.VMEM(end_mine.shape, jnp.int32),
            bf(n_parts, own, model),
            bf(n_parts, own, model),
            bf(n_parts, own, model),
            bf(max(n_parts - 1, 1), own, model),
            pltpu.SemaphoreType.DMA((SEMS,)),
            pltpu.SemaphoreType.DMA((SEMS,)),
            pltpu.SemaphoreType.DMA((8,)),
        ],
        compiler_params=pltpu.CompilerParams(
            collective_id=0, has_side_effects=True, vmem_limit_bytes=61 * 2**20
        ),
        cost_estimate=pl.CostEstimate(
            flops=8 * length * model * width,
            bytes_accessed=100 * 2**20,
            transcendentals=length * length * 4,
        ),
    )(x, end_mine, cos, sin, *mats, cot)


def matmul(kind, left, right, out, rows, cols):
    depth = left.shape[0] if kind == TN else left.shape[1]

    def tile(a, b, made):
        made[...] = low(dot(a[...], b[...], kind))

    a_spec = (
        pl.BlockSpec((depth, rows), lambda i, j: (0, i))
        if kind == TN
        else pl.BlockSpec((rows, depth), lambda i, j: (i, 0))
    )
    b_spec = (
        pl.BlockSpec((cols, depth), lambda i, j: (j, 0))
        if kind == NT
        else pl.BlockSpec((depth, cols), lambda i, j: (0, j))
    )
    pltpu.emit_pipeline(
        tile,
        grid=(out.shape[0] // rows, out.shape[1] // cols),
        in_specs=[a_spec, b_spec],
        out_specs=[pl.BlockSpec((rows, cols), lambda i, j: (i, j))],
    )(left, right, out)


def two_products(left1, right1, left2, right2, out, rows, cols):
    def tile(a, b, c, d, made):
        made[...] = low(dot(a[...], b[...], NT) + dot(c[...], d[...], NT))

    depth = left1.shape[1]
    held = pl.BlockSpec((rows, depth), lambda i, j: (i, 0))
    moving = pl.BlockSpec((cols, depth), lambda i, j: (j, 0))
    pltpu.emit_pipeline(
        tile,
        grid=(out.shape[0] // rows, out.shape[1] // cols),
        in_specs=[held, moving, held, moving],
        out_specs=[pl.BlockSpec((rows, cols), lambda i, j: (i, j))],
    )(left1, right1, left2, right2, out)


def by_rows(make, rows, ins, outs):
    spec = lambda ref: pl.BlockSpec((rows, ref.shape[1]), lambda i: (i, 0))
    pltpu.emit_pipeline(
        make,
        grid=(outs[0].shape[0] // rows,),
        in_specs=[spec(ref) for ref in ins],
        out_specs=[spec(ref) for ref in outs],
    )(*ins, *outs)


def gated(norm, cots, w_gate, w_up, w_down, act, d_gate, d_up, rows, cols):
    def tile(n, c, wg, wu, wd, act_t, gate_t, up_t):
        gate, up = dot(n[...], wg[...]), dot(n[...], wu[...])
        d_act = dot(c[...], wd[...])
        s = 1.0 / (1.0 + jnp.exp(-gate))
        silu = gate * s
        act_t[...] = low(silu * up)
        gate_t[...] = low(d_act * up * s * (1.0 + gate * (1.0 - s)))
        up_t[...] = low(d_act * silu)

    depth = norm.shape[1]
    row = pl.BlockSpec((rows, depth), lambda i, j: (i, 0))
    col = pl.BlockSpec((depth, cols), lambda i, j: (0, j))
    made = pl.BlockSpec((rows, cols), lambda i, j: (i, j))
    pltpu.emit_pipeline(
        tile,
        grid=(act.shape[0] // rows, act.shape[1] // cols),
        in_specs=[row, row, col, col, col],
        out_specs=[made] * 3,
    )(norm, cots, w_gate, w_up, w_down, act, d_gate, d_up)


def norm_back(value, grad):
    average = jnp.mean(value, axis=-1, keepdims=True)
    centred = value - average
    r = lax.rsqrt(jnp.mean(centred * centred, axis=-1, keepdims=True) + eps)
    n = centred * r
    return r * (
        grad - jnp.mean(grad, axis=-1, keepdims=True) - n * jnp.mean(grad * n, axis=-1, keepdims=True)
    )


class Sums:
    def __init__(self, links, made, come, ready, line):
        self.links, self.made = links, made
        self.come, self.ready, self.line = come, ready, line
        n_parts, self.own, _ = come.shape
        self.n_parts = n_parts
        self.chunk = self.own // CHUNKS
        self.spots = [links.take() for _ in range(n_parts)]
        self.line_spots = {
            (part, k): links.take() for part in range(1, n_parts) for k in range(CHUNKS)
        }

    def piece(self, part, other):
        return self.made.at[pl.ds((part * 2 + other) * self.own, self.own)]

    def across(self, part):
        links = self.links
        return links.copy(self.piece(part, 1), self.come.at[part], links.across, self.spots[part])

    def along(self, part, k):
        links = self.links
        rows = pl.ds(k * self.chunk, self.chunk)
        step = len(links.lower) - part.bit_length()
        return links.copy(
            self.ready.at[part - 1, rows], self.line.at[part - 1, rows], links.beside(step),
            self.line_spots[part, k],
        )

    def more(self, part):
        return [part | 1 << k for k in range(part.bit_length(), len(self.links.lower))]

    def far(self, part, at_once=CHUNKS):
        self.across(part).wait_recv()
        ins = [self.piece(part, 0), self.come.at[part]]
        for number in self.more(part):
            for k in range(CHUNKS):
                self.along(number, k).wait_recv()
            ins.append(self.line.at[number - 1])

        def make(*refs):
            total = refs[0][...].astype(jnp.float32)
            for ref in refs[1:-1]:
                total = total + ref[...].astype(jnp.float32)
            refs[-1][...] = low(total)

        by_rows(make, self.chunk, ins, [self.ready.at[part - 1]])
        for k in range(CHUNKS if part & (part - 1) else at_once):
            self.along(part, k).start()

    def start_late(self, first):
        for part in self.more(0):
            for k in range(first, CHUNKS):
                self.along(part, k).start()

    def arrived(self, chunks=range(CHUNKS)):
        if 0 in chunks:
            self.across(0).wait_recv()
        for number in self.more(0):
            for k in chunks:
                self.along(number, k).wait_recv()

    def terms(self, rows=None):
        rows = pl.ds(0, self.own) if rows is None else rows
        return [self.piece(0, 0).at[rows], self.come.at[0, rows]] + [
            self.line.at[number - 1, rows] for number in self.more(0)
        ]

    def finish(self):
        for part in range(self.n_parts):
            self.across(part).wait_send()
        for part, k in self.line_spots:
            self.along(part, k).wait_send()


class Gradient:
    def __init__(self, links, partial, come, stage, stage_sems, near, far):
        self.links, self.partial, self.come, self.stage = links, partial, come, stage
        self.stage_sems, self.near, self.far = stage_sems, near, far
        self.rows = near.shape[0]
        n = len(links.rest)
        self.n = n
        self.kept, self.sent, self.place, self.spots = {}, {}, {}, {}
        for half in range(2):
            order = list(reversed(range(n))) if half == 0 else list(range(n))
            have = list(range(2**n))
            for step, axis in enumerate(order):
                self.sent[half, step] = (axis, [mask for mask in have if mask >> axis & 1])
                have = [mask for mask in have if not mask >> axis & 1]
                self.kept[half, step] = have
                for mask in have:
                    self.place[half, step, mask] = len(self.place)
                    self.spots[half, step, mask] = links.take()
        self.near_spot, self.far_spot = links.take(), links.take()
        self.out_spots = [links.take(), links.take()]

    def slot(self, mask, half):
        start = (self.links.group(mask) * 2 + half) * self.rows
        return self.partial.at[pl.ds(pl.multiple_of(start, self.rows), self.rows)]

    def block(self, half, step, mask):
        return self.come.at[self.place[half, step, mask]]

    def copies(self, step):
        for half in range(2):
            axis, masks = self.sent[half, step]
            for mask in masks:
                goal = mask & ~(1 << axis)
                src = self.slot(mask, half) if step == 0 else self.block(half, step - 1, mask)
                yield self.links.copy(
                    src, self.block(half, step, goal), self.links.over(axis), self.spots[half, step, goal]
                )

    def loads(self):
        number = 0
        for half in range(2):
            for mask in self.kept[half, 0]:
                yield pltpu.make_async_copy(
                    self.slot(mask, half), self.stage.at[number], self.stage_sems.at[number]
                )
                number += 1

    def start(self):
        for copy in self.copies(0):
            copy.start()
        for load in self.loads():
            load.start()

    def step(self, step):
        for copy in self.copies(step):
            copy.wait_recv()
        if step == 0:
            for load in self.loads():
                load.wait()
        number = 0
        for half in range(2):
            for mask in self.kept[half, step]:
                goal = self.block(half, step, mask)
                add = self.stage.at[number] if step == 0 else self.block(half, step - 1, mask)
                number += 1
                rows = min(64, self.rows)

                @pl.loop(0, self.rows // rows)
                def _(i, goal=goal, add=add):
                    spot = pl.ds(pl.multiple_of(i * rows, rows), rows)
                    goal[spot, :] = low(
                        goal[spot, :].astype(jnp.float32) + add[spot, :].astype(jnp.float32)
                    )

        if step + 1 < self.n:
            for copy in self.copies(step + 1):
                copy.start()
        else:
            self.hand()

    def total(self, half):
        first, second = (self.place[k, self.n - 1, 0] for k in range(2))
        return self.come.at[first + half * (second - first)]

    def near_local(self):
        links = self.links
        return pltpu.make_async_copy(self.total(links.c), self.near, links.recv.at[self.near_spot])

    def near_copy(self):
        links = self.links
        return links.copy(self.total(1 - links.c), self.near, links.across, self.near_spot)

    def far_copy(self, half):
        links = self.links
        return links.copy(
            self.total(half), self.far, {links.core: half, links.high: links.c},
            self.out_spots[half], self.far_spot,
        )

    def hand(self):
        links = self.links

        @pl.when(links.same)
        def _():
            self.near_local().start()
            self.near_copy().start()

        @pl.when(~links.same)
        def _():
            for half in range(2):
                self.far_copy(half).start()

    def finish(self):
        links = self.links
        for step in range(self.n):
            for copy in self.copies(step):
                copy.wait_send()

        @pl.when(links.same)
        def _():
            self.near_local().wait()
            self.near_copy().wait_send()

        @pl.when(~links.same)
        def _():
            self.near_copy().wait_recv()
            for half in range(2):
                self.far_copy(half).wait_send()

        self.far_copy(0).wait_recv()


def attention_back(links, q, k, v, grad, att, lse_ref, cos_ref, sin_ref, end_ref, d_q, d_k, d_v, heads, start):
    length = q.shape[0]
    n_pieces, own = end_ref.shape

    def scoped(dq_acc, dk_acc, dv_acc, delta, lses):
        def one(q_ref, k_ref, v_ref, grad_ref, att_ref, dq_ref, dk_ref, dv_ref):
            head = pl.program_id(0) + start
            dq_acc[...] = jnp.zeros_like(dq_acc)
            dk_acc[...] = jnp.zeros_like(dk_acc)
            dv_acc[...] = jnp.zeros_like(dv_acc)
            lanes = lax.broadcasted_iota(jnp.int32, lse_ref.shape, 1)
            mine = jnp.where(lanes == head, lse_ref[...], 0.0)
            lses[...] = jnp.broadcast_to(jnp.sum(mine, axis=1, keepdims=True), mine.shape)
            prod = grad_ref[...].astype(jnp.float32) * att_ref[...].astype(jnp.float32)
            delta[...] = jnp.broadcast_to(jnp.sum(prod, axis=1, keepdims=True), prod.shape)

            @pl.loop(0, n_pieces)
            def _(i):
                rows = pl.ds(pl.multiple_of(i * own, own), own)
                quarter = links.swap_piece(i)

                def step(n, carry):
                    spot = pl.ds(pl.multiple_of(links.piece(n) * own, own), own)
                    allowed = allowed_of(quarter * own, n * own, end_ref[pl.ds(n, 1), :])
                    qb, kb, vb, gb = q_ref[rows, :], k_ref[spot, :], v_ref[spot, :], grad_ref[rows, :]
                    scores = dot(qb, kb, NT) * (SCALE * LOG2E)
                    probs = jnp.where(allowed, jnp.exp2(scores - lses[rows, 0:1]), 0.0)
                    d_probs = dot(gb, vb, NT)
                    d_scores = low(probs * (d_probs - delta[rows, 0:1]))
                    dv_acc[spot, :] += dot(low(probs), gb, TN)
                    dk_acc[spot, :] += dot(d_scores, qb, TN)
                    dq_acc[rows, :] += dot(d_scores, kb)
                    return carry

                lax.fori_loop(0, quarter + 1, step, 0)

            for number in range(n_pieces):
                rows = slice(number * own, (number + 1) * own)
                spot = pl.ds(pl.multiple_of(links.swap_piece(number) * own, own), own)
                cos, sin = cos_ref[spot, :], sin_ref[spot, :]
                dq_ref[rows, :] = low(spin(dq_acc[rows, :] * SCALE, cos, -sin))
                dk_ref[rows, :] = low(spin(dk_acc[rows, :] * SCALE, cos, -sin))
            dv_ref[...] = low(dv_acc[...])

        col = pl.BlockSpec((length, HD), lambda g: (0, g + start))
        pltpu.emit_pipeline(
            one, grid=(heads,), in_specs=[col] * 5, out_specs=[col] * 3
        )(q, k, v, grad, att, d_q, d_k, d_v)

    wide = pltpu.VMEM((length, HD), jnp.float32)
    pl.run_scoped(scoped, wide, wide, wide, wide, wide)


def second_kernel(
    places, norm2, cot, w_gate, w_up, w_down, w_out, w_qkv, norm1, q, k, v, att, hidden, x_own,
    lse_ref, cos_ref, sin_ref, end_ref,
    out_low, d_input, near_down, near_gate, near_up, near_out, near_qkv,
    far_down, far_gate, far_up, far_out, far_qkv,
    cots, act, d_gate, d_up, p_down, p_gate, p_up, p_out, p_qkv, dh, d_hidden, d_att, d_qkv,
    made2, come2, ready2, line2, made3, come3, ready3, line3, made1, come1, ready1, line1, out_mine, d_mine,
    come_down, come_gate, come_up, come_out, come_qkv, stage0, stage1, stage_out, send, recv, stage_sems,
):
    links = Links(places, send, recv)
    own, model = cot.shape
    n_parts = links.n_parts
    width = q.shape[1]
    heads = width // HD
    chunk = own // CHUNKS
    trade = {links.core: links.h, links.high: links.c}
    spread_c, spread_d = Spread(links, cots, own), Spread(links, dh, own)
    sums2 = Sums(links, made2, come2, ready2, line2)
    sums3 = Sums(links, made3, come3, ready3, line3)
    sums1 = Sums(links, made1, come1, ready1, line1)
    swap_spots, out_spot = [links.take(), links.take()], links.take()
    grad = lambda partial, come, stage, sems, near, far: Gradient(
        links, partial, come, stage, stage_sems.at[sems], near, far
    )
    g_down = grad(p_down, come_down, stage0, 0, near_down, far_down)
    g_gate = grad(p_gate, come_gate, stage1, 1, near_gate, far_gate)
    g_up = grad(p_up, come_up, stage0, 0, near_up, far_up)
    g_out = grad(p_out, come_out, stage_out, 2, near_out, far_out)
    g_qkv = grad(p_qkv, come_qkv, stage1.at[:, :, pl.ds(0, 3 * width)], 1, near_qkv, far_qkv)

    near, rest = pl.ds(0, 2 * own), pl.ds(2 * own, 2 * own * (n_parts - 1))

    def trade_start(make, ins, src, dst, spot):
        @pl.when(links.same)
        def _():
            by_rows(make, chunk, ins, [dst])

        @pl.when(~links.same)
        def _():
            by_rows(make, chunk, ins, [src])
            links.copy(src, dst, trade, spot).start()

    def trade_wait(src, dst, spot):
        @pl.when(~links.same)
        def _():
            links.copy(src, dst, trade, spot).wait()

    links.greet()
    def same_rows(src, dst):
        dst[...] = src[...]

    for k_ in range(CHUNKS):
        spread_c.own_ready(k_, cot.at[pl.ds(k_ * chunk, chunk)])
    by_rows(same_rows, chunk, [cot], [cots.at[pl.ds(0, own)]])
    spread_c.wait_near()

    def feed_forward(rows):
        gated(
            norm2.at[rows], cots.at[rows], w_gate, w_up, w_down, act.at[rows], d_gate.at[rows],
            d_up.at[rows], min(512, 2 * own), 256,
        )

    def project_far(sums, make, at_once=CHUNKS):
        for part in reversed(range(1, n_parts)):
            for other in (1, 0):
                rows = pl.ds((part * 2 + other) * own, own)
                make(rows, sums.made.at[rows])
                if other:
                    sums.across(part).start()
            sums.far(part, at_once)

    def project_near(sums, make):
        make(near, sums.made.at[near])
        sums.across(0).start()

    def partials2(rows, goal):
        two_products(d_gate.at[rows], w_gate, d_up.at[rows], w_up, goal, own, 512)

    def partials1(rows, goal):
        matmul(NT, d_qkv.at[rows], w_qkv, goal, own, 512)

    def summed(terms):
        total = terms[0][...].astype(jnp.float32)
        for term in terms[1:]:
            total = total + term[...].astype(jnp.float32)
        return total

    def hidden_back(hid, c, *refs):
        *terms, wide_out, low_out = refs
        made = c[...].astype(jnp.float32) + norm_back(hid[...], summed(terms))
        wide_out[...] = made
        low_out[...] = low(made)

    def finish_out(hid, *refs):
        *terms, made = refs
        made[...] = low(hid[...] + summed(terms))

    def input_back(x, d, *refs):
        *terms, made = refs
        made[...] = low(d[...] + norm_back(x[...].astype(jnp.float32), summed(terms)))

    def last_steps(gradient):
        for step in range(1, gradient.n):
            gradient.step(step)

    feed_forward(near)
    for k_ in range(CHUNKS):
        spread_c.pass_on(k_)
    spread_c.wait_far()
    feed_forward(rest)
    matmul(NT, act.at[rest], w_down, made3.at[rest], 2 * own, 512)
    for part in reversed(range(1, n_parts)):
        sums3.across(part).start()
    matmul(NT, act.at[near], w_down, made3.at[near], 2 * own, 512)
    sums3.across(0).start()
    for part in reversed(range(1, n_parts)):
        sums3.far(part)
    project_far(sums2, partials2)
    matmul(TN, cots, act, p_down, 1024, 512)
    g_down.start()
    sums3.arrived()
    trade_start(finish_out, [hidden] + sums3.terms(), out_mine, out_low, out_spot)
    project_near(sums2, partials2)
    sums2.arrived()
    by_rows(
        hidden_back, chunk, [hidden, cot] + sums2.terms(), [d_hidden, dh.at[pl.ds(0, own)]]
    )
    for k_ in range(CHUNKS):
        spread_d.own_ready(k_)
    g_down.step(0)
    matmul(TN, norm2, d_gate, p_gate, 1024, 512)
    g_gate.start()
    last_steps(g_down)
    matmul(TN, norm2, d_up, p_up, 1024, 512)
    for k_ in range(CHUNKS):
        spread_d.pass_on(k_)
    spread_d.wait_near()
    spread_d.wait_far()
    matmul(NN, dh, w_out, d_att, own, width)
    matmul(TN, dh, att, p_out, 1024, width)
    g_gate.step(0)
    g_up.start()
    d_q, d_k, d_v = (d_qkv.at[:, pl.ds(s * width, width)] for s in range(3))
    half = heads // 2
    attention_back(
        links, q, k, v, d_att, att, lse_ref, cos_ref, sin_ref, end_ref, d_q, d_k, d_v, half, 0
    )
    last_steps(g_gate)
    attention_back(
        links, q, k, v, d_att, att, lse_ref, cos_ref, sin_ref, end_ref, d_q, d_k, d_v, heads - half, half
    )
    first = CHUNKS // 2
    project_far(sums1, partials1, first)
    g_up.step(0)
    g_out.start()
    project_near(sums1, partials1)
    sums1.start_late(first)
    matmul(TN, norm1, d_qkv, p_qkv, 1024, width)
    g_qkv.start()
    last_steps(g_up)
    g_out.step(0)
    for n, chunks in enumerate((range(first), range(first, CHUNKS))):
        rows = pl.ds(chunks[0] * chunk, len(chunks) * chunk)
        sums1.arrived(chunks)
        trade_start(
            input_back, [x_own.at[rows], d_hidden.at[rows]] + sums1.terms(rows), d_mine.at[rows],
            d_input.at[rows], swap_spots[n],
        )
    last_steps(g_out)
    g_qkv.step(0)
    last_steps(g_qkv)
    for n in range(2):
        rows = pl.ds(n * first * chunk, first * chunk)
        trade_wait(d_mine.at[rows], d_input.at[rows], swap_spots[n])
    trade_wait(out_mine, out_low, out_spot)
    for thing in (spread_c, spread_d, sums1, sums2, sums3, g_down, g_gate, g_up, g_out, g_qkv):
        thing.finish()


def second_half(places, norm2, cot, fulls, norm1, q, k, v, att, hidden, x_own, lse, cos, sin, end):
    own, model = cot.shape
    length, width = q.shape
    w_qkv, w_out, w_gate, w_up, w_down = fulls
    ff = w_gate.shape[1]
    groups = 2 ** len(places[0])
    n_parts = 2 ** len(places[3])
    rows = model // (2 * groups)
    shape = lambda *dims: jax.ShapeDtypeStruct(dims, jnp.bfloat16)
    wide = lambda *dims: jax.ShapeDtypeStruct(dims, jnp.float32)
    here, there = pl.BlockSpec(memory_space=pltpu.VMEM), pl.BlockSpec(memory_space=pl.ANY)
    pieces = [shape(rows, cols) for cols in (ff, ff, ff, width, 3 * width)]
    sums = [shape(length, model), shape(n_parts, own, model)] + [shape(n_parts - 1, own, model)] * 2
    out_shape = (
        [shape(own, model)] * 2
        + pieces * 2
        + [shape(length, model)]
        + [shape(length, ff)] * 3
        + [shape(model, cols) for cols in (ff, ff, ff, width, 3 * width)]
        + [shape(length, model), wide(own, model), shape(length, width), shape(length, 3 * width)]
        + sums * 3
        + [shape(own, model)] * 2
    )
    bf = lambda *dims: pltpu.VMEM(dims, jnp.bfloat16)
    blocks = 2 * (groups - 1)
    made = pl.pallas_call(
        functools.partial(second_kernel, places),
        in_specs=[there] * 14 + [here] * 4,
        out_specs=[there] * len(out_shape),
        out_shape=out_shape,
        scratch_shapes=[
            bf(blocks, rows, ff),
            bf(blocks, rows, ff),
            bf(blocks, rows, ff),
            bf(blocks, rows, width),
            bf(blocks, rows, 3 * width),
            bf(groups, rows, ff),
            bf(groups, rows, max(ff, 3 * width)),
            bf(groups, rows, width),
            pltpu.SemaphoreType.DMA((SEMS,)),
            pltpu.SemaphoreType.DMA((SEMS,)),
                        pltpu.SemaphoreType.DMA((3, groups)),
        ],
        compiler_params=pltpu.CompilerParams(
            collective_id=1, has_side_effects=True, vmem_limit_bytes=61 * 2**20
        ),
        cost_estimate=pl.CostEstimate(
            flops=18 * length * model * ff, bytes_accessed=300 * 2**20, transcendentals=length * length * 4
        ),
    )(
        norm2, cot, w_gate, w_up, w_down, w_out, w_qkv, norm1, q, k, v, att, hidden, x_own, lse, cos, sin, end
    )
    grads = [
        a.astype(jnp.float32) + b.astype(jnp.float32) for a, b in zip(made[2:7], made[7:12])
    ]
    return made[0], made[1], grads


def body(places, x, segments, padding, w_query, w_key, w_value, w_out, w_gate, w_up, w_down, cot):
    own = x.shape[0]
    length = segments.shape[0]
    cols = w_query.shape[1]
    same = lax.axis_index(places[1]) == lax.axis_index(places[2])
    counts = [jnp.sum(segments <= number, dtype=jnp.int32) for number in range(3)]
    last = jnp.where(segments == 0, counts[0], jnp.where(segments == 1, counts[1], counts[2])) - 1
    end_own = jnp.where(padding == 0, last, jnp.arange(length, dtype=jnp.int32)).reshape(-1, own)
    end = jnp.where(same, end_own, lax.ppermute(end_own, places[1], [(0, 1), (1, 0)]))
    cos, sin = turn_tables(length)
    mats = (jnp.concatenate([w_query, w_key, w_value], axis=1), w_out, w_gate, w_up, w_down)
    norm1, *fulls, q, k, v, att, lse, x_own, hidden, norm2, cot_own = first_half(
        places, x, end_own, cos, sin, mats, cot
    )
    output, d_input, (g_down, g_gate, g_up, g_out, g_qkv) = second_half(
        places, norm2, cot_own, fulls, norm1, q, k, v, att, hidden, x_own, lse, cos, sin, end
    )
    return (
        output,
        d_input.astype(jnp.float32),
        g_qkv[:, :cols],
        g_qkv[:, cols : 2 * cols],
        g_qkv[:, 2 * cols :],
        g_out,
        g_gate,
        g_up,
        g_down,
    )


def turn_tables(length):
    frequency = 10000.0 ** (-np.arange(HD // 2, dtype=np.float32) / np.float32(HD // 2))
    angles = np.arange(length, dtype=np.float32)[:, None] * frequency.astype(np.float32)[None, :]
    cos, sin = np.cos(angles), np.sin(angles)
    return (
        jnp.asarray(np.concatenate([cos, cos], axis=1), jnp.float32),
        jnp.asarray(np.concatenate([-sin, sin], axis=1), jnp.float32),
    )


def solution(mesh):
    dp, mp = mesh.devices.shape
    n_dp, n_mp = dp.bit_length() - 1, mp.bit_length() - 1
    dp_axes = tuple("d%d" % k for k in range(n_dp))
    mp_axes = tuple("m%d" % k for k in range(n_mp))
    fine = Mesh(mesh.devices.reshape((2,) * (n_dp + n_mp)), dp_axes + mp_axes)
    places = (dp_axes[:-1], dp_axes[-1], mp_axes[0], mp_axes[1:])
    tokens = P(dp_axes + mp_axes, None)
    weight = P(dp_axes, mp_axes)
    return jax.shard_map(
        functools.partial(body, places),
        mesh=fine,
        in_specs=(tokens, P(dp_axes), P(dp_axes)) + (weight,) * 7 + (tokens,),
        out_specs=(tokens, tokens) + (weight,) * 7,
        check_vma=False,
    )
```

```python
import functools
import jax
import jax.numpy as jnp
import numpy as np
from jax import lax
from jax.experimental import pallas as pl
from jax.experimental.pallas import tpu as pltpu
from jax.sharding import Mesh, PartitionSpec as P

HD = 128
SCALE = HD ** (-0.5)
LOG2E = 1.4426950408889634
NEG = -1e30
eps = 1e-05
NN = (((1,), (0,)), ((), ()))
NT = (((1,), (1,)), ((), ()))
TN = (((0,), (0,)), ((), ()))


def dot(left, right, dims=(((1,), (0,)), ((), ()))):
    return lax.dot_general(left, right, dims, preferred_element_type=jnp.float32)


def low(value):
    return value.astype(jnp.bfloat16)


def allowed_of(first_q, first_k, end_row, diagonal):
    blk = end_row.shape[1]
    t = first_q + lax.broadcasted_iota(jnp.int32, (blk, 1), 0)
    if not diagonal:
        return t <= end_row
    u = first_k + lax.broadcasted_iota(jnp.int32, (1, blk), 1)
    return (u <= t) & (t <= end_row)


MESH = pl.DeviceIdType.MESH
CHUNKS = 4
FINE = 8
SEMS = 320
MATS = ("qkv", "out", "gate", "up", "down")


def flipped(bit, other):
    return bit + other - 2 * bit * other


class Links:
    def __init__(self, places, send, recv):
        self.rest, self.core, self.high, self.lower = places
        self.c, self.h = lax.axis_index(self.core), lax.axis_index(self.high)
        self.r = [lax.axis_index(axis) for axis in self.rest]
        self.low = [lax.axis_index(axis) for axis in self.lower]
        self.same = self.c == self.h
        self.n_parts = 2 ** len(self.lower)
        self.send, self.recv, self.used, self.unsent = send, recv, 0, []
        self.across = {self.core: 1 - self.c}

    def beside(self, k):
        return {self.lower[k]: 1 - self.low[k]}

    def over(self, k):
        return {self.rest[k]: 1 - self.r[k]}

    def group(self, mask):
        total = 0
        for k, bit in enumerate(self.r):
            total = total * 2 + (1 - bit if mask >> k & 1 else bit)
        return total

    def swap_piece(self, number):
        other, part = number % 2, number // 2
        return flipped(self.c, other) * self.n_parts + self.turn(part)

    def piece(self, quarter):
        other, part = flipped(self.c, quarter // self.n_parts), self.turn(quarter % self.n_parts)
        return part * 2 + other

    def turn(self, part):
        total = 0
        for k, bit in enumerate(self.low):
            digit = part // 2 ** (len(self.low) - 1 - k) % 2
            total = total * 2 + flipped(bit, digit)
        return total

    def greet(self):
        barrier = pltpu.get_barrier_semaphore()
        partners = [
            self.across,
            {self.high: 1 - self.h},
            {self.core: 1 - self.c, self.high: 1 - self.h},
        ]
        partners += [self.beside(k) for k in range(len(self.lower))]
        partners += [self.over(k) for k in range(len(self.rest))]
        for partner in partners:
            pl.semaphore_signal(barrier, inc=1, device_id=partner, device_id_type=MESH)
        pl.semaphore_wait(barrier, len(partners))

    def take(self, count=1):
        self.used += count
        return self.used - count

    def copy(self, src, dst, partner, spot=None, recv=None):
        spot = self.take() if spot is None else spot
        made = pltpu.make_async_remote_copy(
            src_ref=src, dst_ref=dst, send_sem=self.send.at[spot],
            recv_sem=self.recv.at[spot if recv is None else recv],
            device_id=partner, device_id_type=MESH,
        )
        return made

    def push(self, src, dst, partner):
        made = self.copy(src, dst, partner)
        made.start()
        self.unsent.append(made)
        return made


class Weight:
    def __init__(self, links, shard, full):
        self.links, self.shard, self.full = links, shard, full
        self.rows = shard.shape[0]
        self.arrive = links.take(2)
        self.near, self.far = links.take(), links.take()
        self.stages = []
        n = len(links.rest)
        for step in range(n):
            stage = []
            for half in range(2):
                order = list(range(n)) if half == 0 else list(reversed(range(n)))
                have = [0]
                for k in order[:step]:
                    have = have + [mask | 1 << k for mask in have]
                stage += [(half, mask, order[step], links.take()) for mask in have]
            self.stages.append(stage)

    def slot(self, mask, core):
        start = (self.links.group(mask) * 2 + core) * self.rows
        return self.full.at[pl.ds(pl.multiple_of(start, self.rows), self.rows)]

    def near_copy(self):
        links = self.links
        return links.copy(
            self.shard, self.slot(0, links.c), links.across, self.near, self.arrive + links.c
        )

    def far_copy(self):
        links = self.links
        return links.copy(
            self.shard, self.slot(0, links.c), {links.core: links.h, links.high: 1 - links.h},
            self.far, self.arrive + links.c,
        )

    def keep_near(self, src):
        links = self.links
        pltpu.make_async_copy(
            src, self.slot(0, links.c), links.recv.at[self.arrive + links.c]
        ).start()

    def send_far(self):
        self.far_copy().start()

    def sent_far(self):
        self.far_copy().wait_send()

    def stage_copies(self, step):
        for half, mask, axis, spot in self.stages[step]:
            block = self.slot(mask, half)
            yield self.links.copy(block, block, self.links.over(axis), spot)

    def event(self, step):
        if step == 0:
            for core in range(2):
                block = self.slot(0, core)
                pltpu.make_async_copy(block, block, self.links.recv.at[self.arrive + core]).wait()
        else:
            for copy in self.stage_copies(step - 1):
                copy.wait_recv()
        if step < len(self.stages):
            for copy in self.stage_copies(step):
                copy.start()

    def finish(self):
        @pl.when(~self.links.same)
        def _():
            self.near_copy().wait_send()

        for step in range(len(self.stages)):
            for copy in self.stage_copies(step):
                copy.wait_send()


class Spread:
    def __init__(self, links, full, own, chunks):
        self.links, self.full, self.own, self.chunk = links, full, own, own // chunks
        self.moves, self.chunks = {}, chunks
        n = len(links.lower)
        for k in range(chunks):
            have = [0]
            for step in range(n):
                value = 2 ** (n - 1 - step)
                for part in have:
                    self.moves[k, part, step] = (part | value, links.take())
                have = have + [part | value for part in have]
            for part in range(links.n_parts):
                self.moves[k, part, None] = (part, links.take())

    def rows(self, part, other, k):
        return pl.ds((part * 2 + other) * self.own + k * self.chunk, self.chunk)

    def made(self, k, part, step, src=None):
        goal, spot = self.moves[k, part, step]
        links = self.links
        partner = links.across if step is None else links.beside(step)
        src = self.full.at[self.rows(part, 0, k)] if src is None else src
        dst = self.full.at[self.rows(goal, 1 if step is None else 0, k)]
        return links.copy(src, dst, partner, spot)

    def first_step(self, part):
        n = len(self.links.lower)
        return [s for s in range(n) if (0, part, s) in self.moves]

    def own_ready(self, k, src=None):
        for step in self.first_step(0):
            self.made(k, 0, step, src).start()
        self.made(k, 0, None, src).start()

    def pass_on(self, k):
        n = len(self.links.lower)
        for step in range(n):
            value = 2 ** (n - 1 - step)
            for part in range(self.links.n_parts):
                if (k, part, step) in self.moves:
                    self.made(k, part, step).wait_recv()
                    goal = part | value
                    for later in self.first_step(goal):
                        self.made(k, goal, later).start()
                    self.made(k, goal, None).start()

    def wait_near(self):
        for k in range(self.chunks):
            self.made(k, 0, None).wait_recv()

    def wait_far(self):
        for k in range(self.chunks):
            for part in range(1, self.links.n_parts):
                self.made(k, part, None).wait_recv()

    def finish(self):
        for k, part, step in self.moves:
            self.made(k, part, step).wait_send()


def normed(value):
    average = jnp.mean(value, axis=-1, keepdims=True)
    centred = value - average
    variance = jnp.mean(centred * centred, axis=-1, keepdims=True)
    return centred * lax.rsqrt(variance + eps)


def spin(value, cos, sin):
    return value * cos + pltpu.roll(value, HD // 2, 1) * sin


def first_kernel(
    places, x, end_mine, cos_ref, sin_ref, w_qkv, w_out, w_gate, w_up, w_down, cot,
    norm1, qkv_all, out_all, gate_all, up_all, down_all, q_ref, k_ref, v_ref, att_ref, lse_ref, x_own, hidden,
    norm2, cot_own, norm1_v, qkv_v, out_v, end_other, p_mine, p_other, p_come, line, send, recv, local,
):
    links = Links(places, send, recv)
    own = x.shape[0]
    n_parts, n_pieces = links.n_parts, 2 * links.n_parts
    n_low = len(links.lower)
    chunk = own // FINE
    heads = q_ref.shape[1] // HD
    width = heads * HD
    weights = {
        name: Weight(links, shard, full)
        for name, shard, full in zip(
            MATS,
            (w_qkv, w_out, w_gate, w_up, w_down),
            (qkv_v, out_v, gate_all, up_all, down_all),
        )
    }
    n_steps = len(links.rest)
    swap_spots = [links.take() for _ in range(FINE)]
    cot_spot, end_spot = links.take(), links.take()
    trade = {links.core: links.h, links.high: links.c}

    def swap_copy(k):
        rows = pl.ds(k * chunk, chunk)
        return links.copy(x.at[rows], x_own.at[rows], trade, swap_spots[k])

    def swap_local(k):
        rows = pl.ds(k * chunk, chunk)
        return pltpu.make_async_copy(x.at[rows], x_own.at[rows], recv.at[swap_spots[k]])

    def cot_copy():
        return links.copy(cot, cot_own, trade, cot_spot)

    def cot_local():
        return pltpu.make_async_copy(p_mine.at[0], cot_own, recv.at[cot_spot])

    end_copy = links.copy(end_mine, end_other, links.across, end_spot)
    spread1 = Spread(links, norm1_v, own, FINE)
    norm2_v = norm1_v
    spread2 = Spread(links, norm2_v, own, FINE)
    across_spots = [links.take() for _ in range(n_parts)]
    line_spots = {
        (part, k): links.take() for part in range(1, n_parts) for k in range(FINE)
    }

    rest = []
    for number, name in enumerate(MATS[2:]):
        shard = weights[name].shard
        rows, cols = shard.shape
        hold = p_other.at[number // 2, pl.ds(number % 2 * rows, rows), pl.ds(0, cols)]
        rest.append((name, hold, pltpu.make_async_copy(shard, hold, local.at[number])))
    cot_load = pltpu.make_async_copy(cot, p_mine.at[0], local.at[3])

    links.greet()
    end_copy.start()
    weights["qkv"].send_far()

    @pl.when(links.same)
    def _():
        for k in range(FINE):
            swap_local(k).start()
        for name in MATS[:2]:
            weights[name].keep_near(weights[name].shard)
        for _, _, load in rest:
            load.start()
        cot_load.start()

    @pl.when(~links.same)
    def _():
        for name in MATS:
            weights[name].near_copy().start()

    def norm_chunk(k):
        rows = pl.ds(k * chunk, chunk)
        norm1_v[rows, :] = low(normed(x_own[rows, :].astype(jnp.float32)))
        spread1.own_ready(k)

    def run(name, *steps):
        for step in steps:
            weights[name].event(step)

    last = n_steps

    @pl.when(links.same)
    def _():
        for k in range(FINE):
            swap_local(k).wait()
            norm_chunk(k)
        for name, hold, load in rest:
            load.wait()
            weights[name].keep_near(hold)
        cot_load.wait()
        cot_local().start()
        run("qkv", *range(last + 1))
        run("out", *range(last + 1))
        weights["qkv"].sent_far()
        run("gate", *range(last + 1))
        run("up", 0)

    @pl.when(~links.same)
    def _():
        weights["qkv"].sent_far()
        for k in range(2):
            swap_copy(k).start()
        run("qkv", 0)
        for k in range(FINE):
            swap_copy(k).wait_send()
            if k + 2 < FINE:
                swap_copy(k + 2).start()
            swap_copy(k).wait_recv()
            norm_chunk(k)
            if k == 1:
                run("qkv", *range(1, last))
        run("qkv", last)

    weights["out"].send_far()
    end_copy.wait_recv()
    for k in range(FINE):
        spread1.pass_on(k)

    keep = [pltpu.make_async_copy(qkv_v, qkv_all, local.at[4])]
    keep[0].start()

    def project(pieces):
        for section, goal in enumerate((q_ref, k_ref, v_ref)):
            for number in pieces:
                rows = slice(number * own, (number + 1) * own)
                spot = pl.ds(pl.multiple_of(links.swap_piece(number) * own, own), own)

                @pl.loop(0, heads // 2)
                def _(tile, section=section, goal=goal, rows=rows, spot=spot):
                    start = pl.multiple_of(tile * 2 * HD, 2 * HD)
                    made = dot(norm1_v[rows, :], qkv_v[:, pl.ds(section * width + start, 2 * HD)])
                    for k in range(2):
                        value = made[:, k * HD : (k + 1) * HD]
                        if section < 2:
                            value = spin(value, cos_ref[spot, :], sin_ref[spot, :])
                        goal[rows, pl.ds(pl.multiple_of(start + k * HD, HD), HD)] = low(value)

    spread1.wait_near()
    project((0, 1))
    weights["gate"].send_far()

    @pl.when(links.same)
    def _():
        run("up", *range(1, last))

    @pl.when(~links.same)
    def _():
        run("out", 0)

    spread1.wait_far()
    project(range(2, n_pieces))
    keep.append(pltpu.make_async_copy(norm1_v, norm1, local.at[5]))
    keep[-1].start()

    @pl.when(links.same)
    def _():
        run("up", last)
        run("down", 0)

    @pl.when(~links.same)
    def _():
        run("out", *range(1, last + 1))

    keep.append(pltpu.make_async_copy(out_v, out_all, local.at[6]))
    keep[-1].start()

    lanes = lax.broadcasted_iota(jnp.int32, (own, HD), 1)
    for head in range(heads):
        cols = slice(head * HD, (head + 1) * HD)

        @pl.loop(0, n_pieces)
        def _(i, head=head, cols=cols):
            rows = pl.ds(pl.multiple_of(i * own, own), own)
            quarter = links.swap_piece(i)

            def step(diagonal, n, carry):
                top, total, acc = carry
                spot = pl.ds(pl.multiple_of(links.piece(n) * own, own), own)
                end = jnp.where(links.same, end_mine[pl.ds(n, 1), :], end_other[pl.ds(n, 1), :])
                allowed = allowed_of(quarter * own, n * own, end, diagonal)
                scores = dot(q_ref[rows, cols], k_ref[spot, cols], NT)
                scores = jnp.where(allowed, scores * (SCALE * LOG2E), NEG)
                new_top = jnp.maximum(top, jnp.max(scores, axis=1, keepdims=True))
                grown = jnp.exp2(scores - new_top)
                shrink = jnp.exp2(top - new_top)
                total = total * shrink + jnp.sum(grown, axis=1, keepdims=True)
                return new_top, total, acc * shrink + dot(low(grown), v_ref[spot, cols])

            carry = lax.fori_loop(
                0, quarter, functools.partial(step, False),
                (
                    jnp.full((own, 1), NEG, jnp.float32),
                    jnp.zeros((own, 1), jnp.float32),
                    jnp.zeros((own, HD), jnp.float32),
                ),
            )
            top, total, acc = step(True, quarter, carry)
            att_ref[rows, cols] = low(acc / total)
            lse = jnp.broadcast_to(top + jnp.log2(total), (own, HD))
            lse_ref[rows, :] = lse if head == 0 else jnp.where(lanes == head, lse, lse_ref[rows, :])

        if head == 0:

            @pl.when(links.same)
            def _():
                run("down", *range(1, last))

        if head == heads // 2 - 1:
            weights["gate"].sent_far()
            weights["up"].send_far()

    @pl.when(links.same)
    def _():
        cot_local().wait()
        run("down", last)

    @pl.when(~links.same)
    def _():
        run("gate", 0)

    keep.pop(1).wait()
    spread1.finish()

    def across_copy(part):
        return links.copy(p_other.at[part], p_come.at[part], links.across, across_spots[part])

    def line_copy(part, k):
        rows = pl.ds(k * chunk, chunk)
        step = n_low - part.bit_length()
        return links.copy(
            p_mine.at[part, rows], line.at[part - 1, rows], links.beside(step), line_spots[part, k]
        )

    def out_rows(number, goal):
        rows = slice(number * own, (number + 1) * own)
        tile = 512

        @pl.loop(0, out_v.shape[0] // tile)
        def _(n):
            start = pl.multiple_of(n * tile, tile)
            goal[:, pl.ds(start, tile)] = low(
                dot(att_ref[rows, :], out_v[pl.ds(start, tile), :], NT)
            )

    for part in reversed(range(n_parts)):
        out_rows(part * 2 + 1, p_other.at[part])
        across_copy(part).start()
        out_rows(part * 2, p_mine.at[part])
        across_copy(part).wait_recv()
        for k in range(FINE):
            rows = pl.ds(k * chunk, chunk)
            total = p_mine[part, rows, :].astype(jnp.float32) + p_come[part, rows, :].astype(jnp.float32)
            if part == 0:
                hidden[rows, :] = x_own[rows, :].astype(jnp.float32) + total
            else:
                step = part.bit_length() - 1
                for high in range(step + 1, n_low):
                    more = part | 1 << high
                    line_copy(more, k).wait_recv()
                    total = total + line[more - 1, rows, :].astype(jnp.float32)
                p_mine[part, rows, :] = low(total)
                if k < 2 or part & (part - 1):
                    line_copy(part, k).start()

    @pl.when(~links.same)
    def _():
        run("gate", *range(1, last))

    lined = [1 << step for step in range(n_low)]
    for k in range(FINE):
        rows = pl.ds(k * chunk, chunk)
        for part in lined:
            line_copy(part, k).wait_send()
            if k + 2 < FINE:
                line_copy(part, k + 2).start()
        total = hidden[rows, :]
        for part in lined:
            line_copy(part, k).wait_recv()
            total = total + line[part - 1, rows, :].astype(jnp.float32)
        hidden[rows, :] = total
        norm2_v[rows, :] = low(normed(total))
        spread2.own_ready(k)
        if k == 0:
            weights["up"].sent_far()
            weights["down"].send_far()

        @pl.when(~links.same)
        def _():
            if k == 2:
                run("gate", last)
                run("up", 0)
            if k == 4:
                run("up", *range(1, last))

    for k in range(FINE):

        @pl.when(~links.same)
        def _():
            if k == 0:
                run("up", last)
            if k == 2:
                run("down", 0)
            if k == 4:
                run("down", *range(1, last))

        if k == 2:
            weights["down"].sent_far()

            @pl.when(~links.same)
            def _():
                cot_copy().start()

        spread2.pass_on(k)

    spread2.wait_near()
    spread2.wait_far()
    keep.append(pltpu.make_async_copy(norm2_v, norm2, local.at[7]))
    keep[-1].start()

    @pl.when(~links.same)
    def _():
        run("down", last)
        cot_copy().wait()

    end_copy.wait_send()
    spread2.finish()
    for weight in weights.values():
        weight.finish()
    weights["out"].sent_far()
    for part in range(n_parts):
        across_copy(part).wait_send()
    for part, k in line_spots:
        if part & (part - 1):
            line_copy(part, k).wait_send()
    for made in keep:
        made.wait()


def first_half(places, x, end_mine, cos, sin, mats, cot):
    own, model = x.shape
    n_parts = 2 ** len(places[3])
    length = 2 * n_parts * own
    groups = 2 ** len(places[0])
    width = mats[1].shape[1]
    shape = lambda *dims: jax.ShapeDtypeStruct(dims, jnp.bfloat16)
    wide = lambda *dims: jax.ShapeDtypeStruct(dims, jnp.float32)
    here, there = pl.BlockSpec(memory_space=pltpu.VMEM), pl.BlockSpec(memory_space=pl.ANY)
    fulls = [shape(2 * groups * mat.shape[0], mat.shape[1]) for mat in mats]
    bf = lambda *dims: pltpu.VMEM(dims, jnp.bfloat16)
    return pl.pallas_call(
        functools.partial(first_kernel, places),
        in_specs=[there, here, here, here] + [there] * 6,
        out_specs=[there] * 6 + [here] * 7 + [there] * 2,
        out_shape=[shape(length, model)]
        + fulls
        + [shape(length, width)] * 4
        + [wide(length, HD), shape(own, model), wide(own, model)]
        + [shape(length, model), shape(own, model)],
        scratch_shapes=[
            bf(length, model),
            bf(*fulls[0].shape),
            bf(*fulls[1].shape),
            pltpu.VMEM(end_mine.shape, jnp.int32),
            bf(n_parts, own, model),
            bf(n_parts, own, model),
            bf(n_parts, own, model),
            bf(max(n_parts - 1, 1), own, model),
            pltpu.SemaphoreType.DMA((SEMS,)),
            pltpu.SemaphoreType.DMA((SEMS,)),
            pltpu.SemaphoreType.DMA((8,)),
        ],
        compiler_params=pltpu.CompilerParams(
            collective_id=0, has_side_effects=True, vmem_limit_bytes=61 * 2**20
        ),
        cost_estimate=pl.CostEstimate(
            flops=8 * length * model * width,
            bytes_accessed=100 * 2**20,
            transcendentals=length * length * 4,
        ),
    )(x, end_mine, cos, sin, *mats, cot)


def matmul(kind, left, right, out, rows, cols):
    depth = left.shape[0] if kind == TN else left.shape[1]

    def tile(a, b, made):
        made[...] = low(dot(a[...], b[...], kind))

    a_spec = (
        pl.BlockSpec((depth, rows), lambda i, j: (0, i))
        if kind == TN
        else pl.BlockSpec((rows, depth), lambda i, j: (i, 0))
    )
    b_spec = (
        pl.BlockSpec((cols, depth), lambda i, j: (j, 0))
        if kind == NT
        else pl.BlockSpec((depth, cols), lambda i, j: (0, j))
    )
    pltpu.emit_pipeline(
        tile,
        grid=(out.shape[0] // rows, out.shape[1] // cols),
        in_specs=[a_spec, b_spec],
        out_specs=[pl.BlockSpec((rows, cols), lambda i, j: (i, j))],
    )(left, right, out)


def two_products(left1, right1, left2, right2, out, rows, cols):
    def tile(a, b, c, d, made):
        made[...] = low(dot(a[...], b[...], NT) + dot(c[...], d[...], NT))

    depth = left1.shape[1]
    held = pl.BlockSpec((rows, depth), lambda i, j: (i, 0))
    moving = pl.BlockSpec((cols, depth), lambda i, j: (j, 0))
    pltpu.emit_pipeline(
        tile,
        grid=(out.shape[0] // rows, out.shape[1] // cols),
        in_specs=[held, moving, held, moving],
        out_specs=[pl.BlockSpec((rows, cols), lambda i, j: (i, j))],
    )(left1, right1, left2, right2, out)


def by_rows(make, rows, ins, outs):
    spec = lambda ref: pl.BlockSpec((rows, ref.shape[1]), lambda i: (i, 0))
    pltpu.emit_pipeline(
        make,
        grid=(outs[0].shape[0] // rows,),
        in_specs=[spec(ref) for ref in ins],
        out_specs=[spec(ref) for ref in outs],
    )(*ins, *outs)


def gated(norm, cots, w_gate, w_up, w_down, act, d_gate, d_up, rows, cols):
    def tile(n, c, wg, wu, wd, act_t, gate_t, up_t):
        gate, up = dot(n[...], wg[...]), dot(n[...], wu[...])
        d_act = dot(c[...], wd[...])
        s = 1.0 / (1.0 + jnp.exp(-gate))
        silu = gate * s
        act_t[...] = low(silu * up)
        gate_t[...] = low(d_act * up * s * (1.0 + gate * (1.0 - s)))
        up_t[...] = low(d_act * silu)

    depth = norm.shape[1]
    row = pl.BlockSpec((rows, depth), lambda i, j: (i, 0))
    col = pl.BlockSpec((depth, cols), lambda i, j: (0, j))
    made = pl.BlockSpec((rows, cols), lambda i, j: (i, j))
    pltpu.emit_pipeline(
        tile,
        grid=(act.shape[0] // rows, act.shape[1] // cols),
        in_specs=[row, row, col, col, col],
        out_specs=[made] * 3,
    )(norm, cots, w_gate, w_up, w_down, act, d_gate, d_up)


def norm_back(value, grad):
    average = jnp.mean(value, axis=-1, keepdims=True)
    centred = value - average
    r = lax.rsqrt(jnp.mean(centred * centred, axis=-1, keepdims=True) + eps)
    n = centred * r
    return r * (
        grad - jnp.mean(grad, axis=-1, keepdims=True) - n * jnp.mean(grad * n, axis=-1, keepdims=True)
    )


class Sums:
    def __init__(self, links, made, come, ready, line):
        self.links, self.made = links, made
        self.come, self.ready, self.line = come, ready, line
        n_parts, self.own, _ = come.shape
        self.n_parts = n_parts
        self.chunk = self.own // CHUNKS
        self.spots = [links.take() for _ in range(n_parts)]
        self.line_spots = {
            (part, k): links.take() for part in range(1, n_parts) for k in range(CHUNKS)
        }

    def piece(self, part, other):
        return self.made.at[pl.ds((part * 2 + other) * self.own, self.own)]

    def across(self, part):
        links = self.links
        return links.copy(self.piece(part, 1), self.come.at[part], links.across, self.spots[part])

    def along(self, part, k):
        links = self.links
        rows = pl.ds(k * self.chunk, self.chunk)
        step = len(links.lower) - part.bit_length()
        return links.copy(
            self.ready.at[part - 1, rows], self.line.at[part - 1, rows], links.beside(step),
            self.line_spots[part, k],
        )

    def more(self, part):
        return [part | 1 << k for k in range(part.bit_length(), len(self.links.lower))]

    def far(self, part, at_once=CHUNKS):
        self.across(part).wait_recv()
        ins = [self.piece(part, 0), self.come.at[part]]
        for number in self.more(part):
            for k in range(CHUNKS):
                self.along(number, k).wait_recv()
            ins.append(self.line.at[number - 1])

        def make(*refs):
            total = refs[0][...].astype(jnp.float32)
            for ref in refs[1:-1]:
                total = total + ref[...].astype(jnp.float32)
            refs[-1][...] = low(total)

        by_rows(make, self.chunk, ins, [self.ready.at[part - 1]])
        for k in range(CHUNKS if part & (part - 1) else at_once):
            self.along(part, k).start()

    def start_late(self, first):
        for part in self.more(0):
            for k in range(first, CHUNKS):
                self.along(part, k).start()

    def arrived(self, chunks=range(CHUNKS)):
        if 0 in chunks:
            self.across(0).wait_recv()
        for number in self.more(0):
            for k in chunks:
                self.along(number, k).wait_recv()

    def terms(self, rows=None):
        rows = pl.ds(0, self.own) if rows is None else rows
        return [self.piece(0, 0).at[rows], self.come.at[0, rows]] + [
            self.line.at[number - 1, rows] for number in self.more(0)
        ]

    def finish(self):
        for part in range(self.n_parts):
            self.across(part).wait_send()
        for part, k in self.line_spots:
            self.along(part, k).wait_send()


class Gradient:
    def __init__(self, links, partial, come, stage, stage_sems, near, far):
        self.links, self.partial, self.come, self.stage = links, partial, come, stage
        self.stage_sems, self.near, self.far = stage_sems, near, far
        self.rows = near.shape[0]
        n = len(links.rest)
        self.n = n
        self.kept, self.sent, self.place, self.spots = {}, {}, {}, {}
        for half in range(2):
            order = list(reversed(range(n))) if half == 0 else list(range(n))
            have = list(range(2**n))
            for step, axis in enumerate(order):
                self.sent[half, step] = (axis, [mask for mask in have if mask >> axis & 1])
                have = [mask for mask in have if not mask >> axis & 1]
                self.kept[half, step] = have
                for mask in have:
                    self.place[half, step, mask] = len(self.place)
                    self.spots[half, step, mask] = links.take()
        self.near_spot, self.far_spot = links.take(), links.take()
        self.out_spots = [links.take(), links.take()]

    def slot(self, mask, half):
        start = (self.links.group(mask) * 2 + half) * self.rows
        return self.partial.at[pl.ds(pl.multiple_of(start, self.rows), self.rows)]

    def block(self, half, step, mask):
        return self.come.at[self.place[half, step, mask]]

    def copies(self, step):
        for half in range(2):
            axis, masks = self.sent[half, step]
            for mask in masks:
                goal = mask & ~(1 << axis)
                src = self.slot(mask, half) if step == 0 else self.block(half, step - 1, mask)
                yield self.links.copy(
                    src, self.block(half, step, goal), self.links.over(axis), self.spots[half, step, goal]
                )

    def loads(self):
        number = 0
        for half in range(2):
            for mask in self.kept[half, 0]:
                yield pltpu.make_async_copy(
                    self.slot(mask, half), self.stage.at[number], self.stage_sems.at[number]
                )
                number += 1

    def start(self):
        for copy in self.copies(0):
            copy.start()
        for load in self.loads():
            load.start()

    def step(self, step):
        for copy in self.copies(step):
            copy.wait_recv()
        if step == 0:
            for load in self.loads():
                load.wait()
        number = 0
        for half in range(2):
            for mask in self.kept[half, step]:
                goal = self.block(half, step, mask)
                add = self.stage.at[number] if step == 0 else self.block(half, step - 1, mask)
                number += 1
                rows = min(64, self.rows)

                @pl.loop(0, self.rows // rows)
                def _(i, goal=goal, add=add):
                    spot = pl.ds(pl.multiple_of(i * rows, rows), rows)
                    goal[spot, :] = low(
                        goal[spot, :].astype(jnp.float32) + add[spot, :].astype(jnp.float32)
                    )

        if step + 1 < self.n:
            for copy in self.copies(step + 1):
                copy.start()
        else:
            self.hand()

    def total(self, half):
        first, second = (self.place[k, self.n - 1, 0] for k in range(2))
        return self.come.at[first + half * (second - first)]

    def near_local(self):
        links = self.links
        return pltpu.make_async_copy(self.total(links.c), self.near, links.recv.at[self.near_spot])

    def near_copy(self):
        links = self.links
        return links.copy(self.total(1 - links.c), self.near, links.across, self.near_spot)

    def far_copy(self, half):
        links = self.links
        return links.copy(
            self.total(half), self.far, {links.core: half, links.high: links.c},
            self.out_spots[half], self.far_spot,
        )

    def hand(self):
        links = self.links

        @pl.when(links.same)
        def _():
            self.near_local().start()
            self.near_copy().start()

        @pl.when(~links.same)
        def _():
            for half in range(2):
                self.far_copy(half).start()

    def finish(self):
        links = self.links
        for step in range(self.n):
            for copy in self.copies(step):
                copy.wait_send()

        @pl.when(links.same)
        def _():
            self.near_local().wait()
            self.near_copy().wait_send()

        @pl.when(~links.same)
        def _():
            self.near_copy().wait_recv()
            for half in range(2):
                self.far_copy(half).wait_send()

        self.far_copy(0).wait_recv()


def attention_back(links, q, k, v, grad, att, lse_ref, cos_ref, sin_ref, end_ref, d_q, d_k, d_v, heads, start):
    length = q.shape[0]
    n_pieces, own = end_ref.shape

    def scoped(dq_acc, dk_acc, dv_acc, delta, lses):
        def one(q_ref, k_ref, v_ref, grad_ref, att_ref, dq_ref, dk_ref, dv_ref):
            head = pl.program_id(0) + start
            dq_acc[...] = jnp.zeros_like(dq_acc)
            dk_acc[...] = jnp.zeros_like(dk_acc)
            dv_acc[...] = jnp.zeros_like(dv_acc)
            lanes = lax.broadcasted_iota(jnp.int32, lse_ref.shape, 1)
            mine = jnp.where(lanes == head, lse_ref[...], 0.0)
            lses[...] = jnp.broadcast_to(jnp.sum(mine, axis=1, keepdims=True), mine.shape)
            prod = grad_ref[...].astype(jnp.float32) * att_ref[...].astype(jnp.float32)
            delta[...] = jnp.broadcast_to(jnp.sum(prod, axis=1, keepdims=True), prod.shape)

            @pl.loop(0, n_pieces)
            def _(i):
                rows = pl.ds(pl.multiple_of(i * own, own), own)
                quarter = links.swap_piece(i)

                def step(diagonal, n, carry):
                    spot = pl.ds(pl.multiple_of(links.piece(n) * own, own), own)
                    allowed = allowed_of(quarter * own, n * own, end_ref[pl.ds(n, 1), :], diagonal)
                    qb, kb, vb, gb = q_ref[rows, :], k_ref[spot, :], v_ref[spot, :], grad_ref[rows, :]
                    scores = dot(qb, kb, NT) * (SCALE * LOG2E)
                    probs = jnp.where(allowed, jnp.exp2(scores - lses[rows, 0:1]), 0.0)
                    d_probs = dot(gb, vb, NT)
                    d_scores = low(probs * (d_probs - delta[rows, 0:1]))
                    dv_acc[spot, :] += dot(low(probs), gb, TN)
                    dk_acc[spot, :] += dot(d_scores, qb, TN)
                    dq_acc[rows, :] += dot(d_scores, kb)
                    return carry

                lax.fori_loop(0, quarter, functools.partial(step, False), 0)
                step(True, quarter, 0)

            for number in range(n_pieces):
                rows = slice(number * own, (number + 1) * own)
                spot = pl.ds(pl.multiple_of(links.swap_piece(number) * own, own), own)
                cos, sin = cos_ref[spot, :], sin_ref[spot, :]
                dq_ref[rows, :] = low(spin(dq_acc[rows, :] * SCALE, cos, -sin))
                dk_ref[rows, :] = low(spin(dk_acc[rows, :] * SCALE, cos, -sin))
            dv_ref[...] = low(dv_acc[...])

        col = pl.BlockSpec((length, HD), lambda g: (0, g + start))
        pltpu.emit_pipeline(
            one, grid=(heads,), in_specs=[col] * 5, out_specs=[col] * 3
        )(q, k, v, grad, att, d_q, d_k, d_v)

    wide = pltpu.VMEM((length, HD), jnp.float32)
    pl.run_scoped(scoped, wide, wide, wide, wide, wide)


def second_kernel(
    places, norm2, cot, w_gate, w_up, w_down, w_out, w_qkv, norm1, q, k, v, att, hidden, x_own,
    lse_ref, cos_ref, sin_ref, end_ref,
    out_low, d_input, near_down, near_gate, near_up, near_out, near_qkv,
    far_down, far_gate, far_up, far_out, far_qkv,
    cots, act, d_gate, d_up, p_down, p_gate, p_up, p_out, p_qkv, dh, d_hidden, d_att, d_qkv,
    made2, come2, ready2, line2, made3, come3, ready3, line3, made1, come1, ready1, line1, out_mine, d_mine,
    come_down, come_gate, come_up, come_out, come_qkv, stage0, stage1, stage_out, send, recv, stage_sems,
):
    links = Links(places, send, recv)
    own, model = cot.shape
    n_parts = links.n_parts
    width = q.shape[1]
    heads = width // HD
    chunk = own // CHUNKS
    trade = {links.core: links.h, links.high: links.c}
    spread_c, spread_d = Spread(links, cots, own, CHUNKS), Spread(links, dh, own, CHUNKS)
    sums2 = Sums(links, made2, come2, ready2, line2)
    sums3 = Sums(links, made3, come3, ready3, line3)
    sums1 = Sums(links, made1, come1, ready1, line1)
    swap_spots, out_spot = [links.take(), links.take()], links.take()
    grad = lambda partial, come, stage, sems, near, far: Gradient(
        links, partial, come, stage, stage_sems.at[sems], near, far
    )
    g_down = grad(p_down, come_down, stage0, 0, near_down, far_down)
    g_gate = grad(p_gate, come_gate, stage1, 1, near_gate, far_gate)
    g_up = grad(p_up, come_up, stage0, 0, near_up, far_up)
    g_out = grad(p_out, come_out, stage_out, 2, near_out, far_out)
    g_qkv = grad(p_qkv, come_qkv, stage1.at[:, :, pl.ds(0, 3 * width)], 1, near_qkv, far_qkv)

    near, rest = pl.ds(0, 2 * own), pl.ds(2 * own, 2 * own * (n_parts - 1))

    def trade_start(make, ins, src, dst, spot):
        @pl.when(links.same)
        def _():
            by_rows(make, chunk, ins, [dst])

        @pl.when(~links.same)
        def _():
            by_rows(make, chunk, ins, [src])
            links.copy(src, dst, trade, spot).start()

    def trade_wait(src, dst, spot):
        @pl.when(~links.same)
        def _():
            links.copy(src, dst, trade, spot).wait()

    links.greet()
    def same_rows(src, dst):
        dst[...] = src[...]

    for k_ in range(CHUNKS):
        spread_c.own_ready(k_, cot.at[pl.ds(k_ * chunk, chunk)])
    by_rows(same_rows, chunk, [cot], [cots.at[pl.ds(0, own)]])
    spread_c.wait_near()

    def feed_forward(rows):
        gated(
            norm2.at[rows], cots.at[rows], w_gate, w_up, w_down, act.at[rows], d_gate.at[rows],
            d_up.at[rows], min(512, 2 * own), 256,
        )

    def project_far(sums, make, at_once=CHUNKS):
        for part in reversed(range(1, n_parts)):
            for other in (1, 0):
                rows = pl.ds((part * 2 + other) * own, own)
                make(rows, sums.made.at[rows])
                if other:
                    sums.across(part).start()
            sums.far(part, at_once)

    def project_near(sums, make):
        make(near, sums.made.at[near])
        sums.across(0).start()

    def partials2(rows, goal):
        two_products(d_gate.at[rows], w_gate, d_up.at[rows], w_up, goal, own, 512)

    def partials1(rows, goal):
        matmul(NT, d_qkv.at[rows], w_qkv, goal, own, 512)

    def summed(terms):
        total = terms[0][...].astype(jnp.float32)
        for term in terms[1:]:
            total = total + term[...].astype(jnp.float32)
        return total

    def hidden_back(hid, c, *refs):
        *terms, wide_out, low_out = refs
        made = c[...].astype(jnp.float32) + norm_back(hid[...], summed(terms))
        wide_out[...] = made
        low_out[...] = low(made)

    def finish_out(hid, *refs):
        *terms, made = refs
        made[...] = low(hid[...] + summed(terms))

    def input_back(x, d, *refs):
        *terms, made = refs
        made[...] = low(d[...] + norm_back(x[...].astype(jnp.float32), summed(terms)))

    def last_steps(gradient):
        for step in range(1, gradient.n):
            gradient.step(step)

    feed_forward(near)
    for k_ in range(CHUNKS):
        spread_c.pass_on(k_)
    spread_c.wait_far()
    feed_forward(rest)
    matmul(NT, act.at[rest], w_down, made3.at[rest], 2 * own, 512)
    for part in reversed(range(1, n_parts)):
        sums3.across(part).start()
    matmul(NT, act.at[near], w_down, made3.at[near], 2 * own, 512)
    sums3.across(0).start()
    for part in reversed(range(1, n_parts)):
        sums3.far(part)
    project_far(sums2, partials2)
    matmul(TN, cots, act, p_down, 1024, 512)
    g_down.start()
    sums3.arrived()
    trade_start(finish_out, [hidden] + sums3.terms(), out_mine, out_low, out_spot)
    project_near(sums2, partials2)
    sums2.arrived()
    by_rows(
        hidden_back, chunk, [hidden, cot] + sums2.terms(), [d_hidden, dh.at[pl.ds(0, own)]]
    )
    for k_ in range(CHUNKS):
        spread_d.own_ready(k_)
    g_down.step(0)
    matmul(TN, norm2, d_gate, p_gate, 1024, 512)
    g_gate.start()
    last_steps(g_down)
    matmul(TN, norm2, d_up, p_up, 1024, 512)
    for k_ in range(CHUNKS):
        spread_d.pass_on(k_)
    spread_d.wait_near()
    spread_d.wait_far()
    matmul(NN, dh, w_out, d_att, own, width)
    g_gate.step(0)
    g_up.start()
    matmul(TN, dh, att, p_out, 1024, width)
    d_q, d_k, d_v = (d_qkv.at[:, pl.ds(s * width, width)] for s in range(3))
    half = 1
    attention_back(
        links, q, k, v, d_att, att, lse_ref, cos_ref, sin_ref, end_ref, d_q, d_k, d_v, half, 0
    )
    last_steps(g_gate)
    attention_back(
        links, q, k, v, d_att, att, lse_ref, cos_ref, sin_ref, end_ref, d_q, d_k, d_v, heads - half, half
    )
    first = CHUNKS // 2
    g_up.step(0)
    project_far(sums1, partials1, first)
    last_steps(g_up)
    g_out.start()
    project_near(sums1, partials1)
    sums1.start_late(first)
    matmul(TN, norm1, d_qkv, p_qkv, 1024, width)
    g_qkv.start()
    g_out.step(0)
    for n, chunks in enumerate((range(first), range(first, CHUNKS))):
        rows = pl.ds(chunks[0] * chunk, len(chunks) * chunk)
        sums1.arrived(chunks)
        trade_start(
            input_back, [x_own.at[rows], d_hidden.at[rows]] + sums1.terms(rows), d_mine.at[rows],
            d_input.at[rows], swap_spots[n],
        )
    last_steps(g_out)
    g_qkv.step(0)
    last_steps(g_qkv)
    for n in range(2):
        rows = pl.ds(n * first * chunk, first * chunk)
        trade_wait(d_mine.at[rows], d_input.at[rows], swap_spots[n])
    trade_wait(out_mine, out_low, out_spot)
    for thing in (spread_c, spread_d, sums1, sums2, sums3, g_down, g_gate, g_up, g_out, g_qkv):
        thing.finish()


def second_half(places, norm2, cot, fulls, norm1, q, k, v, att, hidden, x_own, lse, cos, sin, end):
    own, model = cot.shape
    length, width = q.shape
    w_qkv, w_out, w_gate, w_up, w_down = fulls
    ff = w_gate.shape[1]
    groups = 2 ** len(places[0])
    n_parts = 2 ** len(places[3])
    rows = model // (2 * groups)
    shape = lambda *dims: jax.ShapeDtypeStruct(dims, jnp.bfloat16)
    wide = lambda *dims: jax.ShapeDtypeStruct(dims, jnp.float32)
    here, there = pl.BlockSpec(memory_space=pltpu.VMEM), pl.BlockSpec(memory_space=pl.ANY)
    pieces = [shape(rows, cols) for cols in (ff, ff, ff, width, 3 * width)]
    sums = [shape(length, model), shape(n_parts, own, model)] + [shape(n_parts - 1, own, model)] * 2
    out_shape = (
        [shape(own, model)] * 2
        + pieces * 2
        + [shape(length, model)]
        + [shape(length, ff)] * 3
        + [shape(model, cols) for cols in (ff, ff, ff, width, 3 * width)]
        + [shape(length, model), wide(own, model), shape(length, width), shape(length, 3 * width)]
        + sums * 3
        + [shape(own, model)] * 2
    )
    bf = lambda *dims: pltpu.VMEM(dims, jnp.bfloat16)
    blocks = 2 * (groups - 1)
    made = pl.pallas_call(
        functools.partial(second_kernel, places),
        in_specs=[there] * 14 + [here] * 4,
        out_specs=[there] * len(out_shape),
        out_shape=out_shape,
        scratch_shapes=[
            bf(blocks, rows, ff),
            bf(blocks, rows, ff),
            bf(blocks, rows, ff),
            bf(blocks, rows, width),
            bf(blocks, rows, 3 * width),
            bf(groups, rows, ff),
            bf(groups, rows, max(ff, 3 * width)),
            bf(groups, rows, width),
            pltpu.SemaphoreType.DMA((SEMS,)),
            pltpu.SemaphoreType.DMA((SEMS,)),
                        pltpu.SemaphoreType.DMA((3, groups)),
        ],
        compiler_params=pltpu.CompilerParams(
            collective_id=1, has_side_effects=True, vmem_limit_bytes=61 * 2**20
        ),
        cost_estimate=pl.CostEstimate(
            flops=18 * length * model * ff, bytes_accessed=300 * 2**20, transcendentals=length * length * 4
        ),
    )(
        norm2, cot, w_gate, w_up, w_down, w_out, w_qkv, norm1, q, k, v, att, hidden, x_own, lse, cos, sin, end
    )
    return made[:12]


def last_kernel(*refs):
    d_low, near, far = refs[0], refs[1:6], refs[6:11]
    d_input, g_query, g_key, g_value, g_out, g_gate, g_up, g_down = refs[11:]
    add = lambda k: near[k][...].astype(jnp.float32) + far[k][...].astype(jnp.float32)
    d_input[...] = d_low[...].astype(jnp.float32)
    g_down[...], g_gate[...], g_up[...], g_out[...] = add(0), add(1), add(2), add(3)
    cols = g_query.shape[1]
    for k, goal in enumerate((g_query, g_key, g_value)):
        here = slice(k * cols, (k + 1) * cols)
        goal[...] = near[4][:, here].astype(jnp.float32) + far[4][:, here].astype(jnp.float32)


def last_sums(d_low, near, far, steps):
    wide = lambda ref, cols: jax.ShapeDtypeStruct((ref.shape[0], cols), jnp.float32)
    rows = lambda ref: pl.BlockSpec((ref.shape[0] // steps, ref.shape[1]), lambda i: (i, 0))
    cols = near[3].shape[1]
    outs = [wide(d_low, d_low.shape[1])] + [wide(near[3], cols)] * 4
    outs += [wide(near[k], near[k].shape[1]) for k in (1, 2, 0)]
    return pl.pallas_call(
        last_kernel,
        grid=(steps,),
        in_specs=[rows(ref) for ref in (d_low, *near, *far)],
        out_specs=[rows(ref) for ref in outs],
        out_shape=outs,
        compiler_params=pltpu.CompilerParams(vmem_limit_bytes=61 * 2**20),
    )(d_low, *near, *far)


def body(places, x, segments, padding, w_query, w_key, w_value, w_out, w_gate, w_up, w_down, cot):
    own = x.shape[0]
    length = segments.shape[0]
    same = lax.axis_index(places[1]) == lax.axis_index(places[2])
    counts = [jnp.sum(segments <= number, dtype=jnp.int32) for number in range(3)]
    last = jnp.where(segments == 0, counts[0], jnp.where(segments == 1, counts[1], counts[2])) - 1
    end_own = jnp.where(padding == 0, last, jnp.arange(length, dtype=jnp.int32)).reshape(-1, own)
    end = jnp.where(same, end_own, lax.ppermute(end_own, places[1], [(0, 1), (1, 0)]))
    cos, sin = turn_tables(length)
    mats = (jnp.concatenate([w_query, w_key, w_value], axis=1), w_out, w_gate, w_up, w_down)
    norm1, *fulls, q, k, v, att, lse, x_own, hidden, norm2, cot_own = first_half(
        places, x, end_own, cos, sin, mats, cot
    )
    output, d_low, *terms = second_half(
        places, norm2, cot_own, fulls, norm1, q, k, v, att, hidden, x_own, lse, cos, sin, end
    )
    return (output, *last_sums(d_low, terms[:5], terms[5:], 4))


def turn_tables(length):
    frequency = 10000.0 ** (-np.arange(HD // 2, dtype=np.float32) / np.float32(HD // 2))
    angles = np.arange(length, dtype=np.float32)[:, None] * frequency.astype(np.float32)[None, :]
    cos, sin = np.cos(angles), np.sin(angles)
    return (
        jnp.asarray(np.concatenate([cos, cos], axis=1), jnp.float32),
        jnp.asarray(np.concatenate([-sin, sin], axis=1), jnp.float32),
    )


def solution(mesh):
    dp, mp = mesh.devices.shape
    n_dp, n_mp = dp.bit_length() - 1, mp.bit_length() - 1
    dp_axes = tuple("d%d" % k for k in range(n_dp))
    mp_axes = tuple("m%d" % k for k in range(n_mp))
    fine = Mesh(mesh.devices.reshape((2,) * (n_dp + n_mp)), dp_axes + mp_axes)
    places = (dp_axes[:-1], dp_axes[-1], mp_axes[0], mp_axes[1:])
    tokens = P(dp_axes + mp_axes, None)
    weight = P(dp_axes, mp_axes)
    return jax.shard_map(
        functools.partial(body, places),
        mesh=fine,
        in_specs=(tokens, P(dp_axes), P(dp_axes)) + (weight,) * 7 + (tokens,),
        out_specs=(tokens, tokens) + (weight,) * 7,
        check_vma=False,
    )
```
